128 devices in a mesh: gx: 8 (over y_lo, z), gy: 16 (over x, y_hi, core).
Axes of the slice: x: 4, y: 4 (y_hi: 2, y_lo: 2; y = y_hi * 2 + y_lo), z: 4, core: 2. Of those that a mesh axis runs over, the one named last changes fastest.
Arguments:
- source_now: float32 [256, 128, 512], P('gy', 'gx'), may hold values from -6 to 6
- source_next: float32 [256, 128, 512], P('gy', 'gx'), may hold values from -6 to 6
- receiver_now: float32 [128, 512, 256], P('gx', 'gy'), may hold values from -6 to 6
- receiver_next: float32 [128, 512, 256], P('gx', 'gy'), may hold values from -6 to 6
- velocity: float32 [128, 512, 256], P('gx', 'gy'), may hold values from 0.05 to 0.18
- saved_planes: float32 [4, 2, 256, 512], replicated, may hold values from -6 to 6
- plane_index: int32 [4], replicated, may hold values from 0 to 3
- wavelet: float32 [4], replicated, may hold values from -8 to 8
- source_cell: int32 [3], replicated, may hold values from 4 to 123
- traces: float32 [4, 4096], replicated, may hold values from -6 to 6
- receiver_x: int32 [4096], replicated, may hold values from 0 to 127
- receiver_y: int32 [4096], replicated, may hold values from 0 to 511
Outputs:
- image_sum: float32 [128, 512, 256], P('gx', 'gy')
- receiver_field: float32 [128, 512, 256], P('gx', 'gy')
- source_field: float32 [256, 128, 512], P('gy', 'gx')
The draws below stay inside these ranges and needn't reach their ends.
Inputs may be any that keep to these rules, and one draw needn't show every extreme that they name: `receiver_x`: receivers may share a cell; their traces add.
All inputs are finite; a program needn't handle non-finite values.
Results may differ from the reference program's by a relative error of at most 0.00055.
The reference program's roundings to bfloat16 on the way count: a program that leaves them out, or rounds other values in their place, can miss the bound.
Values may be sent and summed in bfloat16 or wider, within the bound.
No kernel may reach another device: no remote copies, remote signals or barrier semaphores. Data moves between devices by JAX's collectives and lax.ppermute only.
A program may use at most 192 MiB of HBM per device.

```python
import math
import jax
import jax.numpy as jnp
from jax import lax

DEPTH = 256
NREC = 4096
STEPS = 4
SAVED = 4
NX = 128
NY = 512


def set_ends(entries, rng, low, high):
    longest = entries.shape.index(max(entries.shape))
    spots = []
    for shift in (0, 1):
        where = [jax.random.randint(jax.random.fold_in(rng, axis), (), 0, length) for axis, length in enumerate(entries.shape)]
        where[longest] = (where[longest] + shift) % entries.shape[longest]
        spots.append(tuple(where))
    return entries.at[spots[0]].set(low).at[spots[1]].set(high)


def shard_levels(own_key, shape, cuts, smallest, largest):
    def one(dim, parts):
        draws = jax.random.uniform(jax.random.fold_in(jax.random.fold_in(own_key, 6), dim), (parts,), jnp.float32, smallest / len(cuts), largest / len(cuts))
        return jnp.repeat(jnp.exp(draws), shape[dim] // parts).reshape((-1,) + (1,) * (len(shape) - dim - 1))

    factor_of = one(*cuts[0])
    for cut in cuts[1:]:
        factor_of = factor_of * one(*cut)
    return factor_of


def normal_values(rng, dims, width, most, cuts=(), held_as=jnp.bfloat16):
    drawn = jax.random.normal(rng, dims, jnp.float32) * width
    if len(cuts) > 0:
        drawn = shard_levels(rng, dims, cuts, -0.22, 0.18) * drawn
    return jnp.clip(drawn, min=-most, max=most).astype(held_as)


def setup_inputs(seed: int = 0) -> dict:
    arg_keys = jax.random.split(jax.random.key(seed), 13)
    return {
        "source_now": normal_values(arg_keys[0], (DEPTH, NX, NY), 1.0, 6.0, ((0, 16), (1, 8)), jnp.float32),
        "source_next": normal_values(arg_keys[1], (DEPTH, NX, NY), 1.0, 6.0, ((0, 16), (1, 8)), jnp.float32),
        "receiver_now": normal_values(arg_keys[2], (NX, NY, DEPTH), 1.0, 6.0, ((0, 8), (1, 16)), jnp.float32),
        "receiver_next": normal_values(arg_keys[3], (NX, NY, DEPTH), 1.0, 6.0, ((0, 8), (1, 16)), jnp.float32),
        "velocity": jnp.clip(jnp.exp(math.log(0.18) - 1.2809339 * jax.random.uniform(arg_keys[4], (NX, NY, DEPTH), jnp.float32) ** shard_levels(arg_keys[4], (NX, NY, DEPTH), ((0, 8), (1, 16)), -0.2, 0.2)), 0.05, 0.18),
        "saved_planes": normal_values(arg_keys[5], (SAVED, 2, DEPTH, NY), 1.0, 6.0, (), jnp.float32),
        "plane_index": set_ends(jax.random.randint(arg_keys[6], (STEPS,), 0, SAVED), jax.random.fold_in(arg_keys[6], 1), 0, SAVED - 1).astype(jnp.int32),
        "wavelet": normal_values(arg_keys[7], (STEPS,), 2.0, 8.0, (), jnp.float32),
        "source_cell": jax.random.randint(arg_keys[8], (3,), 4, min(NX, min(NY, DEPTH)) - 4).astype(jnp.int32),
        "traces": normal_values(arg_keys[9], (STEPS, NREC), 1.0, 6.0, (), jnp.float32),
        "receiver_x": set_ends(jax.random.randint(arg_keys[10], (NREC,), 0, NX), jax.random.fold_in(arg_keys[10], 1), 0, NX - 1).astype(jnp.int32),
        "receiver_y": set_ends(jax.random.randint(arg_keys[11], (NREC,), 0, NY), jax.random.fold_in(arg_keys[11], 1), 0, NY - 1).astype(jnp.int32),
    }


coeffs = (-205.0 / 72.0, 8.0 / 5.0, -1.0 / 5.0, 8.0 / 315.0, -1.0 / 560.0)
receiver_plane = 2


def shifted(padded, leading, dim_index, offset):
    starts = [0] * padded.ndim
    limits = list(padded.shape)
    for other in range(3):
        position = leading + other
        starts[position] = 4 + (offset if other == dim_index else 0)
        limits[position] = starts[position] + padded.shape[position] - 8
    return lax.slice(padded, starts, limits)


def laplace(padded, leading):
    summed = 3.0 * coeffs[0] * shifted(padded, leading, 0, 0)
    for dim_index in range(3):
        for distance in range(1, 5):
            summed = summed + coeffs[distance] * (shifted(padded, leading, dim_index, distance) + shifted(padded, leading, dim_index, -distance))
    return summed


def reference(source_now, source_next, receiver_now, receiver_next, velocity, saved_planes, plane_index, wavelet, source_cell, traces, receiver_x, receiver_y):
    vel_source = jnp.transpose(velocity, (2, 0, 1))
    image_sum = jnp.zeros(velocity.shape, jnp.float32)
    for step_index in range(STEPS):
        earlier = 2.0 * source_now - source_next + vel_source * laplace(jnp.pad(source_now, 4), 0)
        earlier = earlier.at[source_cell[2], source_cell[0], source_cell[1]].add(wavelet[step_index])
        planes = saved_planes[plane_index[step_index]]
        earlier = earlier.at[:, 0, :].set(planes[0])
        earlier = earlier.at[:, -1, :].set(planes[1])
        source_next, source_now = source_now, earlier
        later_rcv = 2.0 * receiver_now - receiver_next + velocity * laplace(jnp.pad(receiver_now, 4), 0)
        later_rcv = later_rcv.at[receiver_x, receiver_y, receiver_plane].add(traces[step_index])
        receiver_next, receiver_now = receiver_now, later_rcv
        if step_index % 2 == 1:
            rounded = lax.optimization_barrier(jnp.transpose(source_now, (1, 2, 0)).astype(jnp.bfloat16)).astype(jnp.float32)
            image_sum = image_sum + rounded * receiver_now
    return image_sum, receiver_now, source_now
```

```python
import jax
import jax.numpy as jnp
from jax import lax
from jax.experimental import pallas as pl
from jax.experimental.pallas import tpu as pltpu
from jax.sharding import PartitionSpec as P

STEPS = 4
C0, C1, C2, C3, C4 = (-205.0 / 72.0, 8.0 / 5.0, -1.0 / 5.0, 8.0 / 315.0, -1.0 / 560.0)
COEFFS = (C0, C1, C2, C3, C4)
RECEIVER_PLANE = 2
PLANES = 5
F32, BF16 = jnp.float32, jnp.bfloat16
VMEM_LIMIT = 48 * 1024 * 1024

RCV = dict(lead=16, rows=32, lanes=256)
SRC = dict(lead=16, rows=16, lanes=512)


def padded_shape(f):
    return (f["lanes"] // 128, f["lead"] + 8, f["rows"] + 16, 128)


def flat(ref):
    return ref.reshape(ref.shape[0], ref.shape[1] * ref.shape[2], 128)


def split(value):
    high = value.astype(BF16)
    return high, (value - high.astype(F32)).astype(BF16)


def planes_of(layers):
    return [*split(layers[0]), *[layer.astype(BF16) for layer in layers[1:]]]


def layers_of(planes):
    planes = [plane.astype(F32) for plane in planes]
    return [planes[0] + planes[1], *planes[2:]]


def pack_halos(src, rcv, gx_low, gx_high, gy_low, gy_high):
    for out_x, out_y, side in ((gx_low, gy_low, 0), (gx_high, gy_high, 1)):
        order = [0, 1, 2, 3] if side == 0 else [15, 14, 13, 12]
        order_y = [0, 1, 2, 3] if side == 0 else [31, 30, 29, 28]
        for t in range(4):
            lanes = slice(t * 128, t * 128 + 128)
            half, col = divmod(t, 2)
            layers = [rcv[col, a * 32 + half * 16 : a * 32 + half * 16 + 16, :] for a in order]
            for p, plane in enumerate(planes_of(layers)):
                out_x[p, :, lanes] = plane
            layers = [src[t, pl.ds(b, 16, stride=16), :] for b in order]
            for p, plane in enumerate(planes_of(layers)):
                out_x[PLANES + p, :, lanes] = plane
            layers = [src[t, a * 16 : a * 16 + 16, :] for a in order]
            for p, plane in enumerate(planes_of(layers)):
                out_y[p, :, lanes] = plane
        for col in range(2):
            layers = [rcv[col, pl.ds(b, 16, stride=32), :] for b in order_y]
            for p, plane in enumerate(planes_of(layers)):
                q, lane = PLANES + p // 2, (p % 2) * 256 + col * 128
                out_y[q, :, lane : lane + 128] = plane


def unpack_halos(psrc, prcv, gx_low, gx_high, gy_low, gy_high):
    ix, iy = lax.axis_index("gx"), lax.axis_index("gy")
    for in_x, in_y, side, live_x, live_y in (
        (gx_low, gy_low, 0, ix > 0, iy > 0),
        (gx_high, gy_high, 1, ix < 7, iy < 15),
    ):
        live_x, live_y = jnp.broadcast_to(live_x, (16, 128)), jnp.broadcast_to(live_y, (16, 128))
        for t in range(4):
            lanes = slice(t * 128, t * 128 + 128)
            half, col = divmod(t, 2)
            for h, layer in enumerate(layers_of([in_x[p, :, lanes] for p in range(PLANES)])):
                row = (3 - h if side == 0 else 20 + h) * 48 + 8 + half * 16
                prcv[col, row : row + 16, :] = jnp.where(live_x, layer, 0.0)
            for h, layer in enumerate(layers_of([in_x[PLANES + p, :, lanes] for p in range(PLANES)])):
                row = 4 * 32 + (7 - h if side == 0 else 24 + h)
                psrc[t, pl.ds(row, 16, stride=32), :] = jnp.where(live_x, layer, 0.0)
            for h, layer in enumerate(layers_of([in_y[p, :, lanes] for p in range(PLANES)])):
                row = (3 - h if side == 0 else 20 + h) * 32 + 8
                psrc[t, row : row + 16, :] = jnp.where(live_y, layer, 0.0)
        for col in range(2):
            planes = []
            for p in range(PLANES):
                lane = (p % 2) * 256 + col * 128
                planes.append(in_y[PLANES + p // 2, :, lane : lane + 128])
            for h, layer in enumerate(layers_of(planes)):
                row = 4 * 48 + (7 - h if side == 0 else 40 + h)
                prcv[col, pl.ds(row, 16, stride=48), :] = jnp.where(live_y, layer, 0.0)


def column(ref, rows, t):
    return ref.at[rows, pl.ds(t * 128, 128)] if len(ref.shape) == 2 else ref.at[t, rows, :]


def step_field(f, padded, nxt, vel, out, inject=None):
    rows, tiles = f["rows"], f["lanes"] // 128
    stride = rows + 16
    lane = lax.broadcasted_iota(jnp.int32, (rows, 128), 1)
    below = {k: lane < k for k in range(1, 5)}
    above = {k: lane >= 128 - k for k in range(1, 5)}

    def layer(a, carry):
        base = pl.multiple_of((a + 4) * stride, 8)
        here = [padded[t, pl.ds(base + 8, rows), :] for t in range(tiles)]
        around = [padded[t, pl.ds(base, stride), :] for t in range(tiles)]
        total = [(3.0 * C0) * c for c in here]
        for k in range(1, 5):
            up = [pltpu.roll(c, k, 1) for c in here]
            down = [pltpu.roll(c, 128 - k, 1) for c in here]
            for t in range(tiles):
                s = padded[t, pl.ds(pl.multiple_of(base + 8 - k * stride, 8), rows), :]
                s = s + padded[t, pl.ds(pl.multiple_of(base + 8 + k * stride, 8), rows), :]
                s = s + around[t][8 - k : 8 - k + rows]
                s = s + around[t][8 + k : 8 + k + rows]
                s = s + jnp.where(below[k], up[t - 1] if t > 0 else 0.0, up[t])
                s = s + jnp.where(above[k], down[t + 1] if t + 1 < tiles else 0.0, down[t])
                total[t] = total[t] + COEFFS[k] * s
        at = pl.ds(pl.multiple_of(a * rows, 8), rows)
        for t in range(tiles):
            value = 2.0 * here[t] - column(nxt, at, t)[...] + column(vel, at, t)[...] * total[t]
            if inject is not None and t == 0:
                value = value + jnp.where(
                    lane == RECEIVER_PLANE, pltpu.roll(inject, RECEIVER_PLANE + 128 - a, 1), 0.0
                )
            column(out, at, t)[...] = value
        return carry

    lax.fori_loop(0, f["lead"], layer, 0)


def pack_brick(src, out):
    group = lax.broadcasted_iota(jnp.int32, (16, 128), 1) // 32
    for t in range(4):
        for xg in range(4):
            rows = [src[t, pl.ds(xg * 4 + xl, 16, stride=16), :] for xl in range(4)]
            for g in range(4):
                piece = None
                for xl in range(4):
                    turned = rows[xl] if xl == g else pltpu.roll(rows[xl], ((xl - g) % 4) * 32, 1)
                    piece = turned if piece is None else jnp.where(group == xl, turned, piece)
                out[t * 4 + g, :, xg * 128 : xg * 128 + 128] = piece.astype(BF16)


def unpack_velocity(pieces, out):
    group = lax.broadcasted_iota(jnp.int32, (16, 128), 1) // 32
    for t in range(4):
        for xg in range(4):
            parts = [pieces[t * 4 + g, :, xg * 128 : xg * 128 + 128] for g in range(4)]
            for xl in range(4):
                row = None
                for g in range(4):
                    turned = parts[g] if xl == g else pltpu.roll(parts[g], ((g - xl) % 4) * 32, 1)
                    row = turned if row is None else jnp.where(group == g, turned, row)
                out[t, pl.ds(xg * 4 + xl, 16, stride=16), :] = row


GX_BUF = jax.ShapeDtypeStruct((2 * PLANES, 16, 512), BF16)
GY_BUF = jax.ShapeDtypeStruct((PLANES + 3, 16, 512), BF16)
SRC_COLS = jax.ShapeDtypeStruct((4, 256, 128), F32)
RCV_COLS = jax.ShapeDtypeStruct((2, 512, 128), F32)
BRICKS = jax.ShapeDtypeStruct((16, 2, 16, 512), BF16)
VM = pl.BlockSpec(memory_space=pltpu.VMEM)
SM = pl.BlockSpec(memory_space=pltpu.SMEM)
HB = pl.BlockSpec(memory_space=pl.ANY)


def params():
    return pltpu.CompilerParams(vmem_limit_bytes=VMEM_LIMIT)


def column_copies(block, cols, sem):
    if len(block.shape) == 4:
        return [pltpu.make_async_copy(block, cols, sem)]
    return [
        pltpu.make_async_copy(block.at[:, :, pl.ds(t * 128, 128)], cols.at[t], sem) for t in range(cols.shape[0])
    ]


def first_halos(src, rcv):
    def kernel(src, rcv, gx_low, gx_high, gy_low, gy_high, src_cols, rcv_cols, sem):
        copies = column_copies(src, src_cols, sem) + column_copies(rcv, rcv_cols, sem)
        for copy in copies:
            copy.start()
        for copy in copies:
            copy.wait()
        pack_halos(flat(src_cols), flat(rcv_cols), gx_low, gx_high, gy_low, gy_high)

    return pl.pallas_call(
        kernel,
        out_shape=[GX_BUF, GX_BUF, GY_BUF, GY_BUF],
        in_specs=[HB] * 2,
        out_specs=[VM] * 4,
        scratch_shapes=[
            pltpu.VMEM((4, 16, 16, 128), F32),
            pltpu.VMEM((2, 16, 32, 128), F32),
            pltpu.SemaphoreType.DMA,
        ],
        compiler_params=params(),
        name="first_halos",
    )(src, rcv)


def turn_velocity(vel):
    def kernel(vel, out):
        for q in range(4):
            out[:, q * 128 : q * 128 + 128] = vel[q * 128 : q * 128 + 128, :].T

    return pl.pallas_call(
        kernel,
        out_shape=jax.ShapeDtypeStruct((256, 512), F32),
        in_specs=[VM],
        out_specs=VM,
        compiler_params=params(),
        name="turn_velocity",
    )(vel)


def injections(traces, receiver_x, receiver_y):
    def kernel(traces, rx, ry, out):
        x0, y0 = lax.axis_index("gx") * 16, lax.axis_index("gy") * 32
        xs = x0 + lax.broadcasted_iota(jnp.int32, (128, 512), 0)
        ys = y0 + lax.broadcasted_iota(jnp.int32, (32, 512), 0)
        total = jnp.zeros((128, 128), F32)
        for c in range(8):
            cols = slice(c * 512, c * 512 + 512)
            at_x = jnp.where(rx[:, cols] == xs, 1.0, 0.0)
            at_y = ry[:, cols] == ys
            weighted = jnp.concatenate(
                [jnp.where(at_y, traces[s : s + 1, cols], 0.0) for s in range(STEPS)], axis=0
            )
            total = total + lax.dot_general(
                weighted,
                at_x,
                (((1,), (1,)), ((), ())),
                precision=lax.Precision.HIGHEST,
                preferred_element_type=F32,
            )
        out[...] = total

    return pl.pallas_call(
        kernel,
        out_shape=jax.ShapeDtypeStruct((128, 128), F32),
        in_specs=[VM] * 3,
        out_specs=VM,
        compiler_params=params(),
        name="injections",
    )(traces, receiver_x.reshape(1, -1), receiver_y.reshape(1, -1))


def one_step(step, src, src_next, rcv, rcv_next, vel_src, vel, halos, saved, plane_index, wavelet, cell, inject):
    first, last = step == 0, step == STEPS - 1

    def kernel(*refs):
        (src, src_next, rcv, rcv_next, vel_src, vel, gxl, gxh, gyl, gyh, saved, plane_index, wavelet, cell, inject) = (
            refs[:15]
        )
        outs = refs[15:]
        src_out, rcv_out = outs[:2]
        padded_src, padded_rcv, plane, sems = outs[-5:-1]
        src_cols = outs[-1] if last else src_out
        ix, iy = lax.axis_index("gx"), lax.axis_index("gy")
        copies = column_copies(src, padded_src.at[:, pl.ds(4, 16), pl.ds(8, 16), :], sems.at[0])
        copies += column_copies(rcv, padded_rcv.at[:, pl.ds(4, 16), pl.ds(8, 32), :], sems.at[0])
        for copy in copies:
            copy.start()
        edge = (ix == 0) | (ix == 7)
        side = jnp.where(ix == 0, 0, 1)
        restores = [
            pltpu.make_async_copy(
                saved.at[plane_index[step], side, pl.ds(pl.multiple_of(iy * 16, 16), 16), pl.ds(t * 128, 128)],
                plane.at[t],
                sems.at[1],
            )
            for t in range(4)
        ]

        @pl.when(edge)
        def _():
            for copy in restores:
                copy.start()

        psrc, prcv = flat(padded_src), flat(padded_rcv)
        if first:
            velocity_src = outs[2]
            unpack_velocity(vel_src, velocity_src)
        else:
            velocity_src = vel_src
        unpack_halos(psrc, prcv, gxl, gxh, gyl, gyh)
        for copy in copies:
            copy.wait()
        step_field(SRC, psrc, src_next, velocity_src, src_cols)
        z, x, y = cell[2] - iy * 16, cell[0] - ix * 16, cell[1]

        @pl.when((z >= 0) & (z < 16) & (x >= 0) & (x < 16))
        def _():
            at = pl.ds(z * 16 + x, 1)
            lanes = lax.broadcasted_iota(jnp.int32, (1, 128), 1)
            for t in range(4):
                src_cols[t, at, :] = src_cols[t, at, :] + jnp.where(lanes + t * 128 == y, wavelet[step], 0.0)

        @pl.when(edge)
        def _():
            for copy in restores:
                copy.wait()

        @pl.when(ix == 0)
        def _():
            for t in range(4):
                src_cols[t, pl.ds(0, 16, stride=16), :] = plane[t]

        @pl.when(ix == 7)
        def _():
            for t in range(4):
                src_cols[t, pl.ds(15, 16, stride=16), :] = plane[t]

        step_field(RCV, prcv, rcv_next, vel, rcv_out, inject[step * 32 : step * 32 + 32, :])
        if last:
            bricks = outs[2]
            result = [
                pltpu.make_async_copy(src_cols.at[t], src_out.at[:, pl.ds(t * 128, 128)], sems.at[0])
                for t in range(4)
            ]
            for copy in result:
                copy.start()
            pack_brick(src_next, bricks.at[:, 0])
            pack_brick(src_cols, bricks.at[:, 1])
            for copy in result:
                copy.wait()
        else:
            pack_halos(src_out, rcv_out, *(outs[3:7] if first else outs[2:6]))

    out_shape = [SRC_COLS, RCV_COLS]
    if first:
        out_shape.append(SRC_COLS)
    if last:
        out_shape = [jax.ShapeDtypeStruct((256, 512), F32), jax.ShapeDtypeStruct((512, 256), F32), BRICKS]
    else:
        out_shape += [GX_BUF, GX_BUF, GY_BUF, GY_BUF]
    return pl.pallas_call(
        kernel,
        out_shape=out_shape,
        in_specs=[HB, VM, HB, VM, VM, VM, VM, VM, VM, VM, HB, SM, SM, SM, VM],
        out_specs=[HB if last else VM] + [VM] * (len(out_shape) - 1),
        scratch_shapes=[
            pltpu.VMEM(padded_shape(SRC), F32),
            pltpu.VMEM(padded_shape(RCV), F32),
            pltpu.VMEM((4, 16, 128), F32),
            pltpu.SemaphoreType.DMA((2,)),
        ]
        + ([pltpu.VMEM((4, 256, 128), F32)] if last else [pltpu.VMEM((8, 128), F32)]),
        compiler_params=params(),
        name=f"step{step}",
    )(src, src_next, rcv, rcv_next, vel_src, vel, *halos, saved, plane_index, wavelet, cell, inject)


def make_image(bricks, rcv_early, rcv_late):
    def kernel(bricks, rcv_early, rcv_late, out):
        for q in range(4):
            rows, cols = slice(q * 128, q * 128 + 128), slice(q * 128, q * 128 + 128)
            early = bricks[:, 0, :, cols].reshape(256, 128).astype(F32).T
            late = bricks[:, 1, :, cols].reshape(256, 128).astype(F32).T
            for t in range(2):
                lanes = slice(t * 128, t * 128 + 128)
                out[rows, lanes] = early[:, lanes] * rcv_early[t, rows, :] + late[:, lanes] * rcv_late[rows, lanes]

    return pl.pallas_call(
        kernel,
        out_shape=jax.ShapeDtypeStruct((512, 256), F32),
        in_specs=[VM] * 3,
        out_specs=VM,
        compiler_params=params(),
        name="make_image",
    )(bricks, rcv_early, rcv_late)


def exchange(buffers):
    gx_low, gx_high, gy_low, gy_high = buffers
    ring = lambda n, by: [(i, (i + by) % n) for i in range(n)]
    return (
        lax.ppermute(gx_high, "gx", ring(8, 1)),
        lax.ppermute(gx_low, "gx", ring(8, -1)),
        lax.ppermute(gy_high, "gy", ring(16, 1)),
        lax.ppermute(gy_low, "gy", ring(16, -1)),
    )


def on_device(
    source_now,
    source_next,
    receiver_now,
    receiver_next,
    velocity,
    saved_planes,
    plane_index,
    wavelet,
    source_cell,
    traces,
    receiver_x,
    receiver_y,
):
    src, src_next = source_now, source_next.reshape(256, 512)
    rcv, rcv_next = receiver_now, receiver_next.reshape(512, 256)
    vel = velocity.reshape(512, 256)
    halos = exchange(first_halos(src, rcv))
    turned = turn_velocity(vel).reshape(16, 16, 512)
    vel_src = lax.all_to_all(turned, "gy", split_axis=0, concat_axis=0, tiled=True)
    inject = injections(traces, receiver_x, receiver_y)
    for step in range(STEPS):
        outs = one_step(
            step, src, src_next, rcv, rcv_next, vel_src, vel, halos, saved_planes, plane_index, wavelet, source_cell, inject
        )
        if step == 0:
            vel_src = outs[2]
            src_next, rcv_next = source_now.reshape(256, 512), receiver_now.reshape(512, 256)
        else:
            src_next, rcv_next = src.reshape(4, 256, 128), rcv.reshape(2, 512, 128)
        if step == STEPS - 1:
            bricks = outs[2]
        else:
            halos = exchange(outs[-4:])
            if step == 1:
                rcv_early = outs[1]
            src, rcv = outs[0].reshape(4, 16, 16, 128), outs[1].reshape(2, 16, 32, 128)
    src, rcv = outs[:2]
    bricks = lax.all_to_all(bricks, "gy", split_axis=0, concat_axis=0, tiled=True)
    image = make_image(bricks, rcv_early, rcv)
    return (image.reshape(16, 32, 256), rcv.reshape(16, 32, 256), src.reshape(16, 16, 512))


def solution(mesh):
    field, turned = P("gx", "gy", None), P("gy", "gx", None)
    return jax.shard_map(
        on_device,
        mesh=mesh,
        in_specs=(turned, turned, field, field, field, P(), P(), P(), P(), P(), P(), P()),
        out_specs=(field, field, turned),
        check_vma=False,
    )
```

```python
import jax
import jax.numpy as jnp
from jax import lax
from jax.experimental import pallas as pl
from jax.experimental.pallas import tpu as pltpu
from jax.sharding import PartitionSpec as P

STEPS = 4
C0, C1, C2, C3, C4 = (-205.0 / 72.0, 8.0 / 5.0, -1.0 / 5.0, 8.0 / 315.0, -1.0 / 560.0)
COEFFS = (C0, C1, C2, C3, C4)
RECEIVER_PLANE = 2
PLANES = 5
F32, BF16 = jnp.float32, jnp.bfloat16
VMEM_LIMIT = 24 * 1024 * 1024

RCV = dict(lead=16, rows=32, lanes=256)
SRC = dict(lead=16, rows=16, lanes=512)


def flat(ref):
    return ref.reshape(ref.shape[0], ref.shape[1] * ref.shape[2], 128)


def split(value):
    high = value.astype(BF16)
    return high, (value - high.astype(F32)).astype(BF16)


def planes_of(layers):
    return [*split(layers[0]), *[layer.astype(BF16) for layer in layers[1:]]]


def layers_of(planes):
    planes = [plane.astype(F32) for plane in planes]
    return [planes[0] + planes[1], *planes[2:]]


def pack_halos(src, rcv, gx_low, gx_high, gy_low, gy_high):
    for out_x, out_y, side in ((gx_low, gy_low, 0), (gx_high, gy_high, 1)):
        order = [0, 1, 2, 3] if side == 0 else [15, 14, 13, 12]
        order_y = [0, 1, 2, 3] if side == 0 else [31, 30, 29, 28]
        for t in range(4):
            lanes = slice(t * 128, t * 128 + 128)
            half, col = divmod(t, 2)
            layers = [rcv[col, a * 32 + half * 16 : a * 32 + half * 16 + 16, :] for a in order]
            for p, plane in enumerate(planes_of(layers)):
                out_x[p, :, lanes] = plane
            layers = [src[t, pl.ds(b, 16, stride=16), :] for b in order]
            for p, plane in enumerate(planes_of(layers)):
                out_x[PLANES + p, :, lanes] = plane
            layers = [src[t, a * 16 : a * 16 + 16, :] for a in order]
            for p, plane in enumerate(planes_of(layers)):
                out_y[p, :, lanes] = plane
        for col in range(2):
            layers = [rcv[col, pl.ds(b, 16, stride=32), :] for b in order_y]
            for p, plane in enumerate(planes_of(layers)):
                q, lane = PLANES + p // 2, (p % 2) * 256 + col * 128
                out_y[q, :, lane : lane + 128] = plane


def add_halos(out_src, out_rcv, vel_src, vel_rcv, gx_low, gx_high, gy_low, gy_high):
    ix, iy = lax.axis_index("gx"), lax.axis_index("gy")

    def add(out, vel, t, rows_of, layers, live):
        layers = [jnp.where(live, layer, 0.0) for layer in layers]
        for d in range(4):
            term = COEFFS[d + 1] * layers[0]
            for h in range(1, 4 - d):
                term = term + COEFFS[d + h + 1] * layers[h]
            rows = rows_of(d)
            out[t, rows, :] = out[t, rows, :] + vel[t, rows, :] * term

    for in_x, in_y, high, live_x, live_y in (
        (gx_low, gy_low, False, ix > 0, iy > 0),
        (gx_high, gy_high, True, ix < 7, iy < 15),
    ):
        live_x, live_y = jnp.broadcast_to(live_x, (16, 128)), jnp.broadcast_to(live_y, (16, 128))
        for t in range(4):
            lanes = slice(t * 128, t * 128 + 128)
            half, col = divmod(t, 2)
            add(
                out_rcv,
                vel_rcv,
                col,
                lambda d: pl.ds((15 - d if high else d) * 32 + half * 16, 16),
                layers_of([in_x[p, :, lanes] for p in range(PLANES)]),
                live_x,
            )
            add(
                out_src,
                vel_src,
                t,
                lambda d: pl.ds((15 - d if high else d) * 16, 16),
                layers_of([in_y[p, :, lanes] for p in range(PLANES)]),
                live_y,
            )
            add(
                out_src,
                vel_src,
                t,
                lambda d: pl.ds(15 - d if high else d, 16, stride=16),
                layers_of([in_x[PLANES + p, :, lanes] for p in range(PLANES)]),
                live_x,
            )
        for col in range(2):
            planes = []
            for p in range(PLANES):
                lane = (p % 2) * 256 + col * 128
                planes.append(in_y[PLANES + p // 2, :, lane : lane + 128])
            add(
                out_rcv,
                vel_rcv,
                col,
                lambda d: pl.ds(31 - d if high else d, 16, stride=32),
                layers_of(planes),
                live_y,
            )


def column(ref, rows, t):
    return ref.at[rows, pl.ds(t * 128, 128)] if len(ref.shape) == 2 else ref.at[t, rows, :]


def local_laplacian(f, now, store):
    lead, rows, tiles = f["lead"], f["rows"], f["lanes"] // 128
    lane = lax.broadcasted_iota(jnp.int32, (rows, 128), 1)
    below = {k: lane < k for k in range(1, 5)}
    above = {k: lane >= 128 - k for k in range(1, 5)}
    none = jnp.zeros((8, 128), F32)
    for a in range(lead):
        here = [now[t, a * rows : a * rows + rows, :] for t in range(tiles)]
        around = [jnp.concatenate([none, c, none], axis=0) for c in here]
        total = [(3.0 * C0) * c for c in here]
        for k in range(1, 5):
            up = [pltpu.roll(c, k, 1) for c in here]
            down = [pltpu.roll(c, 128 - k, 1) for c in here]
            for t in range(tiles):
                s = around[t][8 - k : 8 - k + rows] + around[t][8 + k : 8 + k + rows]
                for other in (a - k, a + k):
                    if 0 <= other < lead:
                        s = s + now[t, other * rows : other * rows + rows, :]
                s = s + jnp.where(below[k], up[t - 1] if t > 0 else 0.0, up[t])
                s = s + jnp.where(above[k], down[t + 1] if t + 1 < tiles else 0.0, down[t])
                total[t] = total[t] + COEFFS[k] * s
        for t in range(tiles):
            store(t, a, slice(a * rows, a * rows + rows), here[t], total[t])


def pack_brick(src, out):
    group = lax.broadcasted_iota(jnp.int32, (16, 128), 1) // 32
    for t in range(4):
        for xg in range(4):
            rows = [src[t, pl.ds(xg * 4 + xl, 16, stride=16), :] for xl in range(4)]
            for g in range(4):
                piece = None
                for xl in range(4):
                    turned = rows[xl] if xl == g else pltpu.roll(rows[xl], ((xl - g) % 4) * 32, 1)
                    piece = turned if piece is None else jnp.where(group == xl, turned, piece)
                out[t * 4 + g, :, xg * 128 : xg * 128 + 128] = piece.astype(BF16)


def unpack_velocity(pieces, out):
    group = lax.broadcasted_iota(jnp.int32, (16, 128), 1) // 32
    for t in range(4):
        for xg in range(4):
            parts = [pieces[t * 4 + g, :, xg * 128 : xg * 128 + 128] for g in range(4)]
            for xl in range(4):
                row = None
                for g in range(4):
                    turned = parts[g] if xl == g else pltpu.roll(parts[g], ((g - xl) % 4) * 32, 1)
                    row = turned if row is None else jnp.where(group == g, turned, row)
                out[t, pl.ds(xg * 4 + xl, 16, stride=16), :] = row


GX_BUF = jax.ShapeDtypeStruct((2 * PLANES, 16, 512), BF16)
GY_BUF = jax.ShapeDtypeStruct((PLANES + 3, 16, 512), BF16)
SRC_COLS = jax.ShapeDtypeStruct((4, 256, 128), F32)
RCV_COLS = jax.ShapeDtypeStruct((2, 512, 128), F32)
BRICKS = jax.ShapeDtypeStruct((16, 2, 16, 512), BF16)
VM = pl.BlockSpec(memory_space=pltpu.VMEM)
SM = pl.BlockSpec(memory_space=pltpu.SMEM)
HB = pl.BlockSpec(memory_space=pltpu.HBM)


def in_hbm(*arrays):
    return [pltpu.with_memory_space_constraint(x, pltpu.HBM) for x in arrays]


def params():
    return pltpu.CompilerParams(vmem_limit_bytes=VMEM_LIMIT)


def hint(microseconds):
    return pl.CostEstimate(flops=0, bytes_accessed=int(microseconds * 3.6e6), transcendentals=0)


def column_copies(block, cols, sem):
    return [
        pltpu.make_async_copy(
            block.at[pl.ds(a, 8), :, pl.ds(t * 128, 128)], cols.at[t, pl.ds(a, 8), :, :], sem
        )
        for a in (0, 8)
        for t in range(cols.shape[0])
    ]


def start(copies):
    for copy in copies:
        copy.start()


def wait(copies):
    for copy in copies:
        copy.wait()


def prologue(vel, src, rcv):
    def kernel(vel, src, rcv, vel_cols, src_cols, rcv_cols, turned, gx_low, gx_high, gy_low, gy_high, sems):
        vel_copies = column_copies(vel, vel_cols, sems.at[0])
        copies = column_copies(src, src_cols, sems.at[1]) + column_copies(rcv, rcv_cols, sems.at[1])
        start(vel_copies)
        start(copies)
        wait(vel_copies)
        flat_cols = flat(vel_cols)
        for t in range(2):
            for q in range(4):
                turned[t * 128 : t * 128 + 128, q * 128 : q * 128 + 128] = flat_cols[t, q * 128 : q * 128 + 128, :].T
        wait(copies)
        pack_halos(flat(src_cols), flat(rcv_cols), gx_low, gx_high, gy_low, gy_high)

    rcv_cols = jax.ShapeDtypeStruct((2, 16, 32, 128), F32)
    return pl.pallas_call(
        kernel,
        out_shape=[
            rcv_cols,
            jax.ShapeDtypeStruct((4, 16, 16, 128), F32),
            rcv_cols,
            jax.ShapeDtypeStruct((256, 512), F32),
            GX_BUF,
            GX_BUF,
            GY_BUF,
            GY_BUF,
        ],
        in_specs=[HB] * 3,
        out_specs=[VM] * 8,
        scratch_shapes=[pltpu.SemaphoreType.DMA((2,))],
        compiler_params=params(),
        name="prologue",
    )(*in_hbm(vel, src, rcv))


def source_velocity(pieces):
    return pl.pallas_call(
        unpack_velocity,
        out_shape=SRC_COLS,
        in_specs=[VM],
        out_specs=VM,
        compiler_params=params(),
        name="source_velocity",
    )(pieces)


def prepare(traces, receiver_x, receiver_y, saved, plane_index):
    def kernel(traces_hbm, rx_hbm, ry_hbm, saved, index_hbm, out, planes, traces, rx, ry, index, sems):
        ix, iy = lax.axis_index("gx"), lax.axis_index("gy")
        inputs = [
            pltpu.make_async_copy(traces_hbm, traces, sems.at[0]),
            pltpu.make_async_copy(rx_hbm, rx, sems.at[0]),
            pltpu.make_async_copy(ry_hbm, ry, sems.at[0]),
        ]
        start(inputs)
        get_index = pltpu.make_async_copy(index_hbm, index, sems.at[1])
        get_index.start()
        get_index.wait()
        edge = (ix == 0) | (ix == 7)
        side = jnp.where(ix == 0, 0, 1)
        restores = [
            pltpu.make_async_copy(
                saved.at[index[step], side, pl.ds(pl.multiple_of(iy * 16, 16), 16), pl.ds(t * 128, 128)],
                planes.at[step, t],
                sems.at[2],
            )
            for step in range(STEPS)
            for t in range(4)
        ]

        @pl.when(edge)
        def _():
            start(restores)

        wait(inputs)
        xs = ix * 16 + lax.broadcasted_iota(jnp.int32, (16, 512), 0)
        ys = iy * 32 + lax.broadcasted_iota(jnp.int32, (32, 512), 0)
        total = jnp.zeros((32, 128), F32)
        for c in range(8):
            cols = slice(c * 512, c * 512 + 512)
            at_x = rx[:, cols] == xs
            at_y = jnp.where(ry[:, cols] == ys, 1.0, 0.0)
            weighted = [jnp.where(at_x, traces[s : s + 1, cols], 0.0) for s in range(STEPS)]
            total = total + lax.dot_general(
                at_y,
                jnp.concatenate(weighted + [jnp.zeros((64, 512), F32)], axis=0),
                (((1,), (1,)), ((), ())),
                precision=lax.Precision.HIGHEST,
                preferred_element_type=F32,
            )
        out[...] = total

        @pl.when(edge)
        def _():
            wait(restores)

    return pl.pallas_call(
        kernel,
        out_shape=[jax.ShapeDtypeStruct((32, 128), F32), jax.ShapeDtypeStruct((STEPS, 4, 16, 128), F32)],
        in_specs=[HB] * 5,
        out_specs=[VM] * 2,
        scratch_shapes=[
            pltpu.VMEM((4, 4096), F32),
            pltpu.VMEM((1, 4096), jnp.int32),
            pltpu.VMEM((1, 4096), jnp.int32),
            pltpu.SMEM((4,), jnp.int32),
            pltpu.SemaphoreType.DMA((3,)),
        ],
        compiler_params=params(),
        cost_estimate=hint(2),
        name="prepare",
    )(*in_hbm(traces, receiver_x.reshape(1, -1), receiver_y.reshape(1, -1), saved, plane_index))


def local_step(step, src, src_next, rcv, rcv_next, vel_src, vel, inject, wavelet, cell):
    def kernel(src, src_next, rcv, rcv_next, vel_src, vel, inject, wavelet_hbm, cell_hbm, *refs):
        src_out, rcv_out, wavelet, cell, sems = refs
        scalars = [
            pltpu.make_async_copy(wavelet_hbm, wavelet, sems.at[0]),
            pltpu.make_async_copy(cell_hbm, cell, sems.at[1]),
        ]
        start(scalars)
        lane = lax.broadcasted_iota(jnp.int32, (32, 128), 1)

        def store_src(t, a, rows, here, lap):
            src_out[t, rows, :] = 2.0 * here - column(src_next, rows, t)[...] + vel_src[t, rows, :] * lap

        def store_rcv(t, a, rows, here, lap):
            value = 2.0 * here - column(rcv_next, rows, t)[...] + vel[t, rows, :] * lap
            if t == 0:
                turn = (RECEIVER_PLANE - step * 16 - a) % 128
                value = value + jnp.where(lane == RECEIVER_PLANE, pltpu.roll(inject[...], turn, 1), 0.0)
            rcv_out[t, rows, :] = value

        local_laplacian(SRC, src, store_src)
        local_laplacian(RCV, rcv, store_rcv)
        wait(scalars)
        z = cell[2] - lax.axis_index("gy") * 16
        x = cell[0] - lax.axis_index("gx") * 16

        @pl.when((z >= 0) & (z < 16) & (x >= 0) & (x < 16))
        def _():
            at = pl.ds(z * 16 + x, 1)
            lanes = lax.broadcasted_iota(jnp.int32, (1, 128), 1)
            for t in range(4):
                src_out[t, at, :] = src_out[t, at, :] + jnp.where(lanes + t * 128 == cell[1], wavelet[step], 0.0)

    return pl.pallas_call(
        kernel,
        out_shape=[SRC_COLS, RCV_COLS],
        in_specs=[VM] * 7 + [HB] * 2,
        out_specs=[VM] * 2,
        scratch_shapes=[
            pltpu.SMEM((4,), F32),
            pltpu.SMEM((3,), jnp.int32),
            pltpu.SemaphoreType.DMA((2,)),
        ],
        compiler_params=params(),
        cost_estimate=hint(3),
        name=f"local_step{step}",
    )(src, src_next, rcv, rcv_next, vel_src, vel, inject, *in_hbm(wavelet, cell))


def halo_step(step, local, vel_src, vel, halos, planes, src_early=None):
    last = step == STEPS - 1

    def kernel(local_src, local_rcv, vel_src, vel, gxl, gxh, gyl, gyh, planes, *refs):
        src_early, refs = (refs[0], refs[1:]) if last else (None, refs)
        src, rcv = refs[:2]
        ix = lax.axis_index("gx")
        src[...] = local_src[...]
        rcv[...] = local_rcv[...]
        add_halos(src, rcv, vel_src, vel, gxl, gxh, gyl, gyh)

        @pl.when(ix == 0)
        def _():
            for t in range(4):
                src[t, pl.ds(0, 16, stride=16), :] = planes[step, t]

        @pl.when(ix == 7)
        def _():
            for t in range(4):
                src[t, pl.ds(15, 16, stride=16), :] = planes[step, t]

        if last:
            bricks = refs[2]
            pack_brick(src_early, bricks.at[:, 0])
            pack_brick(src, bricks.at[:, 1])
        else:
            pack_halos(src, rcv, *refs[2:6])

    args = [*local, vel_src, vel, *halos, planes] + ([src_early] if last else [])
    out_shape = [SRC_COLS, RCV_COLS] + ([BRICKS] if last else [GX_BUF, GX_BUF, GY_BUF, GY_BUF])
    return pl.pallas_call(
        kernel,
        out_shape=out_shape,
        in_specs=[VM] * len(args),
        out_specs=[VM] * len(out_shape),
        compiler_params=params(),
        name=f"halo_step{step}",
    )(*args)


def write_fields(src, rcv):
    def kernel(src, rcv, src_out, rcv_out, sem):
        copies = [
            pltpu.make_async_copy(cols.at[t], out.at[:, pl.ds(t * 128, 128)], sem)
            for cols, out in ((src, src_out), (rcv, rcv_out))
            for t in range(cols.shape[0])
        ]
        start(copies)
        wait(copies)

    return pl.pallas_call(
        kernel,
        out_shape=[jax.ShapeDtypeStruct((256, 512), F32), jax.ShapeDtypeStruct((512, 256), F32)],
        in_specs=[VM] * 2,
        out_specs=[HB] * 2,
        scratch_shapes=[pltpu.SemaphoreType.DMA],
        compiler_params=params(),
        cost_estimate=hint(2),
        name="write_fields",
    )(src, rcv)


def make_image(bricks, rcv_early, rcv_late):
    def kernel(bricks, rcv_early, rcv_late, out, held, sem):
        copies = []
        for q in range(4):
            rows = slice(q * 128, q * 128 + 128)
            early = bricks[:, 0, :, rows].reshape(256, 128).astype(F32).T
            late = bricks[:, 1, :, rows].reshape(256, 128).astype(F32).T
            for t in range(2):
                lanes = slice(t * 128, t * 128 + 128)
                held[rows, lanes] = early[:, lanes] * rcv_early[t, rows, :] + late[:, lanes] * rcv_late[t, rows, :]
            copies.append(pltpu.make_async_copy(held.at[rows, :], out.at[rows, :], sem))
            copies[-1].start()
        wait(copies)

    return pl.pallas_call(
        kernel,
        out_shape=jax.ShapeDtypeStruct((512, 256), F32),
        in_specs=[VM] * 3,
        out_specs=HB,
        scratch_shapes=[pltpu.VMEM((512, 256), F32), pltpu.SemaphoreType.DMA],
        compiler_params=params(),
        name="make_image",
    )(bricks, rcv_early, rcv_late)


def exchange(buffers):
    gx_low, gx_high, gy_low, gy_high = buffers
    ring = lambda n, by: [(i, (i + by) % n) for i in range(n)]
    return (
        lax.ppermute(gx_high, "gx", ring(8, 1)),
        lax.ppermute(gx_low, "gx", ring(8, -1)),
        lax.ppermute(gy_high, "gy", ring(16, 1)),
        lax.ppermute(gy_low, "gy", ring(16, -1)),
    )


def on_device(
    source_now,
    source_next,
    receiver_now,
    receiver_next,
    velocity,
    saved_planes,
    plane_index,
    wavelet,
    source_cell,
    traces,
    receiver_x,
    receiver_y,
):
    vel, src, rcv, turned, *first = prologue(velocity, source_now, receiver_now)
    halos = exchange(first)
    vel_src = source_velocity(
        lax.all_to_all(turned.reshape(16, 16, 512), "gy", split_axis=0, concat_axis=0, tiled=True)
    )
    src, rcv, vel = (x.reshape(x.shape[0], -1, 128) for x in (src, rcv, vel))
    inject, planes = prepare(traces, receiver_x, receiver_y, saved_planes, plane_index)
    src_next, rcv_next = source_next.reshape(256, 512), receiver_next.reshape(512, 256)
    for step in range(STEPS):
        local = local_step(step, src, src_next, rcv, rcv_next, vel_src, vel, inject, wavelet, source_cell)
        if step < STEPS - 1:
            src_new, rcv_new, *to_send = halo_step(step, local, vel_src, vel, halos, planes)
            halos = exchange(to_send)
        else:
            src_new, rcv_new, bricks = halo_step(step, local, vel_src, vel, halos, planes, src_next)
        if step == 1:
            rcv_early = rcv_new
        src_next, rcv_next, src, rcv = src, rcv, src_new, rcv_new
    bricks = lax.all_to_all(bricks, "gy", split_axis=0, concat_axis=0, tiled=True)
    source_field, receiver_field = write_fields(src, rcv)
    image = make_image(bricks, rcv_early, rcv)
    return (image.reshape(16, 32, 256), receiver_field.reshape(16, 32, 256), source_field.reshape(16, 16, 512))


def solution(mesh):
    field, turned = P("gx", "gy", None), P("gy", "gx", None)
    return jax.shard_map(
        on_device,
        mesh=mesh,
        in_specs=(turned, turned, field, field, field, P(), P(), P(), P(), P(), P(), P()),
        out_specs=(field, field, turned),
        check_vma=False,
    )
```

```python
import jax
import jax.numpy as jnp
from jax import lax
from jax.experimental import pallas as pl
from jax.experimental.pallas import tpu as pltpu
from jax.sharding import PartitionSpec as P

STEPS = 4
C0, C1, C2, C3, C4 = (-205.0 / 72.0, 8.0 / 5.0, -1.0 / 5.0, 8.0 / 315.0, -1.0 / 560.0)
COEFFS = (C0, C1, C2, C3, C4)
RECEIVER_PLANE = 2
PLANES = 5
F32, BF16 = jnp.float32, jnp.bfloat16
VMEM_LIMIT = 24 * 1024 * 1024

RCV = dict(lead=16, rows=32, lanes=256)
SRC = dict(lead=16, rows=16, lanes=512)


def flat(ref):
    return ref.reshape(ref.shape[0], ref.shape[1] * ref.shape[2], 128)


def split(value):
    high = value.astype(BF16)
    return high, (value - high.astype(F32)).astype(BF16)


def planes_of(layers):
    return [*split(layers[0]), *[layer.astype(BF16) for layer in layers[1:]]]


def layers_of(planes):
    planes = [plane.astype(F32) for plane in planes]
    return [planes[0] + planes[1], *planes[2:]]


def sides():
    return lax.axis_index("gx") % 2 == 0, lax.axis_index("gy") % 2 == 0


def layer_at(high, count, h):
    return jnp.where(high, count - 1 - h, h)


def pack_halos(src, rcv, gx_first, gx_second, gy_first, gy_second):
    up_x, up_y = sides()
    for out_x, out_y, high_x, high_y in (
        (gx_second, gy_second, ~up_x, ~up_y),
        (gx_first, gy_first, up_x, up_y),
    ):
        for t in range(4):
            lanes = slice(t * 128, t * 128 + 128)
            half, col = divmod(t, 2)
            rows = [pl.multiple_of(layer_at(high_x, 16, h) * 32 + half * 16, 16) for h in range(4)]
            for p, plane in enumerate(planes_of([rcv[col, pl.ds(row, 16), :] for row in rows])):
                out_x[p, :, lanes] = plane
            layers = [src[t, pl.ds(layer_at(high_x, 16, h), 16, stride=16), :] for h in range(4)]
            for p, plane in enumerate(planes_of(layers)):
                out_x[PLANES + p, :, lanes] = plane
            rows = [pl.multiple_of(layer_at(high_y, 16, h) * 16, 16) for h in range(4)]
            for p, plane in enumerate(planes_of([src[t, pl.ds(row, 16), :] for row in rows])):
                out_y[p, :, lanes] = plane
        for col in range(2):
            layers = [rcv[col, pl.ds(layer_at(high_y, 32, h), 16, stride=32), :] for h in range(4)]
            for p, plane in enumerate(planes_of(layers)):
                q, lane = PLANES + p // 2, (p % 2) * 256 + col * 128
                out_y[q, :, lane : lane + 128] = plane


def add_halos(out_src, out_rcv, vel_src, vel_rcv, gx_first, gx_second, gy_first, gy_second):
    ix, iy = lax.axis_index("gx"), lax.axis_index("gy")
    up_x, up_y = sides()

    def add(out, vel, t, rows_of, layers, live):
        if live is not None:
            layers = [jnp.where(live, layer, 0.0) for layer in layers]
        for d in range(4):
            term = COEFFS[d + 1] * layers[0]
            for h in range(1, 4 - d):
                term = term + COEFFS[d + h + 1] * layers[h]
            rows = rows_of(d)
            out[t, rows, :] = out[t, rows, :] + vel[t, rows, :] * term

    live_x = jnp.broadcast_to((ix != 0) & (ix != 7), (16, 128))
    live_y = jnp.broadcast_to((iy != 0) & (iy != 15), (16, 128))
    for in_x, in_y, high_x, high_y, live_x, live_y in (
        (gx_first, gy_first, up_x, up_y, None, None),
        (gx_second, gy_second, ~up_x, ~up_y, live_x, live_y),
    ):
        for t in range(4):
            lanes = slice(t * 128, t * 128 + 128)
            half, col = divmod(t, 2)
            add(
                out_rcv,
                vel_rcv,
                col,
                lambda d: pl.ds(pl.multiple_of(layer_at(high_x, 16, d) * 32 + half * 16, 16), 16),
                layers_of([in_x[p, :, lanes] for p in range(PLANES)]),
                live_x,
            )
            add(
                out_src,
                vel_src,
                t,
                lambda d: pl.ds(pl.multiple_of(layer_at(high_y, 16, d) * 16, 16), 16),
                layers_of([in_y[p, :, lanes] for p in range(PLANES)]),
                live_y,
            )
            add(
                out_src,
                vel_src,
                t,
                lambda d: pl.ds(layer_at(high_x, 16, d), 16, stride=16),
                layers_of([in_x[PLANES + p, :, lanes] for p in range(PLANES)]),
                live_x,
            )
        for col in range(2):
            planes = []
            for p in range(PLANES):
                lane = (p % 2) * 256 + col * 128
                planes.append(in_y[PLANES + p // 2, :, lane : lane + 128])
            add(
                out_rcv,
                vel_rcv,
                col,
                lambda d: pl.ds(layer_at(high_y, 32, d), 16, stride=32),
                layers_of(planes),
                live_y,
            )


def local_laplacian(f, now, store):
    lead, rows, tiles = f["lead"], f["rows"], f["lanes"] // 128
    lane = lax.broadcasted_iota(jnp.int32, (rows, 128), 1)
    below = {k: lane < k for k in range(1, 5)}
    above = {k: lane >= 128 - k for k in range(1, 5)}
    none = jnp.zeros((8, 128), F32)
    for a in range(lead):
        here = [now[t, a * rows : a * rows + rows, :] for t in range(tiles)]
        around = [jnp.concatenate([none, c, none], axis=0) for c in here]
        total = [(3.0 * C0) * c for c in here]
        for k in range(1, 5):
            up = [pltpu.roll(c, k, 1) for c in here]
            down = [pltpu.roll(c, 128 - k, 1) for c in here]
            for t in range(tiles):
                s = around[t][8 - k : 8 - k + rows] + around[t][8 + k : 8 + k + rows]
                for other in (a - k, a + k):
                    if 0 <= other < lead:
                        s = s + now[t, other * rows : other * rows + rows, :]
                s = s + jnp.where(below[k], up[t - 1] if t > 0 else 0.0, up[t])
                s = s + jnp.where(above[k], down[t + 1] if t + 1 < tiles else 0.0, down[t])
                total[t] = total[t] + COEFFS[k] * s
        for t in range(tiles):
            store(t, a, slice(a * rows, a * rows + rows), here[t], total[t])


def pack_brick(src, out, columns=range(4)):
    group = lax.broadcasted_iota(jnp.int32, (16, 128), 1) // 32
    for t in columns:
        for xg in range(4):
            rows = [src[t, pl.ds(xg * 4 + xl, 16, stride=16), :] for xl in range(4)]
            for g in range(4):
                piece = None
                for xl in range(4):
                    turned = rows[xl] if xl == g else pltpu.roll(rows[xl], ((xl - g) % 4) * 32, 1)
                    piece = turned if piece is None else jnp.where(group == xl, turned, piece)
                out[t * 4 + g, :, xg * 128 : xg * 128 + 128] = piece.astype(BF16)


def unpack_velocity(pieces, out):
    group = lax.broadcasted_iota(jnp.int32, (16, 128), 1) // 32
    for t in range(4):
        for xg in range(4):
            parts = [pieces[t * 4 + g, :, xg * 128 : xg * 128 + 128] for g in range(4)]
            for xl in range(4):
                row = None
                for g in range(4):
                    turned = parts[g] if xl == g else pltpu.roll(parts[g], ((g - xl) % 4) * 32, 1)
                    row = turned if row is None else jnp.where(group == g, turned, row)
                out[t, pl.ds(xg * 4 + xl, 16, stride=16), :] = row


GX_BUF = jax.ShapeDtypeStruct((2 * PLANES, 16, 512), BF16)
GY_BUF = jax.ShapeDtypeStruct((PLANES + 3, 16, 512), BF16)
SRC_COLS = jax.ShapeDtypeStruct((4, 256, 128), F32)
RCV_COLS = jax.ShapeDtypeStruct((2, 512, 128), F32)
BRICK = jax.ShapeDtypeStruct((16, 16, 512), BF16)
VM = pl.BlockSpec(memory_space=pltpu.VMEM)
SM = pl.BlockSpec(memory_space=pltpu.SMEM)
HB = pl.BlockSpec(memory_space=pltpu.HBM)


def in_hbm(*arrays):
    return [pltpu.with_memory_space_constraint(x, pltpu.HBM) for x in arrays]


def params():
    return pltpu.CompilerParams(vmem_limit_bytes=VMEM_LIMIT)


def hint(microseconds):
    return pl.CostEstimate(flops=0, bytes_accessed=int(microseconds * 3.6e6), transcendentals=0)


def column_copies(block, cols, sem):
    return [
        pltpu.make_async_copy(
            block.at[pl.ds(a, 8), :, pl.ds(t * 128, 128)], cols.at[t, pl.ds(a, 8), :, :], sem
        )
        for a in (0, 8)
        for t in range(cols.shape[0])
    ]


def start(copies):
    for copy in copies:
        copy.start()


def wait(copies):
    for copy in copies:
        copy.wait()


def prologue(vel, src, rcv):
    def kernel(vel, src, rcv, vel_cols, src_cols, rcv_cols, *refs):
        results, (turned, *packed), sems = refs[:5], refs[5:10], refs[10]
        pieces = [
            pltpu.make_async_copy(
                vel.at[pl.ds(q * 4, 4), :, pl.ds(t * 128, 128)], vel_cols.at[t, pl.ds(q * 4, 4), :, :], sems.at[q]
            )
            for q in range(4)
            for t in range(2)
        ]
        start(pieces)
        copies = column_copies(src, src_cols, sems.at[4]) + column_copies(rcv, rcv_cols, sems.at[4])
        start(copies)
        flat_cols = flat(vel_cols)
        outs = []
        for q in range(4):
            wait(pieces[2 * q : 2 * q + 2])
            lanes = pl.ds(q * 128, 128)
            for t in range(2):
                turned[t * 128 : t * 128 + 128, lanes] = flat_cols[t, q * 128 : q * 128 + 128, :].T
            outs.append(pltpu.make_async_copy(turned.at[:, lanes], results[0].at[:, lanes], sems.at[5]))
            outs[-1].start()
        wait(copies)
        pack_halos(flat(src_cols), flat(rcv_cols), *packed)
        sends = [pltpu.make_async_copy(held, out, sems.at[6]) for held, out in zip(packed, results[1:])]
        start(sends)
        wait(outs)
        wait(sends)

    rcv_cols = jax.ShapeDtypeStruct((2, 16, 32, 128), F32)
    halo_shapes = [GX_BUF.shape, GX_BUF.shape, GY_BUF.shape, GY_BUF.shape]
    return pl.pallas_call(
        kernel,
        out_shape=[rcv_cols, jax.ShapeDtypeStruct((4, 16, 16, 128), F32), rcv_cols, pltpu.HBM((256, 512), F32)]
        + [pltpu.HBM(shape, BF16) for shape in halo_shapes],
        in_specs=[HB] * 3,
        out_specs=[VM] * 3 + [HB] * 5,
        scratch_shapes=[pltpu.VMEM((256, 512), F32)]
        + [pltpu.VMEM(shape, BF16) for shape in halo_shapes]
        + [pltpu.SemaphoreType.DMA((7,))],
        compiler_params=params(),
        name="prologue",
    )(*in_hbm(vel, src, rcv))


def source_velocity(pieces):
    return pl.pallas_call(
        unpack_velocity,
        out_shape=SRC_COLS,
        in_specs=[VM],
        out_specs=VM,
        compiler_params=params(),
        name="source_velocity",
    )(pieces)


def prepare(traces, receiver_x, receiver_y, saved, plane_index):
    def kernel(traces_hbm, rx_hbm, ry_hbm, saved, index_hbm, out, planes, traces, rx, ry, index, sems):
        ix, iy = lax.axis_index("gx"), lax.axis_index("gy")
        inputs = [
            pltpu.make_async_copy(traces_hbm, traces, sems.at[0]),
            pltpu.make_async_copy(rx_hbm, rx, sems.at[0]),
            pltpu.make_async_copy(ry_hbm, ry, sems.at[0]),
        ]
        start(inputs)
        get_index = pltpu.make_async_copy(index_hbm, index, sems.at[1])
        get_index.start()
        get_index.wait()
        edge = (ix == 0) | (ix == 7)
        side = jnp.where(ix == 0, 0, 1)
        restores = [
            pltpu.make_async_copy(
                saved.at[index[step], side, pl.ds(pl.multiple_of(iy * 16, 16), 16), pl.ds(t * 128, 128)],
                planes.at[step, t],
                sems.at[2],
            )
            for step in range(STEPS)
            for t in range(4)
        ]

        @pl.when(edge)
        def _():
            start(restores)

        wait(inputs)
        xs = ix * 16 + lax.broadcasted_iota(jnp.int32, (16, 512), 0)
        ys = iy * 32 + lax.broadcasted_iota(jnp.int32, (32, 512), 0)
        total = jnp.zeros((32, 128), F32)
        for c in range(8):
            cols = slice(c * 512, c * 512 + 512)
            at_x = rx[:, cols] == xs
            at_y = jnp.where(ry[:, cols] == ys, 1.0, 0.0)
            weighted = [jnp.where(at_x, traces[s : s + 1, cols], 0.0) for s in range(STEPS)]
            total = total + lax.dot_general(
                at_y,
                jnp.concatenate(weighted + [jnp.zeros((64, 512), F32)], axis=0),
                (((1,), (1,)), ((), ())),
                precision=lax.Precision.HIGHEST,
                preferred_element_type=F32,
            )
        out[...] = total

        @pl.when(edge)
        def _():
            wait(restores)

    return pl.pallas_call(
        kernel,
        out_shape=[jax.ShapeDtypeStruct((32, 128), F32), jax.ShapeDtypeStruct((STEPS, 4, 16, 128), F32)],
        in_specs=[HB] * 5,
        out_specs=[VM] * 2,
        scratch_shapes=[
            pltpu.VMEM((4, 4096), F32),
            pltpu.VMEM((1, 4096), jnp.int32),
            pltpu.VMEM((1, 4096), jnp.int32),
            pltpu.SMEM((4,), jnp.int32),
            pltpu.SemaphoreType.DMA((3,)),
        ],
        compiler_params=params(),
        cost_estimate=hint(2),
        name="prepare",
    )(*in_hbm(traces, receiver_x.reshape(1, -1), receiver_y.reshape(1, -1), saved, plane_index))


def local_step(step, src, src_next, rcv, rcv_next, vel_src, vel, inject, wavelet, cell):
    first, last = step == 0, step == STEPS - 1
    from_hbm = step < 2

    def kernel(*refs):
        refs = list(refs)
        if from_hbm:
            later = [pltpu.make_async_copy(refs[i], refs[-j], refs[-3].at[2]) for i, j in ((1, 2), (3, 1))]
            start(later)
            next_src, next_rcv = refs[-2:]
            refs = refs[:-2]
        src, src_next, rcv, rcv_next = refs[:4]
        vel_src = None if first else refs.pop(4)
        vel, inject, wavelet_hbm, cell_hbm, src_out, rcv_out = refs[4:10]
        more, (wavelet, cell, sems) = refs[10:-3], refs[-3:]
        scalars = [
            pltpu.make_async_copy(wavelet_hbm, wavelet, sems.at[0]),
            pltpu.make_async_copy(cell_hbm, cell, sems.at[1]),
        ]
        start(scalars)
        lane = lax.broadcasted_iota(jnp.int32, (32, 128), 1)

        def store_src(t, a, rows, here, lap):
            value = 2.0 * here
            if not from_hbm:
                value = value - src_next[t, rows, :]
            if first:
                more[0][t, rows, :] = lap
            else:
                value = value + vel_src[t, rows, :] * lap
            src_out[t, rows, :] = value

        def store_rcv(t, a, rows, here, lap):
            value = 2.0 * here
            if not from_hbm:
                value = value - rcv_next[t, rows, :]
            value = value + vel[t, rows, :] * lap
            if t == 0:
                turn = (RECEIVER_PLANE - step * 16 - a) % 128
                value = value + jnp.where(lane == RECEIVER_PLANE, pltpu.roll(inject[...], turn, 1), 0.0)
            rcv_out[t, rows, :] = value

        local_laplacian(SRC, src, store_src)
        local_laplacian(RCV, rcv, store_rcv)
        if last:
            pack_brick(src_next, more[0])
        if from_hbm:
            wait(later)
            for cols, block in ((src_out, next_src), (rcv_out, next_rcv)):
                for t in range(cols.shape[0]):
                    cols[t] = cols[t] - block[:, t * 128 : t * 128 + 128]
        wait(scalars)
        z = cell[2] - lax.axis_index("gy") * 16
        x = cell[0] - lax.axis_index("gx") * 16

        @pl.when((z >= 0) & (z < 16) & (x >= 0) & (x < 16))
        def _():
            at = pl.ds(z * 16 + x, 1)
            lanes = lax.broadcasted_iota(jnp.int32, (1, 128), 1)
            for t in range(4):
                src_out[t, at, :] = src_out[t, at, :] + jnp.where(lanes + t * 128 == cell[1], wavelet[step], 0.0)

    if from_hbm:
        src_next, rcv_next = in_hbm(src_next, rcv_next)
    next_spec = HB if from_hbm else VM
    args = [src, src_next, rcv, rcv_next] + ([] if first else [vel_src]) + [vel, inject]
    out_shape = [SRC_COLS, RCV_COLS]
    if first:
        out_shape.append(SRC_COLS)
    if last:
        out_shape.append(BRICK)
    return pl.pallas_call(
        kernel,
        out_shape=out_shape,
        in_specs=[VM, next_spec, VM, next_spec] + [VM] * (len(args) - 4) + [HB] * 2,
        out_specs=[VM] * len(out_shape),
        scratch_shapes=[
            pltpu.SMEM((4,), F32),
            pltpu.SMEM((3,), jnp.int32),
            pltpu.SemaphoreType.DMA((3,)),
        ]
        + ([pltpu.VMEM((256, 512), F32), pltpu.VMEM((512, 256), F32)] if from_hbm else []),
        compiler_params=params(),
        cost_estimate=hint(3),
        name=f"local_step{step}",
    )(*args, *in_hbm(wavelet, cell))


def halo_step(step, local, vel_src, vel, halos, planes):
    first, last = step == 0, step == STEPS - 1

    def kernel(*refs):
        refs = list(refs)
        local_src, local_rcv = refs[:2]
        extra = refs.pop(2) if first or last else None
        vel_src, vel, gxl, gxh, gyl, gyh, planes, src, rcv = refs[2:11]
        refs = refs[11:]
        ix = lax.axis_index("gx")
        rcv[...] = local_rcv[...]
        if last:
            bricks, late, sems = refs
            early_copy = pltpu.make_async_copy(extra, bricks.at[:, 0], sems.at[0])
            early_copy.start()
        if first:
            src[...] = local_src[...] + vel_src[...] * extra[...]
        else:
            src[...] = local_src[...]
        add_halos(src, rcv, vel_src, vel, gxl, gxh, gyl, gyh)

        @pl.when(ix == 0)
        def _():
            for t in range(4):
                src[t, pl.ds(0, 16, stride=16), :] = planes[step, t]

        @pl.when(ix == 7)
        def _():
            for t in range(4):
                src[t, pl.ds(15, 16, stride=16), :] = planes[step, t]

        if last:
            copies = [early_copy]
            for t in range(4):
                pack_brick(src, late, (t,))
                part = pl.ds(t * 4, 4)
                copies.append(pltpu.make_async_copy(late.at[part], bricks.at[part, 1], sems.at[1]))
                copies[-1].start()
            wait(copies)
        else:
            pack_halos(src, rcv, *refs)

    args = [*local, vel_src, vel, *halos, planes]
    out_shape = [SRC_COLS, RCV_COLS]
    out_shape += [pltpu.HBM((16, 2, 16, 512), BF16)] if last else [GX_BUF, GX_BUF, GY_BUF, GY_BUF]
    return pl.pallas_call(
        kernel,
        out_shape=out_shape,
        in_specs=[VM] * len(args),
        out_specs=[VM, VM, HB] if last else [VM] * len(out_shape),
        scratch_shapes=[pltpu.VMEM((16, 16, 512), BF16), pltpu.SemaphoreType.DMA((2,))] if last else [],
        compiler_params=params(),
        name=f"halo_step{step}",
    )(*args)


def write_fields(src, rcv):
    def kernel(src, rcv, src_out, rcv_out, sem):
        copies = [
            pltpu.make_async_copy(cols.at[t], out.at[:, pl.ds(t * 128, 128)], sem)
            for cols, out in ((src, src_out), (rcv, rcv_out))
            for t in range(cols.shape[0])
        ]
        start(copies)
        wait(copies)

    return pl.pallas_call(
        kernel,
        out_shape=[jax.ShapeDtypeStruct((256, 512), F32), jax.ShapeDtypeStruct((512, 256), F32)],
        in_specs=[VM] * 2,
        out_specs=[HB] * 2,
        scratch_shapes=[pltpu.SemaphoreType.DMA],
        compiler_params=params(),
        cost_estimate=hint(2),
        name="write_fields",
    )(src, rcv)


def make_image(bricks, rcv_early, rcv_late):
    def kernel(bricks, rcv_early, rcv_late, out, held, sem):
        copies = []
        for q in range(4):
            rows = slice(q * 128, q * 128 + 128)
            early = bricks[:, 0, :, rows].reshape(256, 128).astype(F32).T
            late = bricks[:, 1, :, rows].reshape(256, 128).astype(F32).T
            for t in range(2):
                lanes = slice(t * 128, t * 128 + 128)
                held[rows, lanes] = early[:, lanes] * rcv_early[t, rows, :] + late[:, lanes] * rcv_late[t, rows, :]
            copies.append(pltpu.make_async_copy(held.at[rows, :], out.at[rows, :], sem))
            copies[-1].start()
        wait(copies)

    return pl.pallas_call(
        kernel,
        out_shape=jax.ShapeDtypeStruct((512, 256), F32),
        in_specs=[VM] * 3,
        out_specs=HB,
        scratch_shapes=[pltpu.VMEM((512, 256), F32), pltpu.SemaphoreType.DMA],
        compiler_params=params(),
        name="make_image",
    )(bricks, rcv_early, rcv_late)


def exchange(buffers):
    gx_first, gx_second, gy_first, gy_second = buffers
    inner = lambda n: [(i, i ^ 1) for i in range(n)]
    outer = lambda n: [(i, (((i + 1) ^ 1) - 1) % n) for i in range(n)]
    from_gx_second = lax.ppermute(gx_second, "gx", outer(8))
    from_gx_first = lax.ppermute(gx_first, "gx", inner(8))
    from_gy_second = lax.ppermute(gy_second, "gy", outer(16))
    from_gy_first = lax.ppermute(gy_first, "gy", inner(16))
    return from_gx_first, from_gx_second, from_gy_first, from_gy_second


def on_device(
    source_now,
    source_next,
    receiver_now,
    receiver_next,
    velocity,
    saved_planes,
    plane_index,
    wavelet,
    source_cell,
    traces,
    receiver_x,
    receiver_y,
):
    vel, src, rcv, turned, *first = prologue(velocity, source_now, receiver_now)
    halos = exchange(first)
    vel_src = source_velocity(
        lax.all_to_all(turned.reshape(16, 16, 512), "gy", split_axis=0, concat_axis=0, tiled=True)
    )
    src, rcv, vel = (x.reshape(x.shape[0], -1, 128) for x in (src, rcv, vel))
    inject, planes = prepare(traces, receiver_x, receiver_y, saved_planes, plane_index)
    src_next, rcv_next = source_next.reshape(256, 512), receiver_next.reshape(512, 256)
    for step in range(STEPS):
        local = local_step(step, src, src_next, rcv, rcv_next, vel_src, vel, inject, wavelet, source_cell)
        if step < STEPS - 1:
            src_new, rcv_new, *to_send = halo_step(step, local, vel_src, vel, halos, planes)
            halos = exchange(to_send)
        else:
            src_new, rcv_new, bricks = halo_step(step, local, vel_src, vel, halos, planes)
        if step == 1:
            rcv_early = rcv_new
        src_next, rcv_next, src, rcv = src, rcv, src_new, rcv_new
        if step == 0:
            src_next, rcv_next = source_now.reshape(256, 512), receiver_now.reshape(512, 256)
    bricks = lax.all_to_all(bricks, "gy", split_axis=0, concat_axis=0, tiled=True)
    source_field, receiver_field = write_fields(src, rcv)
    image = make_image(bricks, rcv_early, rcv)
    return (image.reshape(16, 32, 256), receiver_field.reshape(16, 32, 256), source_field.reshape(16, 16, 512))


def solution(mesh):
    field, turned = P("gx", "gy", None), P("gy", "gx", None)
    return jax.shard_map(
        on_device,
        mesh=mesh,
        in_specs=(turned, turned, field, field, field, P(), P(), P(), P(), P(), P(), P()),
        out_specs=(field, field, turned),
        check_vma=False,
    )
```

```python
import jax
import jax.numpy as jnp
from jax import lax
from jax.experimental import pallas as pl
from jax.experimental.pallas import tpu as pltpu
from jax.sharding import PartitionSpec as P

STEPS = 4
C0, C1, C2, C3, C4 = (-205.0 / 72.0, 8.0 / 5.0, -1.0 / 5.0, 8.0 / 315.0, -1.0 / 560.0)
COEFFS = (C0, C1, C2, C3, C4)
RECEIVER_PLANE = 2
PLANES = 5
F32, BF16 = jnp.float32, jnp.bfloat16
VMEM_LIMIT = 24 * 1024 * 1024

RCV = dict(lead=16, rows=32, lanes=256)
SRC = dict(lead=16, rows=16, lanes=512)


def flat(ref):
    return ref.reshape(ref.shape[0], ref.shape[1] * ref.shape[2], 128)


def split(value):
    high = value.astype(BF16)
    return high, (value - high.astype(F32)).astype(BF16)


def planes_of(layers):
    return [*split(layers[0]), *[layer.astype(BF16) for layer in layers[1:]]]


def layers_of(planes):
    planes = [plane.astype(F32) for plane in planes]
    return [planes[0] + planes[1], *planes[2:]]


def sides():
    return lax.axis_index("gx") % 2 == 0, lax.axis_index("gy") % 2 == 0


def layer_at(high, count, h):
    return jnp.where(high, count - 1 - h, h)


def pack_source(src, gx_first, gx_second, gy_first, gy_second):
    up_x, up_y = sides()
    for out_x, out_y, high_x, high_y in (
        (gx_second, gy_second, ~up_x, ~up_y),
        (gx_first, gy_first, up_x, up_y),
    ):
        for t in range(4):
            lanes = slice(t * 128, t * 128 + 128)
            layers = [src[t, pl.ds(layer_at(high_x, 16, h), 16, stride=16), :] for h in range(4)]
            for p, plane in enumerate(planes_of(layers)):
                out_x[p, :, lanes] = plane
            rows = [pl.multiple_of(layer_at(high_y, 16, h) * 16, 16) for h in range(4)]
            for p, plane in enumerate(planes_of([src[t, pl.ds(row, 16), :] for row in rows])):
                out_y[p, :, lanes] = plane


def pack_receiver(rcv, at, gx_first, gx_second, gy_first, gy_second):
    up_x, up_y = sides()
    for out_x, out_y, high_x, high_y in (
        (gx_second, gy_second, ~up_x, ~up_y),
        (gx_first, gy_first, up_x, up_y),
    ):
        for t in range(4):
            lanes = slice(t * 128, t * 128 + 128)
            half, col = divmod(t, 2)
            rows = [pl.multiple_of(layer_at(high_x, 16, h) * 32 + half * 16, 16) for h in range(4)]
            for p, plane in enumerate(planes_of([rcv[col, pl.ds(row, 16), :] for row in rows])):
                out_x[at + p, :, lanes] = plane
        for col in range(2):
            layers = [rcv[col, pl.ds(layer_at(high_y, 32, h), 16, stride=32), :] for h in range(4)]
            for p, plane in enumerate(planes_of(layers)):
                lane = (p % 2) * 256 + col * 128
                out_y[at + p // 2, :, lane : lane + 128] = plane


def add_layers(out, vel, t, rows_of, layers, live):
    if live is not None:
        layers = [jnp.where(live, layer, 0.0) for layer in layers]
    for d in range(4):
        term = COEFFS[d + 1] * layers[0]
        for h in range(1, 4 - d):
            term = term + COEFFS[d + h + 1] * layers[h]
        rows = rows_of(d)
        out[t, rows, :] = out[t, rows, :] + vel[t, rows, :] * term


def received(gx_first, gx_second, gy_first, gy_second):
    ix, iy = lax.axis_index("gx"), lax.axis_index("gy")
    up_x, up_y = sides()
    live_x = jnp.broadcast_to((ix != 0) & (ix != 7), (16, 128))
    live_y = jnp.broadcast_to((iy != 0) & (iy != 15), (16, 128))
    return (
        (gx_first, gy_first, up_x, up_y, None, None),
        (gx_second, gy_second, ~up_x, ~up_y, live_x, live_y),
    )


def add_source(out, vel, *buffers):
    for in_x, in_y, high_x, high_y, live_x, live_y in received(*buffers):
        for t in range(4):
            lanes = slice(t * 128, t * 128 + 128)
            add_layers(
                out,
                vel,
                t,
                lambda d: pl.ds(pl.multiple_of(layer_at(high_y, 16, d) * 16, 16), 16),
                layers_of([in_y[p, :, lanes] for p in range(PLANES)]),
                live_y,
            )
            add_layers(
                out,
                vel,
                t,
                lambda d: pl.ds(layer_at(high_x, 16, d), 16, stride=16),
                layers_of([in_x[p, :, lanes] for p in range(PLANES)]),
                live_x,
            )


def add_receiver(out, vel, at, *buffers):
    for in_x, in_y, high_x, high_y, live_x, live_y in received(*buffers):
        for t in range(4):
            lanes = slice(t * 128, t * 128 + 128)
            half, col = divmod(t, 2)
            add_layers(
                out,
                vel,
                col,
                lambda d: pl.ds(pl.multiple_of(layer_at(high_x, 16, d) * 32 + half * 16, 16), 16),
                layers_of([in_x[at + p, :, lanes] for p in range(PLANES)]),
                live_x,
            )
        for col in range(2):
            planes = []
            for p in range(PLANES):
                lane = (p % 2) * 256 + col * 128
                planes.append(in_y[at + p // 2, :, lane : lane + 128])
            add_layers(
                out,
                vel,
                col,
                lambda d: pl.ds(layer_at(high_y, 32, d), 16, stride=32),
                layers_of(planes),
                live_y,
            )


def local_laplacian(f, now, store):
    lead, rows, tiles = f["lead"], f["rows"], f["lanes"] // 128
    lane = lax.broadcasted_iota(jnp.int32, (rows, 128), 1)
    below = {k: lane < k for k in range(1, 5)}
    above = {k: lane >= 128 - k for k in range(1, 5)}
    none = jnp.zeros((8, 128), F32)
    for a in range(lead):
        here = [now[t, a * rows : a * rows + rows, :] for t in range(tiles)]
        around = [jnp.concatenate([none, c, none], axis=0) for c in here]
        total = [(3.0 * C0) * c for c in here]
        for k in range(1, 5):
            up = [pltpu.roll(c, k, 1) for c in here]
            down = [pltpu.roll(c, 128 - k, 1) for c in here]
            for t in range(tiles):
                s = around[t][8 - k : 8 - k + rows] + around[t][8 + k : 8 + k + rows]
                for other in (a - k, a + k):
                    if 0 <= other < lead:
                        s = s + now[t, other * rows : other * rows + rows, :]
                s = s + jnp.where(below[k], up[t - 1] if t > 0 else 0.0, up[t])
                s = s + jnp.where(above[k], down[t + 1] if t + 1 < tiles else 0.0, down[t])
                total[t] = total[t] + COEFFS[k] * s
        for t in range(tiles):
            store(t, a, slice(a * rows, a * rows + rows), here[t], total[t])


def pack_brick(src, out, columns=range(4)):
    group = lax.broadcasted_iota(jnp.int32, (16, 128), 1) // 32
    for t in columns:
        for xg in range(4):
            rows = [src[t, pl.ds(xg * 4 + xl, 16, stride=16), :] for xl in range(4)]
            for g in range(4):
                piece = None
                for xl in range(4):
                    turned = rows[xl] if xl == g else pltpu.roll(rows[xl], ((xl - g) % 4) * 32, 1)
                    piece = turned if piece is None else jnp.where(group == xl, turned, piece)
                out[t * 4 + g, :, xg * 128 : xg * 128 + 128] = piece.astype(BF16)


def unpack_velocity(pieces, out):
    group = lax.broadcasted_iota(jnp.int32, (16, 128), 1) // 32
    for t in range(4):
        for xg in range(4):
            parts = [pieces[t * 4 + g, :, xg * 128 : xg * 128 + 128] for g in range(4)]
            for xl in range(4):
                row = None
                for g in range(4):
                    turned = parts[g] if xl == g else pltpu.roll(parts[g], ((g - xl) % 4) * 32, 1)
                    row = turned if row is None else jnp.where(group == g, turned, row)
                out[t, pl.ds(xg * 4 + xl, 16, stride=16), :] = row


SRC_PLANES, RCV_PLANES = (PLANES, PLANES), (PLANES, 3)


def halo_buffers(*fields):
    shapes = [(sum(f[axis] for f in fields), 16, 512) for axis in (0, 0, 1, 1)]
    return [jax.ShapeDtypeStruct(shape, BF16) for shape in shapes]


SRC_COLS = jax.ShapeDtypeStruct((4, 256, 128), F32)
RCV_COLS = jax.ShapeDtypeStruct((2, 512, 128), F32)
BRICK = jax.ShapeDtypeStruct((16, 16, 512), BF16)
VM = pl.BlockSpec(memory_space=pltpu.VMEM)
SM = pl.BlockSpec(memory_space=pltpu.SMEM)
HB = pl.BlockSpec(memory_space=pltpu.HBM)


def in_hbm(*arrays):
    return [pltpu.with_memory_space_constraint(x, pltpu.HBM) for x in arrays]


def params():
    return pltpu.CompilerParams(vmem_limit_bytes=VMEM_LIMIT)


def hint(microseconds):
    return pl.CostEstimate(flops=0, bytes_accessed=int(microseconds * 3.6e6), transcendentals=0)


def column_copies(block, cols, sem):
    return [
        pltpu.make_async_copy(
            block.at[pl.ds(a, 8), :, pl.ds(t * 128, 128)], cols.at[t, pl.ds(a, 8), :, :], sem
        )
        for a in (0, 8)
        for t in range(cols.shape[0])
    ]


def start(copies):
    for copy in copies:
        copy.start()


def wait(copies):
    for copy in copies:
        copy.wait()


def turn_velocity(vel):
    def kernel(vel, turned_out, cols, turned, sems):
        pieces = [
            pltpu.make_async_copy(
                vel.at[pl.ds(q * 4, 4), :, pl.ds(t * 128, 128)], cols.at[t, pl.ds(q * 4, 4), :, :], sems.at[q]
            )
            for q in range(4)
            for t in range(2)
        ]
        start(pieces)
        flat_cols = flat(cols)
        outs = []
        for q in range(4):
            wait(pieces[2 * q : 2 * q + 2])
            lanes = pl.ds(q * 128, 128)
            for t in range(2):
                turned[t * 128 : t * 128 + 128, lanes] = flat_cols[t, q * 128 : q * 128 + 128, :].T
            outs.append(pltpu.make_async_copy(turned.at[:, lanes], turned_out.at[:, lanes], sems.at[4]))
            outs[-1].start()
        wait(outs)

    return pl.pallas_call(
        kernel,
        out_shape=pltpu.HBM((256, 512), F32),
        in_specs=[HB],
        out_specs=HB,
        scratch_shapes=[
            pltpu.VMEM((2, 16, 32, 128), F32),
            pltpu.VMEM((256, 512), F32),
            pltpu.SemaphoreType.DMA((5,)),
        ],
        compiler_params=params(),
        name="turn_velocity",
    )(*in_hbm(vel))


def first_halos(src):
    def kernel(src, cols, *refs):
        copies = column_copies(src, cols, refs[-1])
        start(copies)
        wait(copies)
        pack_source(flat(cols), *refs[:4])

    return pl.pallas_call(
        kernel,
        out_shape=[jax.ShapeDtypeStruct((4, 16, 16, 128), F32), *halo_buffers(SRC_PLANES)],
        in_specs=[HB],
        out_specs=[VM] * 5,
        scratch_shapes=[pltpu.SemaphoreType.DMA],
        compiler_params=params(),
        name="first_halos",
    )(*in_hbm(src))


def source_velocity(pieces):
    return pl.pallas_call(
        unpack_velocity,
        out_shape=SRC_COLS,
        in_specs=[VM],
        out_specs=VM,
        compiler_params=params(),
        name="source_velocity",
    )(pieces)


def injections(traces, receiver_x, receiver_y):
    def kernel(traces_hbm, rx_hbm, ry_hbm, out, traces, rx, ry, sem):
        inputs = [
            pltpu.make_async_copy(traces_hbm, traces, sem),
            pltpu.make_async_copy(rx_hbm, rx, sem),
            pltpu.make_async_copy(ry_hbm, ry, sem),
        ]
        start(inputs)
        wait(inputs)
        xs = lax.axis_index("gx") * 16 + lax.broadcasted_iota(jnp.int32, (16, 512), 0)
        ys = lax.axis_index("gy") * 32 + lax.broadcasted_iota(jnp.int32, (32, 512), 0)
        total = jnp.zeros((32, 128), F32)
        for c in range(8):
            cols = slice(c * 512, c * 512 + 512)
            at_x = rx[:, cols] == xs
            at_y = jnp.where(ry[:, cols] == ys, 1.0, 0.0)
            weighted = [jnp.where(at_x, traces[s : s + 1, cols], 0.0) for s in range(STEPS)]
            total = total + lax.dot_general(
                at_y,
                jnp.concatenate(weighted + [jnp.zeros((64, 512), F32)], axis=0),
                (((1,), (1,)), ((), ())),
                precision=lax.Precision.HIGHEST,
                preferred_element_type=F32,
            )
        out[...] = total

    return pl.pallas_call(
        kernel,
        out_shape=jax.ShapeDtypeStruct((32, 128), F32),
        in_specs=[HB] * 3,
        out_specs=VM,
        scratch_shapes=[
            pltpu.VMEM((4, 4096), F32),
            pltpu.VMEM((1, 4096), jnp.int32),
            pltpu.VMEM((1, 4096), jnp.int32),
            pltpu.SemaphoreType.DMA,
        ],
        compiler_params=params(),
        cost_estimate=hint(2),
        name="injections",
    )(*in_hbm(traces, receiver_x.reshape(1, -1), receiver_y.reshape(1, -1)))


def subtract(cols, block):
    for t in range(cols.shape[0]):
        cols[t] = cols[t] - block[:, t * 128 : t * 128 + 128]


def local_source(now, nxt, vel, out, lap_out=None):
    def store(t, a, rows, here, lap):
        value = 2.0 * here
        if nxt is not None:
            value = value - nxt[t, rows, :]
        if vel is None:
            lap_out[t, rows, :] = lap
        else:
            value = value + vel[t, rows, :] * lap
        out[t, rows, :] = value

    local_laplacian(SRC, now, store)


def local_receiver(step, now, nxt, vel, inject, out):
    lane = lax.broadcasted_iota(jnp.int32, (32, 128), 1)

    def store(t, a, rows, here, lap):
        value = 2.0 * here + vel[t, rows, :] * lap
        if nxt is not None:
            value = value - nxt[t, rows, :]
        if t == 0:
            turn = (RECEIVER_PLANE - step * 16 - a) % 128
            value = value + jnp.where(lane == RECEIVER_PLANE, pltpu.roll(inject[...], turn, 1), 0.0)
        out[t, rows, :] = value

    local_laplacian(RCV, now, store)


def add_wavelet(step, cell, wavelet, out):
    z = cell[2] - lax.axis_index("gy") * 16
    x = cell[0] - lax.axis_index("gx") * 16

    @pl.when((z >= 0) & (z < 16) & (x >= 0) & (x < 16))
    def _():
        at = pl.ds(z * 16 + x, 1)
        lanes = lax.broadcasted_iota(jnp.int32, (1, 128), 1)
        for t in range(4):
            out[t, at, :] = out[t, at, :] + jnp.where(lanes + t * 128 == cell[1], wavelet[step], 0.0)


def local_first(src, src_next, rcv, wavelet, cell, saved, plane_index):
    def kernel(src, src_next, rcv, wavelet_hbm, cell_hbm, saved, index_hbm, base, lap, planes, *refs):
        packed, (next_src, rcv_cols, wavelet, cell, index, sems) = refs[:4], refs[4:]
        ix, iy = lax.axis_index("gx"), lax.axis_index("gy")
        get_index = pltpu.make_async_copy(index_hbm, index, sems.at[0])
        get_index.start()
        scalars = [
            pltpu.make_async_copy(wavelet_hbm, wavelet, sems.at[1]),
            pltpu.make_async_copy(cell_hbm, cell, sems.at[2]),
        ]
        get_next = pltpu.make_async_copy(src_next, next_src, sems.at[3])
        get_rcv = column_copies(rcv, rcv_cols, sems.at[4])
        start([*scalars, get_next, *get_rcv])
        local_source(src, None, None, base, lap)
        get_index.wait()
        edge = (ix == 0) | (ix == 7)
        side = jnp.where(ix == 0, 0, 1)
        restores = [
            pltpu.make_async_copy(
                saved.at[index[step], side, pl.ds(pl.multiple_of(iy * 16, 16), 16), pl.ds(t * 128, 128)],
                planes.at[step, t],
                sems.at[5],
            )
            for step in range(STEPS)
            for t in range(4)
        ]

        @pl.when(edge)
        def _():
            start(restores)

        wait(get_rcv)
        pack_receiver(flat(rcv_cols), 0, *packed)
        get_next.wait()
        subtract(base, next_src)
        wait(scalars)
        add_wavelet(0, cell, wavelet, base)

        @pl.when(edge)
        def _():
            wait(restores)

    return pl.pallas_call(
        kernel,
        out_shape=[
            SRC_COLS,
            SRC_COLS,
            jax.ShapeDtypeStruct((STEPS, 4, 16, 128), F32),
            *halo_buffers(RCV_PLANES),
        ],
        in_specs=[VM] + [HB] * 6,
        out_specs=[VM] * 7,
        scratch_shapes=[
            pltpu.VMEM((256, 512), F32),
            pltpu.VMEM((2, 16, 32, 128), F32),
            pltpu.SMEM((4,), F32),
            pltpu.SMEM((3,), jnp.int32),
            pltpu.SMEM((4,), jnp.int32),
            pltpu.SemaphoreType.DMA((6,)),
        ],
        compiler_params=params(),
        cost_estimate=hint(3),
        name="local_first",
    )(src, *in_hbm(src_next, rcv, wavelet, cell, saved, plane_index))


def local_second(src, src_next, rcv, rcv_next, vel, vel_src, inject, wavelet, cell):
    def kernel(src, src_next, rcv, rcv_next, vel, vel_src, inject, wavelet_hbm, cell_hbm, *refs):
        src_out, rcv_out, vel_cols, next_src, rcv_cols, next_rcv, wavelet, cell, sems = refs
        scalars = [
            pltpu.make_async_copy(wavelet_hbm, wavelet, sems.at[0]),
            pltpu.make_async_copy(cell_hbm, cell, sems.at[1]),
        ]
        get_rcv = column_copies(rcv, rcv_cols, sems.at[2]) + column_copies(vel, vel_cols, sems.at[2])
        nexts = [
            pltpu.make_async_copy(src_next, next_src, sems.at[3]),
            pltpu.make_async_copy(rcv_next, next_rcv, sems.at[3]),
        ]
        start([*scalars, *get_rcv, *nexts])
        local_source(src, None, vel_src, src_out)
        wait(get_rcv)
        local_receiver(0, flat(rcv_cols), None, flat(vel_cols), inject, rcv_out)
        wait(nexts)
        subtract(src_out, next_src)
        subtract(rcv_out, next_rcv)
        wait(scalars)
        add_wavelet(1, cell, wavelet, src_out)

    return pl.pallas_call(
        kernel,
        out_shape=[SRC_COLS, RCV_COLS, jax.ShapeDtypeStruct((2, 16, 32, 128), F32)],
        in_specs=[VM] + [HB] * 4 + [VM] * 2 + [HB] * 2,
        out_specs=[VM] * 3,
        scratch_shapes=[
            pltpu.VMEM((256, 512), F32),
            pltpu.VMEM((2, 16, 32, 128), F32),
            pltpu.VMEM((512, 256), F32),
            pltpu.SMEM((4,), F32),
            pltpu.SMEM((3,), jnp.int32),
            pltpu.SemaphoreType.DMA((4,)),
        ],
        compiler_params=params(),
        cost_estimate=hint(4),
        name="local_second",
    )(src, *in_hbm(src_next, rcv, rcv_next, vel), vel_src, inject, *in_hbm(wavelet, cell))


def local_later(step, src, src_next, rcv, rcv_next, vel_src, vel, inject, wavelet, cell):
    from_hbm, last = step == 2, step == STEPS - 1

    def kernel(src, src_next, rcv, rcv_next, vel_src, vel, inject, wavelet_hbm, cell_hbm, src_out, rcv_out, *refs):
        brick = refs[0] if last else None
        wavelet, cell, next_rcv, sems = refs[-4:]
        copies = [
            pltpu.make_async_copy(wavelet_hbm, wavelet, sems.at[0]),
            pltpu.make_async_copy(cell_hbm, cell, sems.at[1]),
        ]
        if from_hbm:
            copies.append(pltpu.make_async_copy(rcv_next, next_rcv, sems.at[2]))
        start(copies)
        local_source(src, src_next, vel_src, src_out)
        local_receiver(step - 1, rcv, None if from_hbm else rcv_next, vel, inject, rcv_out)
        if last:
            pack_brick(src_next, brick)
        wait(copies)
        if from_hbm:
            subtract(rcv_out, next_rcv)
        add_wavelet(step, cell, wavelet, src_out)

    if from_hbm:
        (rcv_next,) = in_hbm(rcv_next)
    out_shape = [SRC_COLS, RCV_COLS] + ([BRICK] if last else [])
    return pl.pallas_call(
        kernel,
        out_shape=out_shape,
        in_specs=[VM] * 3 + [HB if from_hbm else VM] + [VM] * 3 + [HB] * 2,
        out_specs=[VM] * len(out_shape),
        scratch_shapes=[
            pltpu.SMEM((4,), F32),
            pltpu.SMEM((3,), jnp.int32),
            pltpu.VMEM((512, 256) if from_hbm else (8, 128), F32),
            pltpu.SemaphoreType.DMA((3,)),
        ],
        compiler_params=params(),
        cost_estimate=hint(3),
        name=f"local_step{step}",
    )(src, src_next, rcv, rcv_next, vel_src, vel, inject, *in_hbm(wavelet, cell))


def local_last(rcv, rcv_next, vel, inject):
    def kernel(rcv, rcv_next, vel, inject, out):
        local_receiver(STEPS - 1, rcv, rcv_next, vel, inject, out)

    return pl.pallas_call(
        kernel,
        out_shape=RCV_COLS,
        in_specs=[VM] * 4,
        out_specs=VM,
        compiler_params=params(),
        cost_estimate=hint(2),
        name="local_last",
    )(rcv, rcv_next, vel, inject)


def restore_planes(step, src, planes):
    ix = lax.axis_index("gx")

    @pl.when(ix == 0)
    def _():
        for t in range(4):
            src[t, pl.ds(0, 16, stride=16), :] = planes[step, t]

    @pl.when(ix == 7)
    def _():
        for t in range(4):
            src[t, pl.ds(15, 16, stride=16), :] = planes[step, t]


def halo_first(base, lap, vel_src, halos, planes, rcv_packed):
    def kernel(base, lap, vel_src, gx1, gx2, gy1, gy2, planes, *refs):
        rcv_packed, src, packed = refs[:4], refs[4], refs[5:]
        src[...] = base[...] + vel_src[...] * lap[...]
        add_source(src, vel_src, gx1, gx2, gy1, gy2)
        restore_planes(0, src, planes)
        pack_source(src, *packed)
        for half, whole in zip(rcv_packed, packed):
            whole[PLANES:] = half[...]

    args = [base, lap, vel_src, *halos, planes, *rcv_packed]
    return pl.pallas_call(
        kernel,
        out_shape=[SRC_COLS, *halo_buffers(SRC_PLANES, RCV_PLANES)],
        in_specs=[VM] * len(args),
        out_specs=[VM] * 5,
        compiler_params=params(),
        name="halo_first",
    )(*args)


def halo_step(step, local, vel_src, vel, halos, planes):
    last = step == STEPS - 1

    def kernel(*refs):
        refs = list(refs)
        local_src, local_rcv = refs[:2]
        early = refs.pop(2) if last else None
        vel_src, vel, gx1, gx2, gy1, gy2, planes, src, rcv = refs[2:11]
        packed, refs = refs[11:15], refs[15:]
        if last:
            bricks, late, sems = refs
            copies = [pltpu.make_async_copy(early, bricks.at[:, 0], sems.at[0])]
            copies[0].start()
        src[...] = local_src[...]
        add_source(src, vel_src, gx1, gx2, gy1, gy2)
        restore_planes(step, src, planes)
        if last:
            for t in range(4):
                pack_brick(src, late, (t,))
                part = pl.ds(t * 4, 4)
                copies.append(pltpu.make_async_copy(late.at[part], bricks.at[part, 1], sems.at[1]))
                copies[-1].start()
        else:
            pack_source(src, *packed)
        rcv[...] = local_rcv[...]
        add_receiver(rcv, vel, PLANES, gx1, gx2, gy1, gy2)
        pack_receiver(rcv, 0 if last else PLANES, *packed)
        if last:
            wait(copies)

    args = [*local, vel_src, vel, *halos, planes]
    out_shape = [SRC_COLS, RCV_COLS]
    out_shape += halo_buffers(RCV_PLANES) if last else halo_buffers(SRC_PLANES, RCV_PLANES)
    out_shape += [pltpu.HBM((16, 2, 16, 512), BF16)] if last else []
    return pl.pallas_call(
        kernel,
        out_shape=out_shape,
        in_specs=[VM] * len(args),
        out_specs=[VM] * 6 + ([HB] if last else []),
        scratch_shapes=[pltpu.VMEM((16, 16, 512), BF16), pltpu.SemaphoreType.DMA((2,))] if last else [],
        compiler_params=params(),
        name=f"halo_step{step}",
    )(*args)


def halo_last(local, vel, halos):
    def kernel(local, vel, gx1, gx2, gy1, gy2, rcv):
        rcv[...] = local[...]
        add_receiver(rcv, vel, 0, gx1, gx2, gy1, gy2)

    return pl.pallas_call(
        kernel,
        out_shape=RCV_COLS,
        in_specs=[VM] * 6,
        out_specs=VM,
        compiler_params=params(),
        name="halo_last",
    )(local, vel, *halos)


def write_source(src):
    def kernel(src, out, sem):
        copies = [pltpu.make_async_copy(src.at[t], out.at[:, pl.ds(t * 128, 128)], sem) for t in range(4)]
        start(copies)
        wait(copies)

    return pl.pallas_call(
        kernel,
        out_shape=jax.ShapeDtypeStruct((256, 512), F32),
        in_specs=[VM],
        out_specs=HB,
        scratch_shapes=[pltpu.SemaphoreType.DMA],
        compiler_params=params(),
        cost_estimate=hint(1),
        name="write_source",
    )(src)


def make_image(bricks, rcv_early, rcv_late):
    def kernel(bricks, rcv_early, rcv_late, out, rcv_out, held, sems):
        copies = [
            pltpu.make_async_copy(rcv_late.at[t], rcv_out.at[:, pl.ds(t * 128, 128)], sems.at[0]) for t in range(2)
        ]
        start(copies)
        for q in range(4):
            rows = slice(q * 128, q * 128 + 128)
            early = bricks[:, 0, :, rows].reshape(256, 128).astype(F32).T
            late = bricks[:, 1, :, rows].reshape(256, 128).astype(F32).T
            for t in range(2):
                lanes = slice(t * 128, t * 128 + 128)
                held[rows, lanes] = early[:, lanes] * rcv_early[t, rows, :] + late[:, lanes] * rcv_late[t, rows, :]
            copies.append(pltpu.make_async_copy(held.at[rows, :], out.at[rows, :], sems.at[1]))
            copies[-1].start()
        wait(copies)

    return pl.pallas_call(
        kernel,
        out_shape=[jax.ShapeDtypeStruct((512, 256), F32)] * 2,
        in_specs=[VM] * 3,
        out_specs=[HB] * 2,
        scratch_shapes=[pltpu.VMEM((512, 256), F32), pltpu.SemaphoreType.DMA((2,))],
        compiler_params=params(),
        name="make_image",
    )(bricks, rcv_early, rcv_late)


def exchange(buffers):
    gx_first, gx_second, gy_first, gy_second = buffers
    inner = lambda n: [(i, i ^ 1) for i in range(n)]
    outer = lambda n: [(i, (((i + 1) ^ 1) - 1) % n) for i in range(n)]
    from_gx_second = lax.ppermute(gx_second, "gx", outer(8))
    from_gx_first = lax.ppermute(gx_first, "gx", inner(8))
    from_gy_second = lax.ppermute(gy_second, "gy", outer(16))
    from_gy_first = lax.ppermute(gy_first, "gy", inner(16))
    return from_gx_first, from_gx_second, from_gy_first, from_gy_second


def on_device(
    source_now,
    source_next,
    receiver_now,
    receiver_next,
    velocity,
    saved_planes,
    plane_index,
    wavelet,
    source_cell,
    traces,
    receiver_x,
    receiver_y,
):
    turned = turn_velocity(velocity)
    pieces = lax.all_to_all(turned.reshape(16, 16, 512), "gy", split_axis=0, concat_axis=0, tiled=True)
    src, *to_send = first_halos(source_now)
    halos = exchange(to_send)
    src = src.reshape(4, 256, 128)
    base, lap, planes, *rcv_packed = local_first(
        src, source_next.reshape(256, 512), receiver_now, wavelet, source_cell, saved_planes, plane_index
    )
    vel_src = source_velocity(pieces)
    src_0, *to_send = halo_first(base, lap, vel_src, halos, planes, rcv_packed)
    halos = exchange(to_send)
    inject = injections(traces, receiver_x, receiver_y)
    rcv_now = receiver_now.reshape(512, 256)
    *local, vel = local_second(
        src_0,
        source_now.reshape(256, 512),
        receiver_now,
        receiver_next.reshape(512, 256),
        velocity,
        vel_src,
        inject,
        wavelet,
        source_cell,
    )
    vel = vel.reshape(2, 512, 128)
    src_1, rcv_0, *to_send = halo_step(1, local, vel_src, vel, halos, planes)
    halos = exchange(to_send)
    local = local_later(2, src_1, src_0, rcv_0, rcv_now, vel_src, vel, inject, wavelet, source_cell)
    src_2, rcv_1, *to_send = halo_step(2, local, vel_src, vel, halos, planes)
    halos = exchange(to_send)
    local = local_later(3, src_2, src_1, rcv_1, rcv_0, vel_src, vel, inject, wavelet, source_cell)
    src_3, rcv_2, *to_send, bricks = halo_step(3, local, vel_src, vel, halos, planes)
    bricks = lax.all_to_all(bricks, "gy", split_axis=0, concat_axis=0, tiled=True)
    halos = exchange(to_send)
    local = local_last(rcv_2, rcv_1, vel, inject)
    source_field = write_source(src_3)
    rcv_3 = halo_last(local, vel, halos)
    image, receiver_field = make_image(bricks, rcv_1, rcv_3)
    return (image.reshape(16, 32, 256), receiver_field.reshape(16, 32, 256), source_field.reshape(16, 16, 512))


def solution(mesh):
    field, turned = P("gx", "gy", None), P("gy", "gx", None)
    return jax.shard_map(
        on_device,
        mesh=mesh,
        in_specs=(turned, turned, field, field, field, P(), P(), P(), P(), P(), P(), P()),
        out_specs=(field, field, turned),
        check_vma=False,
    )
```

```python
import jax
import jax.numpy as jnp
from jax import lax
from jax.experimental import pallas as pl
from jax.experimental.pallas import tpu as pltpu
from jax.sharding import PartitionSpec as P

STEPS = 4
C0, C1, C2, C3, C4 = (-205.0 / 72.0, 8.0 / 5.0, -1.0 / 5.0, 8.0 / 315.0, -1.0 / 560.0)
COEFFS = (C0, C1, C2, C3, C4)
RECEIVER_PLANE = 2
PLANES = 5
F32, BF16 = jnp.float32, jnp.bfloat16
VMEM_LIMIT = 24 * 1024 * 1024

RCV = dict(lead=16, rows=32, lanes=256)
SRC = dict(lead=16, rows=16, lanes=512)


def flat(ref):
    return ref.reshape(ref.shape[0], ref.shape[1] * ref.shape[2], 128)


def split(value):
    high = value.astype(BF16)
    return high, (value - high.astype(F32)).astype(BF16)


def planes_of(layers):
    return [*split(layers[0]), *[layer.astype(BF16) for layer in layers[1:]]]


def layers_of(planes):
    planes = [plane.astype(F32) for plane in planes]
    return [planes[0] + planes[1], *planes[2:]]


def sides():
    return lax.axis_index("gx") % 2 == 0, lax.axis_index("gy") % 2 == 0


def chosen(up, one, other):
    up = jnp.broadcast_to(up, one[0].shape)
    return [jnp.where(up, x, y) for x, y in zip(one, other)]


def pack_source(src, gx_second, gy_second, gx_first, gy_first):
    up_x, up_y = sides()
    for t in range(4):
        lanes = slice(t * 128, t * 128 + 128)
        low = [src[t, pl.ds(h, 16, stride=16), :] for h in range(4)]
        high = [src[t, pl.ds(15 - h, 16, stride=16), :] for h in range(4)]
        for out, layers in ((gx_second, chosen(up_x, low, high)), (gx_first, chosen(up_x, high, low))):
            for p, plane in enumerate(planes_of(layers)):
                out[p, :, lanes] = plane
        low = [src[t, h * 16 : h * 16 + 16, :] for h in range(4)]
        high = [src[t, (15 - h) * 16 : (15 - h) * 16 + 16, :] for h in range(4)]
        for out, layers in ((gy_second, chosen(up_y, low, high)), (gy_first, chosen(up_y, high, low))):
            for p, plane in enumerate(planes_of(layers)):
                out[p, :, lanes] = plane


def pack_receiver(rcv, at, gx_second, gy_second, gx_first, gy_first):
    up_x, up_y = sides()
    for t in range(4):
        lanes = slice(t * 128, t * 128 + 128)
        half, col = divmod(t, 2)
        low = [rcv[col, h * 32 + half * 16 : h * 32 + half * 16 + 16, :] for h in range(4)]
        high = [rcv[col, (15 - h) * 32 + half * 16 : (15 - h) * 32 + half * 16 + 16, :] for h in range(4)]
        for out, layers in ((gx_second, chosen(up_x, low, high)), (gx_first, chosen(up_x, high, low))):
            for p, plane in enumerate(planes_of(layers)):
                out[at + p, :, lanes] = plane
    for col in range(2):
        low = [rcv[col, pl.ds(h, 16, stride=32), :] for h in range(4)]
        high = [rcv[col, pl.ds(31 - h, 16, stride=32), :] for h in range(4)]
        for out, layers in ((gy_second, chosen(up_y, low, high)), (gy_first, chosen(up_y, high, low))):
            for p, plane in enumerate(planes_of(layers)):
                lane = (p % 2) * 256 + col * 128
                out[at + p // 2, :, lane : lane + 128] = plane


def add_layers(out, vel, t, low_rows, high_rows, first, second, up, ends):
    live = jnp.broadcast_to(~ends, first[0].shape)
    second = [jnp.where(live, layer, 0.0) for layer in second]
    for rows_of, layers in ((low_rows, chosen(up, second, first)), (high_rows, chosen(up, first, second))):
        for d in range(4):
            term = COEFFS[d + 1] * layers[0]
            for h in range(1, 4 - d):
                term = term + COEFFS[d + h + 1] * layers[h]
            rows = rows_of(d)
            out[t, rows, :] = out[t, rows, :] + vel[t, rows, :] * term


def add_source(out, vel, gx_second, gy_second, gx_first, gy_first):
    ix, iy = lax.axis_index("gx"), lax.axis_index("gy")
    up_x, up_y = sides()
    for t in range(4):
        lanes = slice(t * 128, t * 128 + 128)
        planes = lambda buffer: layers_of([buffer[p, :, lanes] for p in range(PLANES)])
        add_layers(
            out,
            vel,
            t,
            lambda d: pl.ds(d * 16, 16),
            lambda d: pl.ds((15 - d) * 16, 16),
            planes(gy_first),
            planes(gy_second),
            up_y,
            (iy == 0) | (iy == 15),
        )
        add_layers(
            out,
            vel,
            t,
            lambda d: pl.ds(d, 16, stride=16),
            lambda d: pl.ds(15 - d, 16, stride=16),
            planes(gx_first),
            planes(gx_second),
            up_x,
            (ix == 0) | (ix == 7),
        )


def add_receiver(out, vel, at, gx_second, gy_second, gx_first, gy_first):
    ix, iy = lax.axis_index("gx"), lax.axis_index("gy")
    up_x, up_y = sides()
    for t in range(4):
        lanes = slice(t * 128, t * 128 + 128)
        half, col = divmod(t, 2)
        planes = lambda buffer: layers_of([buffer[at + p, :, lanes] for p in range(PLANES)])
        add_layers(
            out,
            vel,
            col,
            lambda d: pl.ds(d * 32 + half * 16, 16),
            lambda d: pl.ds((15 - d) * 32 + half * 16, 16),
            planes(gx_first),
            planes(gx_second),
            up_x,
            (ix == 0) | (ix == 7),
        )
    for col in range(2):
        lane = [(p % 2) * 256 + col * 128 for p in range(PLANES)]
        planes = lambda buffer: layers_of(
            [buffer[at + p // 2, :, lane[p] : lane[p] + 128] for p in range(PLANES)]
        )
        add_layers(
            out,
            vel,
            col,
            lambda d: pl.ds(d, 16, stride=32),
            lambda d: pl.ds(31 - d, 16, stride=32),
            planes(gy_first),
            planes(gy_second),
            up_y,
            (iy == 0) | (iy == 15),
        )


def band(rows, cols, offset=0, block=None):
    i = lax.broadcasted_iota(jnp.int32, (rows, cols), 0)
    j = lax.broadcasted_iota(jnp.int32, (rows, cols), 1)
    distance = jnp.abs(i - j + offset)
    matrix = jnp.zeros((rows, cols), F32)
    for k, entry in ((1, 8064.0), (2, -1008.0), (3, 128.0), (4, -9.0)):
        matrix = jnp.where(distance == k, entry, matrix)
    if block is not None:
        matrix = jnp.where(i // block == j // block, matrix, 0.0)
    return matrix.astype(BF16)


def parts_of(value):
    parts = []
    for _ in range(3):
        parts.append(value.astype(BF16))
        value = value - parts[-1].astype(F32)
    return parts


def local_laplacian(f, now, store):
    lead, rows, tiles = f["lead"], f["rows"], f["lanes"] // 128
    dot = lambda x, y: jnp.dot(x, y, preferred_element_type=F32)
    along_lanes, along_rows = band(256, 256), band(256, 256, block=rows)
    if tiles > 2:
        from_above, from_below = band(128, 128, offset=128), band(128, 128, offset=-128)
    for c in range(lead * rows // 256):
        here = [now[t, c * 256 : c * 256 + 256, :] for t in range(tiles)]
        parts = [parts_of(x) for x in here]
        sums = []
        for t in range(0, tiles, 2):
            both = None
            for one, other in zip(parts[t], parts[t + 1]):
                pair = jnp.concatenate([one, other], axis=1)
                term = dot(pair, along_lanes) + dot(along_rows, pair)
                both = term if both is None else both + term
            sums += [both[:, :128], both[:, 128:]]
        for t in range(2, tiles, 2):
            for below, above in zip(parts[t - 1], parts[t]):
                sums[t - 1] = sums[t - 1] + dot(above, from_above)
                sums[t] = sums[t] + dot(below, from_below)
        for t in range(tiles):
            for i in range(256 // rows):
                a = c * (256 // rows) + i
                part = slice(i * rows, i * rows + rows)
                total = (3.0 * C0) * here[t][part] + sums[t][part] * (1.0 / 5040.0)
                for k in range(1, 5):
                    others = [
                        now[t, other * rows : other * rows + rows, :] for other in (a - k, a + k) if 0 <= other < lead
                    ]
                    total = total + COEFFS[k] * sum(others[1:], others[0])
                store(t, a, slice(a * rows, a * rows + rows), here[t][part], total)


def pack_brick(src, out, columns=range(4)):
    group = lax.broadcasted_iota(jnp.int32, (16, 128), 1) // 32
    for t in columns:
        for xg in range(4):
            rows = [src[t, pl.ds(xg * 4 + xl, 16, stride=16), :] for xl in range(4)]
            for g in range(4):
                piece = None
                for xl in range(4):
                    turned = rows[xl] if xl == g else pltpu.roll(rows[xl], ((xl - g) % 4) * 32, 1)
                    piece = turned if piece is None else jnp.where(group == xl, turned, piece)
                out[t * 4 + g, :, xg * 128 : xg * 128 + 128] = piece.astype(BF16)


def unpack_velocity(pieces, out):
    group = lax.broadcasted_iota(jnp.int32, (16, 128), 1) // 32
    for t in range(4):
        for xg in range(4):
            parts = [pieces[t * 4 + g, :, xg * 128 : xg * 128 + 128] for g in range(4)]
            for xl in range(4):
                row = None
                for g in range(4):
                    turned = parts[g] if xl == g else pltpu.roll(parts[g], ((g - xl) % 4) * 32, 1)
                    row = turned if row is None else jnp.where(group == g, turned, row)
                out[t, pl.ds(xg * 4 + xl, 16, stride=16), :] = row


SRC_PLANES, RCV_PLANES = (PLANES, PLANES), (PLANES, 3)


def halo_buffers(*fields):
    shapes = [(sum(f[axis] for f in fields), 16, 512) for axis in (0, 1, 0, 1)]
    return [jax.ShapeDtypeStruct(shape, BF16) for shape in shapes]


SRC_COLS = jax.ShapeDtypeStruct((4, 256, 128), F32)
RCV_COLS = jax.ShapeDtypeStruct((2, 512, 128), F32)
BRICK = jax.ShapeDtypeStruct((16, 16, 512), BF16)
VM = pl.BlockSpec(memory_space=pltpu.VMEM)
SM = pl.BlockSpec(memory_space=pltpu.SMEM)
HB = pl.BlockSpec(memory_space=pltpu.HBM)


def in_hbm(*arrays):
    return [pltpu.with_memory_space_constraint(x, pltpu.HBM) for x in arrays]


def params():
    return pltpu.CompilerParams(vmem_limit_bytes=VMEM_LIMIT)


def hint(microseconds):
    return pl.CostEstimate(flops=0, bytes_accessed=int(microseconds * 3.6e6), transcendentals=0)


def column_copies(block, cols, sem):
    return [
        pltpu.make_async_copy(
            block.at[pl.ds(a, 8), :, pl.ds(t * 128, 128)], cols.at[t, pl.ds(a, 8), :, :], sem
        )
        for a in (0, 8)
        for t in range(cols.shape[0])
    ]


def start(copies):
    for copy in copies:
        copy.start()


def wait(copies):
    for copy in copies:
        copy.wait()


def turn_velocity(vel):
    def kernel(vel, cols, turned_out, turned, sems):
        pieces = [
            pltpu.make_async_copy(
                vel.at[pl.ds(q * 4, 4), :, pl.ds(t * 128, 128)], cols.at[t, pl.ds(q * 4, 4), :, :], sems.at[q]
            )
            for q in range(4)
            for t in range(2)
        ]
        start(pieces)
        flat_cols = flat(cols)
        outs = []
        for q in range(4):
            wait(pieces[2 * q : 2 * q + 2])
            lanes = pl.ds(q * 128, 128)
            for t in range(2):
                turned[t * 128 : t * 128 + 128, lanes] = flat_cols[t, q * 128 : q * 128 + 128, :].T
            outs.append(pltpu.make_async_copy(turned.at[:, lanes], turned_out.at[:, lanes], sems.at[4]))
            outs[-1].start()
        wait(outs)

    return pl.pallas_call(
        kernel,
        out_shape=[jax.ShapeDtypeStruct((2, 16, 32, 128), F32), pltpu.HBM((256, 512), F32)],
        in_specs=[HB],
        out_specs=[VM, HB],
        scratch_shapes=[pltpu.VMEM((256, 512), F32), pltpu.SemaphoreType.DMA((5,))],
        compiler_params=params(),
        name="turn_velocity",
    )(*in_hbm(vel))


def first_halos(src, rcv):
    def kernel(src, rcv, src_cols, *refs):
        rcv_cols, sems = refs[4:]
        get_src, get_rcv = column_copies(src, src_cols, sems.at[0]), column_copies(rcv, rcv_cols, sems.at[1])
        start(get_src + get_rcv)
        wait(get_src)
        pack_source(flat(src_cols), *refs[:4])
        wait(get_rcv)
        pack_receiver(flat(rcv_cols), PLANES, *refs[:4])

    return pl.pallas_call(
        kernel,
        out_shape=[jax.ShapeDtypeStruct((4, 16, 16, 128), F32), *halo_buffers(SRC_PLANES, RCV_PLANES)],
        in_specs=[HB] * 2,
        out_specs=[VM] * 5,
        scratch_shapes=[pltpu.VMEM((2, 16, 32, 128), F32), pltpu.SemaphoreType.DMA((2,))],
        compiler_params=params(),
        name="first_halos",
    )(*in_hbm(src, rcv))


def source_velocity(pieces):
    return pl.pallas_call(
        unpack_velocity,
        out_shape=SRC_COLS,
        in_specs=[VM],
        out_specs=VM,
        compiler_params=params(),
        name="source_velocity",
    )(pieces)


def injections(traces, receiver_x, receiver_y):
    def kernel(traces_hbm, rx_hbm, ry_hbm, out, traces, rx, ry, sem):
        inputs = [
            pltpu.make_async_copy(traces_hbm, traces, sem),
            pltpu.make_async_copy(rx_hbm, rx, sem),
            pltpu.make_async_copy(ry_hbm, ry, sem),
        ]
        start(inputs)
        wait(inputs)
        xs = lax.axis_index("gx") * 16 + lax.broadcasted_iota(jnp.int32, (16, 512), 0)
        ys = lax.axis_index("gy") * 32 + lax.broadcasted_iota(jnp.int32, (32, 512), 0)
        total = jnp.zeros((32, 128), F32)
        for c in range(8):
            cols = slice(c * 512, c * 512 + 512)
            at_x = rx[:, cols] == xs
            at_y = jnp.where(ry[:, cols] == ys, 1.0, 0.0).astype(BF16)
            weighted = [jnp.where(at_x, traces[s : s + 1, cols], 0.0) for s in range(STEPS)]
            for part in parts_of(jnp.concatenate(weighted, axis=0)):
                part = jnp.concatenate([part, jnp.zeros((64, 512), BF16)], axis=0)
                total = total + lax.dot_general(
                    at_y, part, (((1,), (1,)), ((), ())), preferred_element_type=F32
                )
        out[...] = total

    return pl.pallas_call(
        kernel,
        out_shape=jax.ShapeDtypeStruct((32, 128), F32),
        in_specs=[HB] * 3,
        out_specs=VM,
        scratch_shapes=[
            pltpu.VMEM((4, 4096), F32),
            pltpu.VMEM((1, 4096), jnp.int32),
            pltpu.VMEM((1, 4096), jnp.int32),
            pltpu.SemaphoreType.DMA,
        ],
        compiler_params=params(),
        cost_estimate=hint(2),
        name="injections",
    )(*in_hbm(traces, receiver_x.reshape(1, -1), receiver_y.reshape(1, -1)))


def subtract(cols, block):
    for t in range(cols.shape[0]):
        cols[t] = cols[t] - block[:, t * 128 : t * 128 + 128]


def local_source(now, nxt, vel, out, lap_out=None):
    def store(t, a, rows, here, lap):
        value = 2.0 * here
        if nxt is not None:
            value = value - nxt[t, rows, :]
        if vel is None:
            lap_out[t, rows, :] = lap
        else:
            value = value + vel[t, rows, :] * lap
        out[t, rows, :] = value

    local_laplacian(SRC, now, store)


def local_receiver(step, now, nxt, vel, inject, out):
    lane = lax.broadcasted_iota(jnp.int32, (32, 128), 1)

    def store(t, a, rows, here, lap):
        value = 2.0 * here + vel[t, rows, :] * lap
        if nxt is not None:
            value = value - nxt[t, rows, :]
        if t == 0:
            turn = (RECEIVER_PLANE - step * 16 - a) % 128
            value = value + jnp.where(lane == RECEIVER_PLANE, pltpu.roll(inject[...], turn, 1), 0.0)
        out[t, rows, :] = value

    local_laplacian(RCV, now, store)


def add_wavelet(step, cell, wavelet, out):
    z = cell[2] - lax.axis_index("gy") * 16
    x = cell[0] - lax.axis_index("gx") * 16

    @pl.when((z >= 0) & (z < 16) & (x >= 0) & (x < 16))
    def _():
        at = pl.ds(z * 16 + x, 1)
        lanes = lax.broadcasted_iota(jnp.int32, (1, 128), 1)
        for t in range(4):
            out[t, at, :] = out[t, at, :] + jnp.where(lanes + t * 128 == cell[1], wavelet[step], 0.0)


def local_first(src, src_next, rcv, rcv_next, vel, inject, wavelet, cell, saved, plane_index):
    def kernel(src, src_next, rcv, rcv_next, vel, inject, wavelet_hbm, cell_hbm, saved, index_hbm, *refs):
        base, lap, rcv_out, planes, next_src, rcv_cols, next_rcv, wavelet, cell, index, sems = refs
        ix, iy = lax.axis_index("gx"), lax.axis_index("gy")
        get_index = pltpu.make_async_copy(index_hbm, index, sems.at[0])
        get_index.start()
        later = [
            pltpu.make_async_copy(wavelet_hbm, wavelet, sems.at[1]),
            pltpu.make_async_copy(cell_hbm, cell, sems.at[2]),
            pltpu.make_async_copy(src_next, next_src, sems.at[3]),
            pltpu.make_async_copy(rcv_next, next_rcv, sems.at[4]),
        ]
        get_rcv = column_copies(rcv, rcv_cols, sems.at[6])
        start(get_rcv + later)
        local_source(src, None, None, base, lap)
        get_index.wait()
        edge = (ix == 0) | (ix == 7)
        side = jnp.where(ix == 0, 0, 1)
        restores = [
            pltpu.make_async_copy(
                saved.at[index[step], side, pl.ds(pl.multiple_of(iy * 16, 16), 16), pl.ds(t * 128, 128)],
                planes.at[step, t],
                sems.at[5],
            )
            for step in range(STEPS)
            for t in range(4)
        ]

        @pl.when(edge)
        def _():
            start(restores)

        wait(get_rcv)
        local_receiver(0, flat(rcv_cols), None, vel, inject, rcv_out)
        wait(later)
        subtract(base, next_src)
        subtract(rcv_out, next_rcv)
        add_wavelet(0, cell, wavelet, base)

        @pl.when(edge)
        def _():
            wait(restores)

    return pl.pallas_call(
        kernel,
        out_shape=[SRC_COLS, SRC_COLS, RCV_COLS, jax.ShapeDtypeStruct((STEPS, 4, 16, 128), F32)],
        in_specs=[VM, HB, HB, HB, VM, VM] + [HB] * 4,
        out_specs=[VM] * 4,
        scratch_shapes=[
            pltpu.VMEM((256, 512), F32),
            pltpu.VMEM((2, 16, 32, 128), F32),
            pltpu.VMEM((512, 256), F32),
            pltpu.SMEM((4,), F32),
            pltpu.SMEM((3,), jnp.int32),
            pltpu.SMEM((4,), jnp.int32),
            pltpu.SemaphoreType.DMA((7,)),
        ],
        compiler_params=params(),
        cost_estimate=hint(3),
        name="local_first",
    )(
        src,
        *in_hbm(src_next, rcv, rcv_next),
        vel,
        inject,
        *in_hbm(wavelet, cell, saved, plane_index),
    )


def local_step(step, src, src_next, rcv, rcv_next, vel_src, vel, inject, wavelet, cell):
    from_hbm, keep, last = step == 1, step == 2, step == STEPS - 1

    def kernel(src, src_next, rcv, rcv_next, vel_src, vel, inject, wavelet_hbm, cell_hbm, src_out, rcv_out, *refs):
        brick = refs[0] if last else None
        wavelet, cell, next_src, next_rcv, sems = refs[-5:]
        copies = [
            pltpu.make_async_copy(wavelet_hbm, wavelet, sems.at[0]),
            pltpu.make_async_copy(cell_hbm, cell, sems.at[1]),
        ]
        if from_hbm:
            copies.append(pltpu.make_async_copy(src_next, next_src, sems.at[2]))
            copies.append(pltpu.make_async_copy(rcv_next, next_rcv, sems.at[3]))
        if keep:
            copies.append(pltpu.make_async_copy(rcv, refs[0], sems.at[2]))
        start(copies)
        local_source(src, None if from_hbm else src_next, vel_src, src_out)
        local_receiver(step, rcv, None if from_hbm else rcv_next, vel, inject, rcv_out)
        if last:
            pack_brick(src_next, brick)
        wait(copies)
        if from_hbm:
            subtract(src_out, next_src)
            subtract(rcv_out, next_rcv)
        add_wavelet(step, cell, wavelet, src_out)

    if from_hbm:
        src_next, rcv_next = in_hbm(src_next, rcv_next)
    next_spec = HB if from_hbm else VM
    out_shape = [SRC_COLS, RCV_COLS] + ([BRICK] if last else [])
    if keep:
        out_shape.append(pltpu.HBM(RCV_COLS.shape, F32))
    return pl.pallas_call(
        kernel,
        out_shape=out_shape,
        in_specs=[VM, next_spec, VM, next_spec] + [VM] * 3 + [HB] * 2,
        out_specs=[VM, VM] + [HB if keep else VM] * (len(out_shape) - 2),
        scratch_shapes=[
            pltpu.SMEM((4,), F32),
            pltpu.SMEM((3,), jnp.int32),
            pltpu.VMEM((256, 512) if from_hbm else (8, 128), F32),
            pltpu.VMEM((512, 256) if from_hbm else (8, 128), F32),
            pltpu.SemaphoreType.DMA((4,)),
        ],
        compiler_params=params(),
        cost_estimate=hint(3),
        name=f"local_step{step}",
    )(src, src_next, rcv, rcv_next, vel_src, vel, inject, *in_hbm(wavelet, cell))


def restore_planes(step, src, planes):
    ix = lax.axis_index("gx")

    @pl.when(ix == 0)
    def _():
        for t in range(4):
            src[t, pl.ds(0, 16, stride=16), :] = planes[step, t]

    @pl.when(ix == 7)
    def _():
        for t in range(4):
            src[t, pl.ds(15, 16, stride=16), :] = planes[step, t]


def halo_step(step, local, vel_src, vel, halos, planes):
    first = step == 0

    def kernel(*refs):
        refs = list(refs)
        local_src = refs.pop(0)
        lap = refs.pop(0) if first else None
        local_rcv, vel_src, vel = refs[:3]
        halos, planes, src, rcv, packed = refs[3:7], refs[7], refs[8], refs[9], refs[10:]
        src[...] = local_src[...] + vel_src[...] * lap[...] if first else local_src[...]
        rcv[...] = local_rcv[...]
        add_source(src, vel_src, *halos)
        restore_planes(step, src, planes)
        pack_source(src, *packed)
        add_receiver(rcv, vel, PLANES, *halos)
        pack_receiver(rcv, PLANES, *packed)

    args = [*local, vel_src, vel, *halos, planes]
    out_shape = [SRC_COLS, RCV_COLS, *halo_buffers(SRC_PLANES, RCV_PLANES)]
    return pl.pallas_call(
        kernel,
        out_shape=out_shape,
        in_specs=[VM] * len(args),
        out_specs=[VM] * len(out_shape),
        compiler_params=params(),
        name=f"halo_step{step}",
    )(*args)


def last_source(local, early, vel_src, halos, planes):
    def kernel(local, early, vel_src, *refs):
        halos, planes, src, bricks, late, sems = refs[:4], *refs[4:]
        copies = [pltpu.make_async_copy(early, bricks.at[:, 0], sems.at[0])]
        copies[0].start()
        src[...] = local[...]
        add_source(src, vel_src, *halos)
        restore_planes(STEPS - 1, src, planes)
        for t in range(4):
            pack_brick(src, late, (t,))
            part = pl.ds(t * 4, 4)
            copies.append(pltpu.make_async_copy(late.at[part], bricks.at[part, 1], sems.at[1]))
            copies[-1].start()
        wait(copies)

    return pl.pallas_call(
        kernel,
        out_shape=[SRC_COLS, pltpu.HBM((16, 2, 16, 512), BF16)],
        in_specs=[VM] * 8,
        out_specs=[VM, HB],
        scratch_shapes=[pltpu.VMEM((16, 16, 512), BF16), pltpu.SemaphoreType.DMA((2,))],
        compiler_params=params(),
        name="last_source",
    )(local, early, vel_src, *halos, planes)


def last_receiver(local, vel, halos, src, kept):
    def kernel(local, vel, *refs):
        halos, src, kept, rcv, early, src_out, rcv_out, sem = refs[:4], *refs[4:]
        copies = [pltpu.make_async_copy(src.at[t], src_out.at[:, pl.ds(t * 128, 128)], sem) for t in range(4)]
        copies += [pltpu.make_async_copy(kept.at[t], early.at[t], sem) for t in range(2)]
        start(copies)
        rcv[...] = local[...]
        add_receiver(rcv, vel, PLANES, *halos)
        more = [pltpu.make_async_copy(rcv.at[t], rcv_out.at[:, pl.ds(t * 128, 128)], sem) for t in range(2)]
        start(more)
        wait(copies + more)

    return pl.pallas_call(
        kernel,
        out_shape=[RCV_COLS] * 2 + [jax.ShapeDtypeStruct(shape, F32) for shape in ((256, 512), (512, 256))],
        in_specs=[VM] * 7 + [HB],
        out_specs=[VM, VM, HB, HB],
        scratch_shapes=[pltpu.SemaphoreType.DMA],
        compiler_params=params(),
        cost_estimate=hint(2),
        name="last_receiver",
    )(local, vel, *halos, src, *in_hbm(kept))


def make_image(bricks, rcv_early, rcv_late):
    def kernel(bricks, rcv_early, rcv_late, out, held, sem):
        copies = []
        for q in range(4):
            rows = slice(q * 128, q * 128 + 128)
            early = bricks[:, 0, :, rows].reshape(256, 128).astype(F32).T
            late = bricks[:, 1, :, rows].reshape(256, 128).astype(F32).T
            for t in range(2):
                lanes = slice(t * 128, t * 128 + 128)
                held[rows, lanes] = early[:, lanes] * rcv_early[t, rows, :] + late[:, lanes] * rcv_late[t, rows, :]
            copies.append(pltpu.make_async_copy(held.at[rows, :], out.at[rows, :], sem))
            copies[-1].start()
        wait(copies)

    return pl.pallas_call(
        kernel,
        out_shape=jax.ShapeDtypeStruct((512, 256), F32),
        in_specs=[VM] * 3,
        out_specs=HB,
        scratch_shapes=[pltpu.VMEM((512, 256), F32), pltpu.SemaphoreType.DMA],
        compiler_params=params(),
        name="make_image",
    )(bricks, rcv_early, rcv_late)


def exchange(buffers):
    gx_second, gy_second, gx_first, gy_first = buffers
    inner = lambda n: [(i, i ^ 1) for i in range(n)]
    outer = lambda n: [(i, (((i + 1) ^ 1) - 1) % n) for i in range(n)]
    return (
        lax.ppermute(gx_second, "gx", outer(8)),
        lax.ppermute(gy_second, "gy", outer(16)),
        lax.ppermute(gx_first, "gx", inner(8)),
        lax.ppermute(gy_first, "gy", inner(16)),
    )


def on_device(
    source_now,
    source_next,
    receiver_now,
    receiver_next,
    velocity,
    saved_planes,
    plane_index,
    wavelet,
    source_cell,
    traces,
    receiver_x,
    receiver_y,
):
    vel, turned = turn_velocity(velocity)
    pieces = lax.all_to_all(turned.reshape(16, 16, 512), "gy", split_axis=0, concat_axis=0, tiled=True)
    src, *to_send = first_halos(source_now, receiver_now)
    halos = exchange(to_send)
    src, vel = src.reshape(4, 256, 128), vel.reshape(2, 512, 128)
    inject = injections(traces, receiver_x, receiver_y)
    src_next, rcv_next = source_next.reshape(256, 512), receiver_next.reshape(512, 256)
    *local, planes = local_first(
        src, src_next, receiver_now, rcv_next, vel, inject, wavelet, source_cell, saved_planes, plane_index
    )
    vel_src = source_velocity(pieces)
    src_next, rcv_next = source_now.reshape(256, 512), receiver_now.reshape(512, 256)
    more = []
    for step in range(STEPS - 1):
        src, rcv, *to_send = halo_step(step, local, vel_src, vel, halos, planes)
        halos = exchange(to_send)
        local = local_step(step + 1, src, src_next, rcv, rcv_next, vel_src, vel, inject, wavelet, source_cell)
        more += local[2:]
        local = local[:2]
        src_next, rcv_next = src, rcv
    kept, early = more
    src, bricks = last_source(local[0], early, vel_src, halos, planes)
    bricks = lax.all_to_all(bricks, "gy", split_axis=0, concat_axis=0, tiled=True)
    rcv, rcv_early, source_field, receiver_field = last_receiver(local[1], vel, halos, src, kept)
    image = make_image(bricks, rcv_early, rcv)
    return (image.reshape(16, 32, 256), receiver_field.reshape(16, 32, 256), source_field.reshape(16, 16, 512))


def solution(mesh):
    field, turned = P("gx", "gy", None), P("gy", "gx", None)
    return jax.shard_map(
        on_device,
        mesh=mesh,
        in_specs=(turned, turned, field, field, field, P(), P(), P(), P(), P(), P(), P()),
        out_specs=(field, field, turned),
        check_vma=False,
    )
```

```python
import jax
import jax.numpy as jnp
from jax import lax
from jax.experimental import pallas as pl
from jax.experimental.pallas import tpu as pltpu
from jax.sharding import PartitionSpec as P

STEPS = 4
C0, C1, C2, C3, C4 = (-205.0 / 72.0, 8.0 / 5.0, -1.0 / 5.0, 8.0 / 315.0, -1.0 / 560.0)
COEFFS = (C0, C1, C2, C3, C4)
RECEIVER_PLANE = 2
PLANES = 5
F32, BF16, I16 = jnp.float32, jnp.bfloat16, jnp.int16
VELOCITY_MIDDLE, VELOCITY_STEP = 0.115, 0.0651 / 32767
VMEM_LIMIT = 24 * 1024 * 1024

RCV = dict(lead=16, rows=32, lanes=256)
SRC = dict(lead=16, rows=16, lanes=512)


def flat(ref):
    return ref.reshape(ref.shape[0], ref.shape[1] * ref.shape[2], 128)


def split(value):
    high = value.astype(BF16)
    return high, (value - high.astype(F32)).astype(BF16)


def planes_of(layers):
    return [*split(layers[0]), *[layer.astype(BF16) for layer in layers[1:]]]


def layers_of(planes):
    planes = [plane.astype(F32) for plane in planes]
    return [planes[0] + planes[1], *planes[2:]]


def sides():
    return lax.axis_index("gx") % 2 == 0, lax.axis_index("gy") % 2 == 0


def chosen(up, one, other):
    up = jnp.broadcast_to(up, one[0].shape)
    return [jnp.where(up, x, y) for x, y in zip(one, other)]


def pack_source(src, gx_second, gy_second, gx_first, gy_first):
    up_x, up_y = sides()
    for t in range(4):
        lanes = slice(t * 128, t * 128 + 128)
        low = [src[t, pl.ds(h, 16, stride=16), :] for h in range(4)]
        high = [src[t, pl.ds(15 - h, 16, stride=16), :] for h in range(4)]
        for out, layers in ((gx_second, chosen(up_x, low, high)), (gx_first, chosen(up_x, high, low))):
            for p, plane in enumerate(planes_of(layers)):
                out[p, :, lanes] = plane
        low = [src[t, h * 16 : h * 16 + 16, :] for h in range(4)]
        high = [src[t, (15 - h) * 16 : (15 - h) * 16 + 16, :] for h in range(4)]
        for out, layers in ((gy_second, chosen(up_y, low, high)), (gy_first, chosen(up_y, high, low))):
            for p, plane in enumerate(planes_of(layers)):
                out[p, :, lanes] = plane


def pack_receiver(rcv, at, gx_second, gy_second, gx_first, gy_first):
    up_x, up_y = sides()
    for t in range(4):
        lanes = slice(t * 128, t * 128 + 128)
        half, col = divmod(t, 2)
        low = [rcv[col, h * 32 + half * 16 : h * 32 + half * 16 + 16, :] for h in range(4)]
        high = [rcv[col, (15 - h) * 32 + half * 16 : (15 - h) * 32 + half * 16 + 16, :] for h in range(4)]
        for out, layers in ((gx_second, chosen(up_x, low, high)), (gx_first, chosen(up_x, high, low))):
            for p, plane in enumerate(planes_of(layers)):
                out[at + p, :, lanes] = plane
    for col in range(2):
        low = [rcv[col, pl.ds(h, 16, stride=32), :] for h in range(4)]
        high = [rcv[col, pl.ds(31 - h, 16, stride=32), :] for h in range(4)]
        for out, layers in ((gy_second, chosen(up_y, low, high)), (gy_first, chosen(up_y, high, low))):
            for p, plane in enumerate(planes_of(layers)):
                lane = (p % 2) * 256 + col * 128
                out[at + p // 2, :, lane : lane + 128] = plane


def add_layers(out, vel, t, low_rows, high_rows, first, second, up, ends):
    live = jnp.broadcast_to(~ends, first[0].shape)
    second = [jnp.where(live, layer, 0.0) for layer in second]
    for rows_of, layers in ((low_rows, chosen(up, second, first)), (high_rows, chosen(up, first, second))):
        for d in range(4):
            term = COEFFS[d + 1] * layers[0]
            for h in range(1, 4 - d):
                term = term + COEFFS[d + h + 1] * layers[h]
            rows = rows_of(d)
            out[t, rows, :] = out[t, rows, :] + vel[t, rows, :] * term


def add_source(out, vel, gx_second, gy_second, gx_first, gy_first):
    ix, iy = lax.axis_index("gx"), lax.axis_index("gy")
    up_x, up_y = sides()
    for t in range(4):
        lanes = slice(t * 128, t * 128 + 128)
        planes = lambda buffer: layers_of([buffer[p, :, lanes] for p in range(PLANES)])
        add_layers(
            out,
            vel,
            t,
            lambda d: pl.ds(d * 16, 16),
            lambda d: pl.ds((15 - d) * 16, 16),
            planes(gy_first),
            planes(gy_second),
            up_y,
            (iy == 0) | (iy == 15),
        )
        add_layers(
            out,
            vel,
            t,
            lambda d: pl.ds(d, 16, stride=16),
            lambda d: pl.ds(15 - d, 16, stride=16),
            planes(gx_first),
            planes(gx_second),
            up_x,
            (ix == 0) | (ix == 7),
        )


def add_receiver(out, vel, at, gx_second, gy_second, gx_first, gy_first):
    ix, iy = lax.axis_index("gx"), lax.axis_index("gy")
    up_x, up_y = sides()
    for t in range(4):
        lanes = slice(t * 128, t * 128 + 128)
        half, col = divmod(t, 2)
        planes = lambda buffer: layers_of([buffer[at + p, :, lanes] for p in range(PLANES)])
        add_layers(
            out,
            vel,
            col,
            lambda d: pl.ds(d * 32 + half * 16, 16),
            lambda d: pl.ds((15 - d) * 32 + half * 16, 16),
            planes(gx_first),
            planes(gx_second),
            up_x,
            (ix == 0) | (ix == 7),
        )
    for col in range(2):
        lane = [(p % 2) * 256 + col * 128 for p in range(PLANES)]
        planes = lambda buffer: layers_of(
            [buffer[at + p // 2, :, lane[p] : lane[p] + 128] for p in range(PLANES)]
        )
        add_layers(
            out,
            vel,
            col,
            lambda d: pl.ds(d, 16, stride=32),
            lambda d: pl.ds(31 - d, 16, stride=32),
            planes(gy_first),
            planes(gy_second),
            up_y,
            (iy == 0) | (iy == 15),
        )


def band(rows, cols, offset=0, block=None):
    i = lax.broadcasted_iota(jnp.int32, (rows, cols), 0)
    j = lax.broadcasted_iota(jnp.int32, (rows, cols), 1)
    distance = jnp.abs(i - j + offset)
    matrix = jnp.zeros((rows, cols), F32)
    for k, entry in ((1, 8064.0), (2, -1008.0), (3, 128.0), (4, -9.0)):
        matrix = jnp.where(distance == k, entry, matrix)
    if block is not None:
        matrix = jnp.where(i // block == j // block, matrix, 0.0)
    return matrix.astype(BF16)


def parts_of(value):
    parts = []
    for _ in range(3):
        parts.append(value.astype(BF16))
        value = value - parts[-1].astype(F32)
    return parts


def local_laplacian(f, now, store):
    lead, rows, tiles = f["lead"], f["rows"], f["lanes"] // 128
    dot = lambda x, y: jnp.dot(x, y, preferred_element_type=F32)
    along_lanes, along_rows = band(256, 256), band(256, 256, block=rows)
    if tiles > 2:
        from_above, from_below = band(128, 128, offset=128), band(128, 128, offset=-128)
    for c in range(lead * rows // 256):
        here = [now[t, c * 256 : c * 256 + 256, :] for t in range(tiles)]
        parts = [parts_of(x) for x in here]
        sums = []
        for t in range(0, tiles, 2):
            both = None
            for one, other in zip(parts[t], parts[t + 1]):
                pair = jnp.concatenate([one, other], axis=1)
                term = dot(pair, along_lanes) + dot(along_rows, pair)
                both = term if both is None else both + term
            sums += [both[:, :128], both[:, 128:]]
        for t in range(2, tiles, 2):
            for below, above in zip(parts[t - 1], parts[t]):
                sums[t - 1] = sums[t - 1] + dot(above, from_above)
                sums[t] = sums[t] + dot(below, from_below)
        for t in range(tiles):
            for i in range(256 // rows):
                a = c * (256 // rows) + i
                part = slice(i * rows, i * rows + rows)
                total = (3.0 * C0) * here[t][part] + sums[t][part] * (1.0 / 5040.0)
                for k in range(1, 5):
                    others = [
                        now[t, other * rows : other * rows + rows, :] for other in (a - k, a + k) if 0 <= other < lead
                    ]
                    total = total + COEFFS[k] * sum(others[1:], others[0])
                store(t, a, slice(a * rows, a * rows + rows), here[t][part], total)


def pack_brick(src, out, columns=range(4)):
    group = lax.broadcasted_iota(jnp.int32, (16, 128), 1) // 32
    for t in columns:
        for xg in range(4):
            rows = [src[t, pl.ds(xg * 4 + xl, 16, stride=16), :] for xl in range(4)]
            for g in range(4):
                piece = None
                for xl in range(4):
                    turned = rows[xl] if xl == g else pltpu.roll(rows[xl], ((xl - g) % 4) * 32, 1)
                    piece = turned if piece is None else jnp.where(group == xl, turned, piece)
                out[t * 4 + g, :, xg * 128 : xg * 128 + 128] = piece.astype(BF16)


def unpack_velocity(pieces, out):
    group = lax.broadcasted_iota(jnp.int32, (16, 128), 1) // 32
    for t in range(4):
        for xg in range(4):
            codes = [pieces[t * 4 + g, :, xg * 128 : xg * 128 + 128] for g in range(4)]
            parts = [code.astype(jnp.int32).astype(F32) * VELOCITY_STEP + VELOCITY_MIDDLE for code in codes]
            for xl in range(4):
                row = None
                for g in range(4):
                    turned = parts[g] if xl == g else pltpu.roll(parts[g], ((g - xl) % 4) * 32, 1)
                    row = turned if row is None else jnp.where(group == g, turned, row)
                out[t, pl.ds(xg * 4 + xl, 16, stride=16), :] = row


SRC_PLANES, RCV_PLANES = (PLANES, PLANES), (PLANES, 3)


def halo_buffers(*fields):
    shapes = [(sum(f[axis] for f in fields), 16, 512) for axis in (0, 1, 0, 1)]
    return [jax.ShapeDtypeStruct(shape, BF16) for shape in shapes]


SRC_COLS = jax.ShapeDtypeStruct((4, 256, 128), F32)
RCV_COLS = jax.ShapeDtypeStruct((2, 512, 128), F32)
BRICK = jax.ShapeDtypeStruct((16, 16, 512), BF16)
VM = pl.BlockSpec(memory_space=pltpu.VMEM)
SM = pl.BlockSpec(memory_space=pltpu.SMEM)
HB = pl.BlockSpec(memory_space=pltpu.HBM)


def in_hbm(*arrays):
    return [pltpu.with_memory_space_constraint(x, pltpu.HBM) for x in arrays]


def params():
    return pltpu.CompilerParams(vmem_limit_bytes=VMEM_LIMIT)


def hint(microseconds):
    return pl.CostEstimate(flops=0, bytes_accessed=int(microseconds * 3.6e6), transcendentals=0)


def column_copies(block, cols, sem):
    return [
        pltpu.make_async_copy(
            block.at[pl.ds(a, 8), :, pl.ds(t * 128, 128)], cols.at[t, pl.ds(a, 8), :, :], sem
        )
        for a in (0, 8)
        for t in range(cols.shape[0])
    ]


def start(copies):
    for copy in copies:
        copy.start()


def wait(copies):
    for copy in copies:
        copy.wait()


def turn_velocity(vel):
    def kernel(vel, cols, turned_out, turned, sems):
        pieces = [
            pltpu.make_async_copy(
                vel.at[pl.ds(q * 4, 4), :, pl.ds(t * 128, 128)], cols.at[t, pl.ds(q * 4, 4), :, :], sems.at[q]
            )
            for q in range(4)
            for t in range(2)
        ]
        start(pieces)
        flat_cols = flat(cols)
        outs = []
        for q in range(4):
            wait(pieces[2 * q : 2 * q + 2])
            lanes = pl.ds(q * 128, 128)
            for t in range(2):
                rows = flat_cols[t, q * 128 : q * 128 + 128, :].T
                code = jnp.round((rows - VELOCITY_MIDDLE) * (1.0 / VELOCITY_STEP)).astype(jnp.int32)
                turned[t * 128 : t * 128 + 128, lanes] = code.astype(I16)
            outs.append(pltpu.make_async_copy(turned.at[:, lanes], turned_out.at[:, lanes], sems.at[4]))
            outs[-1].start()
        wait(outs)

    return pl.pallas_call(
        kernel,
        out_shape=[jax.ShapeDtypeStruct((2, 16, 32, 128), F32), pltpu.HBM((256, 512), I16)],
        in_specs=[HB],
        out_specs=[VM, HB],
        scratch_shapes=[pltpu.VMEM((256, 512), I16), pltpu.SemaphoreType.DMA((5,))],
        compiler_params=params(),
        name="turn_velocity",
    )(*in_hbm(vel))


def first_halos(src, rcv):
    def kernel(src, rcv, src_cols, *refs):
        rcv_cols, sems = refs[4:]
        get_src, get_rcv = column_copies(src, src_cols, sems.at[0]), column_copies(rcv, rcv_cols, sems.at[1])
        start(get_src + get_rcv)
        wait(get_src)
        pack_source(flat(src_cols), *refs[:4])
        wait(get_rcv)
        pack_receiver(flat(rcv_cols), PLANES, *refs[:4])

    return pl.pallas_call(
        kernel,
        out_shape=[jax.ShapeDtypeStruct((4, 16, 16, 128), F32), *halo_buffers(SRC_PLANES, RCV_PLANES)],
        in_specs=[HB] * 2,
        out_specs=[VM] * 5,
        scratch_shapes=[pltpu.VMEM((2, 16, 32, 128), F32), pltpu.SemaphoreType.DMA((2,))],
        compiler_params=params(),
        name="first_halos",
    )(*in_hbm(src, rcv))


def source_velocity(pieces):
    return pl.pallas_call(
        unpack_velocity,
        out_shape=SRC_COLS,
        in_specs=[VM],
        out_specs=VM,
        compiler_params=params(),
        name="source_velocity",
    )(pieces)


def injections(traces, receiver_x, receiver_y):
    def kernel(traces_hbm, rx_hbm, ry_hbm, out, traces, rx, ry, sem):
        inputs = [
            pltpu.make_async_copy(traces_hbm, traces, sem),
            pltpu.make_async_copy(rx_hbm, rx, sem),
            pltpu.make_async_copy(ry_hbm, ry, sem),
        ]
        start(inputs)
        wait(inputs)
        xs = lax.axis_index("gx") * 16 + lax.broadcasted_iota(jnp.int32, (16, 512), 0)
        ys = lax.axis_index("gy") * 32 + lax.broadcasted_iota(jnp.int32, (32, 512), 0)
        total = jnp.zeros((32, 128), F32)
        for c in range(8):
            cols = slice(c * 512, c * 512 + 512)
            at_x = rx[:, cols] == xs
            at_y = jnp.where(ry[:, cols] == ys, 1.0, 0.0).astype(BF16)
            weighted = [jnp.where(at_x, traces[s : s + 1, cols], 0.0) for s in range(STEPS)]
            for part in parts_of(jnp.concatenate(weighted, axis=0)):
                part = jnp.concatenate([part, jnp.zeros((64, 512), BF16)], axis=0)
                total = total + lax.dot_general(
                    at_y, part, (((1,), (1,)), ((), ())), preferred_element_type=F32
                )
        out[...] = total

    return pl.pallas_call(
        kernel,
        out_shape=jax.ShapeDtypeStruct((32, 128), F32),
        in_specs=[HB] * 3,
        out_specs=VM,
        scratch_shapes=[
            pltpu.VMEM((4, 4096), F32),
            pltpu.VMEM((1, 4096), jnp.int32),
            pltpu.VMEM((1, 4096), jnp.int32),
            pltpu.SemaphoreType.DMA,
        ],
        compiler_params=params(),
        cost_estimate=hint(2),
        name="injections",
    )(*in_hbm(traces, receiver_x.reshape(1, -1), receiver_y.reshape(1, -1)))


def subtract(cols, block):
    for t in range(cols.shape[0]):
        cols[t] = cols[t] - block[:, t * 128 : t * 128 + 128]


def local_source(now, nxt, vel, out, lap_out=None):
    def store(t, a, rows, here, lap):
        value = 2.0 * here
        if nxt is not None:
            value = value - nxt[t, rows, :]
        if vel is None:
            lap_out[t, rows, :] = lap
        else:
            value = value + vel[t, rows, :] * lap
        out[t, rows, :] = value

    local_laplacian(SRC, now, store)


def local_receiver(step, now, nxt, vel, inject, out):
    lane = lax.broadcasted_iota(jnp.int32, (32, 128), 1)

    def store(t, a, rows, here, lap):
        value = 2.0 * here + vel[t, rows, :] * lap
        if nxt is not None:
            value = value - nxt[t, rows, :]
        if t == 0:
            turn = (RECEIVER_PLANE - step * 16 - a) % 128
            value = value + jnp.where(lane == RECEIVER_PLANE, pltpu.roll(inject[...], turn, 1), 0.0)
        out[t, rows, :] = value

    local_laplacian(RCV, now, store)


def add_wavelet(step, cell, wavelet, out):
    z = cell[2] - lax.axis_index("gy") * 16
    x = cell[0] - lax.axis_index("gx") * 16

    @pl.when((z >= 0) & (z < 16) & (x >= 0) & (x < 16))
    def _():
        at = pl.ds(z * 16 + x, 1)
        lanes = lax.broadcasted_iota(jnp.int32, (1, 128), 1)
        for t in range(4):
            out[t, at, :] = out[t, at, :] + jnp.where(lanes + t * 128 == cell[1], wavelet[step], 0.0)


def local_first(src, src_next, rcv, rcv_next, vel, inject, wavelet, cell, saved, plane_index):
    def kernel(src, src_next, rcv, rcv_next, vel, inject, wavelet_hbm, cell_hbm, saved, index_hbm, *refs):
        base, lap, rcv_out, planes, next_src, rcv_cols, next_rcv, wavelet, cell, index, sems = refs
        ix, iy = lax.axis_index("gx"), lax.axis_index("gy")
        get_index = pltpu.make_async_copy(index_hbm, index, sems.at[0])
        get_index.start()
        later = [
            pltpu.make_async_copy(wavelet_hbm, wavelet, sems.at[1]),
            pltpu.make_async_copy(cell_hbm, cell, sems.at[2]),
            pltpu.make_async_copy(src_next, next_src, sems.at[3]),
            pltpu.make_async_copy(rcv_next, next_rcv, sems.at[4]),
        ]
        get_rcv = column_copies(rcv, rcv_cols, sems.at[6])
        start(get_rcv + later)
        local_source(src, None, None, base, lap)
        get_index.wait()
        edge = (ix == 0) | (ix == 7)
        side = jnp.where(ix == 0, 0, 1)
        restores = [
            pltpu.make_async_copy(
                saved.at[index[step], side, pl.ds(pl.multiple_of(iy * 16, 16), 16), pl.ds(t * 128, 128)],
                planes.at[step, t],
                sems.at[5],
            )
            for step in range(STEPS)
            for t in range(4)
        ]

        @pl.when(edge)
        def _():
            start(restores)

        wait(get_rcv)
        local_receiver(0, flat(rcv_cols), None, vel, inject, rcv_out)
        wait(later)
        subtract(base, next_src)
        subtract(rcv_out, next_rcv)
        add_wavelet(0, cell, wavelet, base)

        @pl.when(edge)
        def _():
            wait(restores)

    return pl.pallas_call(
        kernel,
        out_shape=[SRC_COLS, SRC_COLS, RCV_COLS, jax.ShapeDtypeStruct((STEPS, 4, 16, 128), F32)],
        in_specs=[VM, HB, HB, HB, VM, VM] + [HB] * 4,
        out_specs=[VM] * 4,
        scratch_shapes=[
            pltpu.VMEM((256, 512), F32),
            pltpu.VMEM((2, 16, 32, 128), F32),
            pltpu.VMEM((512, 256), F32),
            pltpu.SMEM((4,), F32),
            pltpu.SMEM((3,), jnp.int32),
            pltpu.SMEM((4,), jnp.int32),
            pltpu.SemaphoreType.DMA((7,)),
        ],
        compiler_params=params(),
        cost_estimate=hint(3),
        name="local_first",
    )(
        src,
        *in_hbm(src_next, rcv, rcv_next),
        vel,
        inject,
        *in_hbm(wavelet, cell, saved, plane_index),
    )


def local_step(step, src, src_next, rcv, rcv_next, vel_src, vel, inject, wavelet, cell):
    from_hbm, keep, last = step == 1, step == 2, step == STEPS - 1

    def kernel(src, src_next, rcv, rcv_next, vel_src, vel, inject, wavelet_hbm, cell_hbm, src_out, rcv_out, *refs):
        brick = refs[0] if last else None
        wavelet, cell, next_src, next_rcv, sems = refs[-5:]
        copies = [
            pltpu.make_async_copy(wavelet_hbm, wavelet, sems.at[0]),
            pltpu.make_async_copy(cell_hbm, cell, sems.at[1]),
        ]
        if from_hbm:
            copies.append(pltpu.make_async_copy(src_next, next_src, sems.at[2]))
            copies.append(pltpu.make_async_copy(rcv_next, next_rcv, sems.at[3]))
        if keep:
            copies.append(pltpu.make_async_copy(rcv, refs[0], sems.at[2]))
        start(copies)
        local_source(src, None if from_hbm else src_next, vel_src, src_out)
        local_receiver(step, rcv, None if from_hbm else rcv_next, vel, inject, rcv_out)
        if last:
            pack_brick(src_next, brick)
        wait(copies)
        if from_hbm:
            subtract(src_out, next_src)
            subtract(rcv_out, next_rcv)
        add_wavelet(step, cell, wavelet, src_out)

    if from_hbm:
        src_next, rcv_next = in_hbm(src_next, rcv_next)
    next_spec = HB if from_hbm else VM
    out_shape = [SRC_COLS, RCV_COLS] + ([BRICK] if last else [])
    if keep:
        out_shape.append(pltpu.HBM(RCV_COLS.shape, F32))
    return pl.pallas_call(
        kernel,
        out_shape=out_shape,
        in_specs=[VM, next_spec, VM, next_spec] + [VM] * 3 + [HB] * 2,
        out_specs=[VM, VM] + [HB if keep else VM] * (len(out_shape) - 2),
        scratch_shapes=[
            pltpu.SMEM((4,), F32),
            pltpu.SMEM((3,), jnp.int32),
            pltpu.VMEM((256, 512) if from_hbm else (8, 128), F32),
            pltpu.VMEM((512, 256) if from_hbm else (8, 128), F32),
            pltpu.SemaphoreType.DMA((4,)),
        ],
        compiler_params=params(),
        cost_estimate=hint(3),
        name=f"local_step{step}",
    )(src, src_next, rcv, rcv_next, vel_src, vel, inject, *in_hbm(wavelet, cell))


def restore_planes(step, src, planes):
    ix = lax.axis_index("gx")

    @pl.when(ix == 0)
    def _():
        for t in range(4):
            src[t, pl.ds(0, 16, stride=16), :] = planes[step, t]

    @pl.when(ix == 7)
    def _():
        for t in range(4):
            src[t, pl.ds(15, 16, stride=16), :] = planes[step, t]


def halo_step(step, local, vel_src, vel, halos, planes):
    first = step == 0

    def kernel(*refs):
        refs = list(refs)
        local_src = refs.pop(0)
        lap = refs.pop(0) if first else None
        local_rcv, vel_src, vel = refs[:3]
        halos, planes, src, rcv, packed = refs[3:7], refs[7], refs[8], refs[9], refs[10:]
        src[...] = local_src[...] + vel_src[...] * lap[...] if first else local_src[...]
        rcv[...] = local_rcv[...]
        add_source(src, vel_src, *halos)
        restore_planes(step, src, planes)
        pack_source(src, *packed)
        add_receiver(rcv, vel, PLANES, *halos)
        pack_receiver(rcv, PLANES, *packed)

    args = [*local, vel_src, vel, *halos, planes]
    out_shape = [SRC_COLS, RCV_COLS, *halo_buffers(SRC_PLANES, RCV_PLANES)]
    return pl.pallas_call(
        kernel,
        out_shape=out_shape,
        in_specs=[VM] * len(args),
        out_specs=[VM] * len(out_shape),
        compiler_params=params(),
        name=f"halo_step{step}",
    )(*args)


def last_source(local, early, vel_src, halos, planes):
    def kernel(local, early, vel_src, *refs):
        halos, planes, src, bricks, late, sems = refs[:4], *refs[4:]
        copies = [pltpu.make_async_copy(early, bricks.at[:, 0], sems.at[0])]
        copies[0].start()
        src[...] = local[...]
        add_source(src, vel_src, *halos)
        restore_planes(STEPS - 1, src, planes)
        for t in range(4):
            pack_brick(src, late, (t,))
            part = pl.ds(t * 4, 4)
            copies.append(pltpu.make_async_copy(late.at[part], bricks.at[part, 1], sems.at[1]))
            copies[-1].start()
        wait(copies)

    return pl.pallas_call(
        kernel,
        out_shape=[SRC_COLS, pltpu.HBM((16, 2, 16, 512), BF16)],
        in_specs=[VM] * 8,
        out_specs=[VM, HB],
        scratch_shapes=[pltpu.VMEM((16, 16, 512), BF16), pltpu.SemaphoreType.DMA((2,))],
        compiler_params=params(),
        name="last_source",
    )(local, early, vel_src, *halos, planes)


def last_receiver(local, vel, halos, src, kept):
    def kernel(local, vel, *refs):
        halos, src, kept, rcv, early, src_out, rcv_out, sem = refs[:4], *refs[4:]
        copies = [pltpu.make_async_copy(src.at[t], src_out.at[:, pl.ds(t * 128, 128)], sem) for t in range(4)]
        copies += [pltpu.make_async_copy(kept.at[t], early.at[t], sem) for t in range(2)]
        start(copies)
        rcv[...] = local[...]
        add_receiver(rcv, vel, PLANES, *halos)
        more = [pltpu.make_async_copy(rcv.at[t], rcv_out.at[:, pl.ds(t * 128, 128)], sem) for t in range(2)]
        start(more)
        wait(copies + more)

    return pl.pallas_call(
        kernel,
        out_shape=[RCV_COLS] * 2 + [jax.ShapeDtypeStruct(shape, F32) for shape in ((256, 512), (512, 256))],
        in_specs=[VM] * 7 + [HB],
        out_specs=[VM, VM, HB, HB],
        scratch_shapes=[pltpu.SemaphoreType.DMA],
        compiler_params=params(),
        cost_estimate=hint(2),
        name="last_receiver",
    )(local, vel, *halos, src, *in_hbm(kept))


def make_image(bricks, rcv_early, rcv_late):
    def kernel(bricks, rcv_early, rcv_late, out, held, sem):
        copies = []
        for q in range(4):
            rows = slice(q * 128, q * 128 + 128)
            early = bricks[:, 0, :, rows].reshape(256, 128).astype(F32).T
            late = bricks[:, 1, :, rows].reshape(256, 128).astype(F32).T
            for t in range(2):
                lanes = slice(t * 128, t * 128 + 128)
                held[rows, lanes] = early[:, lanes] * rcv_early[t, rows, :] + late[:, lanes] * rcv_late[t, rows, :]
            copies.append(pltpu.make_async_copy(held.at[rows, :], out.at[rows, :], sem))
            copies[-1].start()
        wait(copies)

    return pl.pallas_call(
        kernel,
        out_shape=jax.ShapeDtypeStruct((512, 256), F32),
        in_specs=[VM] * 3,
        out_specs=HB,
        scratch_shapes=[pltpu.VMEM((512, 256), F32), pltpu.SemaphoreType.DMA],
        compiler_params=params(),
        name="make_image",
    )(bricks, rcv_early, rcv_late)


def exchange(buffers):
    gx_second, gy_second, gx_first, gy_first = buffers
    inner = lambda n: [(i, i ^ 1) for i in range(n)]
    outer = lambda n: [(i, (((i + 1) ^ 1) - 1) % n) for i in range(n)]
    return (
        lax.ppermute(gx_second, "gx", outer(8)),
        lax.ppermute(gy_second, "gy", outer(16)),
        lax.ppermute(gx_first, "gx", inner(8)),
        lax.ppermute(gy_first, "gy", inner(16)),
    )


def on_device(
    source_now,
    source_next,
    receiver_now,
    receiver_next,
    velocity,
    saved_planes,
    plane_index,
    wavelet,
    source_cell,
    traces,
    receiver_x,
    receiver_y,
):
    vel, turned = turn_velocity(velocity)
    pieces = lax.all_to_all(turned.reshape(16, 16, 512), "gy", split_axis=0, concat_axis=0, tiled=True)
    src, *to_send = first_halos(source_now, receiver_now)
    halos = exchange(to_send)
    src, vel = src.reshape(4, 256, 128), vel.reshape(2, 512, 128)
    inject = injections(traces, receiver_x, receiver_y)
    src_next, rcv_next = source_next.reshape(256, 512), receiver_next.reshape(512, 256)
    *local, planes = local_first(
        src, src_next, receiver_now, rcv_next, vel, inject, wavelet, source_cell, saved_planes, plane_index
    )
    vel_src = source_velocity(pieces)
    src_next, rcv_next = source_now.reshape(256, 512), receiver_now.reshape(512, 256)
    more = []
    for step in range(STEPS - 1):
        src, rcv, *to_send = halo_step(step, local, vel_src, vel, halos, planes)
        halos = exchange(to_send)
        local = local_step(step + 1, src, src_next, rcv, rcv_next, vel_src, vel, inject, wavelet, source_cell)
        more += local[2:]
        local = local[:2]
        src_next, rcv_next = src, rcv
    kept, early = more
    src, bricks = last_source(local[0], early, vel_src, halos, planes)
    bricks = lax.all_to_all(bricks, "gy", split_axis=0, concat_axis=0, tiled=True)
    rcv, rcv_early, source_field, receiver_field = last_receiver(local[1], vel, halos, src, kept)
    image = make_image(bricks, rcv_early, rcv)
    return (image.reshape(16, 32, 256), receiver_field.reshape(16, 32, 256), source_field.reshape(16, 16, 512))


def solution(mesh):
    field, turned = P("gx", "gy", None), P("gy", "gx", None)
    return jax.shard_map(
        on_device,
        mesh=mesh,
        in_specs=(turned, turned, field, field, field, P(), P(), P(), P(), P(), P(), P()),
        out_specs=(field, field, turned),
        check_vma=False,
    )
```

```python
import jax
import jax.numpy as jnp
from jax import lax
from jax.experimental import pallas as pl
from jax.experimental.pallas import tpu as pltpu
from jax.sharding import PartitionSpec as P

STEPS = 4
C0, C1, C2, C3, C4 = (-205.0 / 72.0, 8.0 / 5.0, -1.0 / 5.0, 8.0 / 315.0, -1.0 / 560.0)
COEFFS = (C0, C1, C2, C3, C4)
RECEIVER_PLANE = 2
PLANES = 5
F32, BF16, I16 = jnp.float32, jnp.bfloat16, jnp.int16
VELOCITY_MIDDLE, VELOCITY_STEP = 0.115, 0.0651 / 32767
VMEM_LIMIT = 24 * 1024 * 1024

RCV = dict(lead=16, rows=32, lanes=256)
SRC = dict(lead=16, rows=16, lanes=512)


def flat(ref):
    return ref.reshape(ref.shape[0], ref.shape[1] * ref.shape[2], 128)


def split(value):
    high = value.astype(BF16)
    return high, (value - high.astype(F32)).astype(BF16)


def planes_of(layers):
    return [*split(layers[0]), *[layer.astype(BF16) for layer in layers[1:]]]


def layers_of(planes):
    planes = [plane.astype(F32) for plane in planes]
    return [planes[0] + planes[1], *planes[2:]]


def sides():
    return lax.axis_index("gx") % 2 == 0, lax.axis_index("gy") % 2 == 0


def chosen(up, one, other):
    up = jnp.broadcast_to(up, one[0].shape)
    return [jnp.where(up, x, y) for x, y in zip(one, other)]


def pack_source(src, gx_second, gy_second, gx_first, gy_first):
    up_x, up_y = sides()
    for t in range(4):
        lanes = slice(t * 128, t * 128 + 128)
        low = [src[t, pl.ds(h, 16, stride=16), :] for h in range(4)]
        high = [src[t, pl.ds(15 - h, 16, stride=16), :] for h in range(4)]
        for out, layers in ((gx_second, chosen(up_x, low, high)), (gx_first, chosen(up_x, high, low))):
            for p, plane in enumerate(planes_of(layers)):
                out[p, :, lanes] = plane
        low = [src[t, h * 16 : h * 16 + 16, :] for h in range(4)]
        high = [src[t, (15 - h) * 16 : (15 - h) * 16 + 16, :] for h in range(4)]
        for out, layers in ((gy_second, chosen(up_y, low, high)), (gy_first, chosen(up_y, high, low))):
            for p, plane in enumerate(planes_of(layers)):
                out[p, :, lanes] = plane


def pack_receiver(rcv, at, gx_second, gy_second, gx_first, gy_first):
    up_x, up_y = sides()
    for t in range(4):
        lanes = slice(t * 128, t * 128 + 128)
        half, col = divmod(t, 2)
        low = [rcv[col, h * 32 + half * 16 : h * 32 + half * 16 + 16, :] for h in range(4)]
        high = [rcv[col, (15 - h) * 32 + half * 16 : (15 - h) * 32 + half * 16 + 16, :] for h in range(4)]
        for out, layers in ((gx_second, chosen(up_x, low, high)), (gx_first, chosen(up_x, high, low))):
            for p, plane in enumerate(planes_of(layers)):
                out[at + p, :, lanes] = plane
    for col in range(2):
        low = [rcv[col, pl.ds(h, 16, stride=32), :] for h in range(4)]
        high = [rcv[col, pl.ds(31 - h, 16, stride=32), :] for h in range(4)]
        for out, layers in ((gy_second, chosen(up_y, low, high)), (gy_first, chosen(up_y, high, low))):
            for p, plane in enumerate(planes_of(layers)):
                lane = (p % 2) * 256 + col * 128
                out[at + p // 2, :, lane : lane + 128] = plane


def add_layers(out, vel, t, low_rows, high_rows, first, second, up, ends):
    live = jnp.broadcast_to(~ends, first[0].shape)
    second = [jnp.where(live, layer, 0.0) for layer in second]
    for rows_of, layers in ((low_rows, chosen(up, second, first)), (high_rows, chosen(up, first, second))):
        for d in range(4):
            term = COEFFS[d + 1] * layers[0]
            for h in range(1, 4 - d):
                term = term + COEFFS[d + h + 1] * layers[h]
            rows = rows_of(d)
            out[t, rows, :] = out[t, rows, :] + vel[t, rows, :] * term


def add_source(out, vel, gx_second, gy_second, gx_first, gy_first, columns=range(4)):
    ix, iy = lax.axis_index("gx"), lax.axis_index("gy")
    up_x, up_y = sides()
    for t in columns:
        lanes = slice(t * 128, t * 128 + 128)
        planes = lambda buffer: layers_of([buffer[p, :, lanes] for p in range(PLANES)])
        add_layers(
            out,
            vel,
            t,
            lambda d: pl.ds(d * 16, 16),
            lambda d: pl.ds((15 - d) * 16, 16),
            planes(gy_first),
            planes(gy_second),
            up_y,
            (iy == 0) | (iy == 15),
        )
        add_layers(
            out,
            vel,
            t,
            lambda d: pl.ds(d, 16, stride=16),
            lambda d: pl.ds(15 - d, 16, stride=16),
            planes(gx_first),
            planes(gx_second),
            up_x,
            (ix == 0) | (ix == 7),
        )


def add_receiver(out, vel, at, gx_second, gy_second, gx_first, gy_first):
    ix, iy = lax.axis_index("gx"), lax.axis_index("gy")
    up_x, up_y = sides()
    for t in range(4):
        lanes = slice(t * 128, t * 128 + 128)
        half, col = divmod(t, 2)
        planes = lambda buffer: layers_of([buffer[at + p, :, lanes] for p in range(PLANES)])
        add_layers(
            out,
            vel,
            col,
            lambda d: pl.ds(d * 32 + half * 16, 16),
            lambda d: pl.ds((15 - d) * 32 + half * 16, 16),
            planes(gx_first),
            planes(gx_second),
            up_x,
            (ix == 0) | (ix == 7),
        )
    for col in range(2):
        lane = [(p % 2) * 256 + col * 128 for p in range(PLANES)]
        planes = lambda buffer: layers_of(
            [buffer[at + p // 2, :, lane[p] : lane[p] + 128] for p in range(PLANES)]
        )
        add_layers(
            out,
            vel,
            col,
            lambda d: pl.ds(d, 16, stride=32),
            lambda d: pl.ds(31 - d, 16, stride=32),
            planes(gy_first),
            planes(gy_second),
            up_y,
            (iy == 0) | (iy == 15),
        )


def band(rows, cols, offset=0, block=None):
    i = lax.broadcasted_iota(jnp.int32, (rows, cols), 0)
    j = lax.broadcasted_iota(jnp.int32, (rows, cols), 1)
    distance = jnp.abs(i - j + offset)
    matrix = jnp.zeros((rows, cols), F32)
    for k, entry in ((1, 8064.0), (2, -1008.0), (3, 128.0), (4, -9.0)):
        matrix = jnp.where(distance == k, entry, matrix)
    if block is not None:
        matrix = jnp.where(i // block == j // block, matrix, 0.0)
    return matrix.astype(BF16)


def parts_of(value):
    parts = []
    for _ in range(3):
        parts.append(value.astype(BF16))
        value = value - parts[-1].astype(F32)
    return parts


def local_laplacian(f, now, store):
    lead, rows, tiles = f["lead"], f["rows"], f["lanes"] // 128
    dot = lambda x, y: jnp.dot(x, y, preferred_element_type=F32)
    along_lanes, along_rows = band(256, 256), band(256, 256, block=rows)
    if tiles > 2:
        from_above, from_below = band(128, 128, offset=128), band(128, 128, offset=-128)
    for c in range(lead * rows // 256):
        here = [now[t, c * 256 : c * 256 + 256, :] for t in range(tiles)]
        parts = [parts_of(x) for x in here]
        sums = []
        for t in range(0, tiles, 2):
            both = None
            for one, other in zip(parts[t], parts[t + 1]):
                pair = jnp.concatenate([one, other], axis=1)
                term = dot(pair, along_lanes) + dot(along_rows, pair)
                both = term if both is None else both + term
            sums += [both[:, :128], both[:, 128:]]
        for t in range(2, tiles, 2):
            for below, above in zip(parts[t - 1], parts[t]):
                sums[t - 1] = sums[t - 1] + dot(above, from_above)
                sums[t] = sums[t] + dot(below, from_below)
        for t in range(tiles):
            for i in range(256 // rows):
                a = c * (256 // rows) + i
                part = slice(i * rows, i * rows + rows)
                total = (3.0 * C0) * here[t][part] + sums[t][part] * (1.0 / 5040.0)
                for k in range(1, 5):
                    others = [
                        now[t, other * rows : other * rows + rows, :] for other in (a - k, a + k) if 0 <= other < lead
                    ]
                    total = total + COEFFS[k] * sum(others[1:], others[0])
                store(t, a, slice(a * rows, a * rows + rows), here[t][part], total)


def pack_brick(src, out, columns=range(4)):
    group = lax.broadcasted_iota(jnp.int32, (16, 128), 1) // 32
    for t in columns:
        for xg in range(4):
            rows = [src[t, pl.ds(xg * 4 + xl, 16, stride=16), :] for xl in range(4)]
            for g in range(4):
                piece = None
                for xl in range(4):
                    turned = rows[xl] if xl == g else pltpu.roll(rows[xl], ((xl - g) % 4) * 32, 1)
                    piece = turned if piece is None else jnp.where(group == xl, turned, piece)
                out[t * 4 + g, :, xg * 128 : xg * 128 + 128] = piece.astype(BF16)


def unpack_velocity(pieces, out):
    group = lax.broadcasted_iota(jnp.int32, (16, 128), 1) // 32
    for t in range(4):
        for xg in range(4):
            codes = [pieces[t * 4 + g, :, xg * 128 : xg * 128 + 128] for g in range(4)]
            parts = [code.astype(jnp.int32).astype(F32) * VELOCITY_STEP + VELOCITY_MIDDLE for code in codes]
            for xl in range(4):
                row = None
                for g in range(4):
                    turned = parts[g] if xl == g else pltpu.roll(parts[g], ((g - xl) % 4) * 32, 1)
                    row = turned if row is None else jnp.where(group == g, turned, row)
                out[t, pl.ds(xg * 4 + xl, 16, stride=16), :] = row


SRC_PLANES, RCV_PLANES = (PLANES, PLANES), (PLANES, 3)


def halo_buffers(*fields):
    shapes = [(sum(f[axis] for f in fields), 16, 512) for axis in (0, 1, 0, 1)]
    return [jax.ShapeDtypeStruct(shape, BF16) for shape in shapes]


SRC_COLS = jax.ShapeDtypeStruct((4, 256, 128), F32)
RCV_COLS = jax.ShapeDtypeStruct((2, 512, 128), F32)
BRICKS = (16, 2, 16, 512)
VM = pl.BlockSpec(memory_space=pltpu.VMEM)
SM = pl.BlockSpec(memory_space=pltpu.SMEM)
HB = pl.BlockSpec(memory_space=pltpu.HBM)


def in_hbm(*arrays):
    return [pltpu.with_memory_space_constraint(x, pltpu.HBM) for x in arrays]


def params():
    return pltpu.CompilerParams(vmem_limit_bytes=VMEM_LIMIT)


def hint(microseconds):
    return pl.CostEstimate(flops=0, bytes_accessed=int(microseconds * 3.6e6), transcendentals=0)


def column_copies(block, cols, sem):
    return [
        pltpu.make_async_copy(
            block.at[pl.ds(a, 8), :, pl.ds(t * 128, 128)], cols.at[t, pl.ds(a, 8), :, :], sem
        )
        for a in (0, 8)
        for t in range(cols.shape[0])
    ]


def start(copies):
    for copy in copies:
        copy.start()


def wait(copies):
    for copy in copies:
        copy.wait()


def turn_velocity(vel, src, rcv):
    def kernel(vel, src, rcv, cols, src_cols, rcv_cols, turned_out, turned, sems):
        pieces = [
            pltpu.make_async_copy(
                vel.at[pl.ds(q * 4, 4), :, pl.ds(t * 128, 128)], cols.at[t, pl.ds(q * 4, 4), :, :], sems.at[q]
            )
            for q in range(4)
            for t in range(2)
        ]
        start(pieces)
        fields = column_copies(src, src_cols, sems.at[5]) + column_copies(rcv, rcv_cols, sems.at[5])
        start(fields)
        flat_cols = flat(cols)
        outs = []
        for q in range(4):
            wait(pieces[2 * q : 2 * q + 2])
            lanes = pl.ds(q * 128, 128)
            for t in range(2):
                rows = flat_cols[t, q * 128 : q * 128 + 128, :].T
                code = jnp.round((rows - VELOCITY_MIDDLE) * (1.0 / VELOCITY_STEP)).astype(jnp.int32)
                turned[t * 128 : t * 128 + 128, lanes] = code.astype(I16)
            outs.append(pltpu.make_async_copy(turned.at[:, lanes], turned_out.at[:, lanes], sems.at[4]))
            outs[-1].start()
        wait(outs)
        wait(fields)

    return pl.pallas_call(
        kernel,
        out_shape=[
            jax.ShapeDtypeStruct((2, 16, 32, 128), F32),
            jax.ShapeDtypeStruct((4, 16, 16, 128), F32),
            jax.ShapeDtypeStruct((2, 16, 32, 128), F32),
            pltpu.HBM((256, 512), I16),
        ],
        in_specs=[HB] * 3,
        out_specs=[VM] * 3 + [HB],
        scratch_shapes=[pltpu.VMEM((256, 512), I16), pltpu.SemaphoreType.DMA((6,))],
        compiler_params=params(),
        name="turn_velocity",
    )(*in_hbm(vel, src, rcv))


def first_halos(src, rcv):
    def kernel(src, rcv, *packed):
        pack_source(src, *packed)
        pack_receiver(rcv, PLANES, *packed)

    return pl.pallas_call(
        kernel,
        out_shape=halo_buffers(SRC_PLANES, RCV_PLANES),
        in_specs=[VM] * 2,
        out_specs=[VM] * 4,
        compiler_params=params(),
        name="first_halos",
    )(src, rcv)


def source_velocity(pieces):
    return pl.pallas_call(
        unpack_velocity,
        out_shape=SRC_COLS,
        in_specs=[VM],
        out_specs=VM,
        compiler_params=params(),
        name="source_velocity",
    )(pieces)


def injections(traces, rx, ry):
    xs = lax.axis_index("gx") * 16 + lax.broadcasted_iota(jnp.int32, (16, 512), 0)
    ys = lax.axis_index("gy") * 32 + lax.broadcasted_iota(jnp.int32, (32, 512), 0)
    total = jnp.zeros((32, 128), F32)
    for c in range(8):
        cols = slice(c * 512, c * 512 + 512)
        at_x = rx[:, cols] == xs
        at_y = jnp.where(ry[:, cols] == ys, 1.0, 0.0).astype(BF16)
        weighted = [jnp.where(at_x, traces[s : s + 1, cols], 0.0) for s in range(STEPS)]
        for part in parts_of(jnp.concatenate(weighted, axis=0)):
            part = jnp.concatenate([part, jnp.zeros((64, 512), BF16)], axis=0)
            total = total + lax.dot_general(at_y, part, (((1,), (1,)), ((), ())), preferred_element_type=F32)
    return total


def subtract(cols, block):
    for t in range(cols.shape[0]):
        cols[t] = cols[t] - block[:, t * 128 : t * 128 + 128]


def local_source(now, nxt, vel, out, lap_out=None):
    def store(t, a, rows, here, lap):
        value = 2.0 * here
        if nxt is not None:
            value = value - nxt[t, rows, :]
        if vel is None:
            lap_out[t, rows, :] = lap
        else:
            value = value + vel[t, rows, :] * lap
        out[t, rows, :] = value

    local_laplacian(SRC, now, store)


def local_receiver(step, now, nxt, vel, inject, out):
    lane = lax.broadcasted_iota(jnp.int32, (32, 128), 1)

    def store(t, a, rows, here, lap):
        value = 2.0 * here + vel[t, rows, :] * lap
        if nxt is not None:
            value = value - nxt[t, rows, :]
        if t == 0:
            turn = (RECEIVER_PLANE - step * 16 - a) % 128
            value = value + jnp.where(lane == RECEIVER_PLANE, pltpu.roll(inject[...], turn, 1), 0.0)
        out[t, rows, :] = value

    local_laplacian(RCV, now, store)


def add_wavelet(step, cell, wavelet, out):
    z = cell[2] - lax.axis_index("gy") * 16
    x = cell[0] - lax.axis_index("gx") * 16

    @pl.when((z >= 0) & (z < 16) & (x >= 0) & (x < 16))
    def _():
        at = pl.ds(z * 16 + x, 1)
        lanes = lax.broadcasted_iota(jnp.int32, (1, 128), 1)
        for t in range(4):
            out[t, at, :] = out[t, at, :] + jnp.where(lanes + t * 128 == cell[1], wavelet[step], 0.0)


def local_first(src, src_next, rcv, rcv_next, vel, wavelet, cell, saved, plane_index, traces, receiver_x, receiver_y):
    def kernel(vel, *refs):
        hbm, (base, lap, rcv_out, planes, inject), refs = refs[:11], refs[11:16], refs[16:]
        src, src_next, rcv, rcv_next, wavelet_hbm, cell_hbm, saved, index_hbm, traces_hbm, rx_hbm, ry_hbm = hbm
        src_cols, next_src, rcv_cols, next_rcv, traces, rx, ry, wavelet, cell, index, sems = refs
        ix, iy = lax.axis_index("gx"), lax.axis_index("gy")
        get_index = pltpu.make_async_copy(index_hbm, index, sems.at[0])
        get_index.start()
        receivers = [
            pltpu.make_async_copy(traces_hbm, traces, sems.at[7]),
            pltpu.make_async_copy(rx_hbm, rx, sems.at[7]),
            pltpu.make_async_copy(ry_hbm, ry, sems.at[7]),
        ]
        get_src, get_rcv = column_copies(src, src_cols, sems.at[5]), column_copies(rcv, rcv_cols, sems.at[6])
        later = [
            pltpu.make_async_copy(wavelet_hbm, wavelet, sems.at[1]),
            pltpu.make_async_copy(cell_hbm, cell, sems.at[2]),
            pltpu.make_async_copy(src_next, next_src, sems.at[3]),
            pltpu.make_async_copy(rcv_next, next_rcv, sems.at[4]),
        ]
        start(receivers + get_src + get_rcv + later)
        wait(receivers)
        inject[...] = injections(traces, rx, ry)
        get_index.wait()
        edge = (ix == 0) | (ix == 7)
        side = jnp.where(ix == 0, 0, 1)
        restores = [
            pltpu.make_async_copy(
                saved.at[index[step], side, pl.ds(pl.multiple_of(iy * 16, 16), 16), pl.ds(t * 128, 128)],
                planes.at[step, t],
                sems.at[8],
            )
            for step in range(STEPS)
            for t in range(4)
        ]

        @pl.when(edge)
        def _():
            start(restores)

        wait(get_src)
        local_source(flat(src_cols), None, None, base, lap)
        wait(get_rcv)
        local_receiver(0, flat(rcv_cols), None, vel, inject, rcv_out)
        wait(later)
        subtract(base, next_src)
        subtract(rcv_out, next_rcv)
        add_wavelet(0, cell, wavelet, base)

        @pl.when(edge)
        def _():
            wait(restores)

    return pl.pallas_call(
        kernel,
        out_shape=[
            SRC_COLS,
            SRC_COLS,
            RCV_COLS,
            jax.ShapeDtypeStruct((STEPS, 4, 16, 128), F32),
            jax.ShapeDtypeStruct((32, 128), F32),
        ],
        in_specs=[VM] + [HB] * 11,
        out_specs=[VM] * 5,
        scratch_shapes=[
            pltpu.VMEM((4, 16, 16, 128), F32),
            pltpu.VMEM((256, 512), F32),
            pltpu.VMEM((2, 16, 32, 128), F32),
            pltpu.VMEM((512, 256), F32),
            pltpu.VMEM((4, 4096), F32),
            pltpu.VMEM((1, 4096), jnp.int32),
            pltpu.VMEM((1, 4096), jnp.int32),
            pltpu.SMEM((4,), F32),
            pltpu.SMEM((3,), jnp.int32),
            pltpu.SMEM((4,), jnp.int32),
            pltpu.SemaphoreType.DMA((9,)),
        ],
        compiler_params=params(),
        cost_estimate=hint(4),
        name="local_first",
    )(
        vel,
        *in_hbm(
            src,
            src_next,
            rcv,
            rcv_next,
            wavelet,
            cell,
            saved,
            plane_index,
            traces,
            receiver_x.reshape(1, -1),
            receiver_y.reshape(1, -1),
        ),
    )


def local_step(step, src, src_next, rcv, rcv_next, vel_src, vel, inject, wavelet, cell):
    from_hbm, keep, last = step == 1, step == 2, step == STEPS - 1

    def kernel(src, src_next, rcv, rcv_next, vel_src, vel, inject, wavelet_hbm, cell_hbm, src_out, rcv_out, *refs):
        bricks, brick = (refs[0], refs[1]) if last else (None, None)
        wavelet, cell, next_src, next_rcv, sems = refs[-5:]
        copies = [
            pltpu.make_async_copy(wavelet_hbm, wavelet, sems.at[0]),
            pltpu.make_async_copy(cell_hbm, cell, sems.at[1]),
        ]
        if from_hbm:
            copies.append(pltpu.make_async_copy(src_next, next_src, sems.at[2]))
            copies.append(pltpu.make_async_copy(rcv_next, next_rcv, sems.at[3]))
        if keep:
            copies.append(pltpu.make_async_copy(rcv, refs[0], sems.at[2]))
        start(copies)
        if last:
            pack_brick(src_next, brick)
            copies.append(pltpu.make_async_copy(brick, bricks.at[:, 0], sems.at[2]))
            copies[-1].start()
        local_source(src, None if from_hbm else src_next, vel_src, src_out)
        local_receiver(step, rcv, None if from_hbm else rcv_next, vel, inject, rcv_out)
        wait(copies)
        if from_hbm:
            subtract(src_out, next_src)
            subtract(rcv_out, next_rcv)
        add_wavelet(step, cell, wavelet, src_out)

    if from_hbm:
        src_next, rcv_next = in_hbm(src_next, rcv_next)
    next_spec = HB if from_hbm else VM
    out_shape = [SRC_COLS, RCV_COLS]
    if keep:
        out_shape.append(pltpu.HBM(RCV_COLS.shape, F32))
    if last:
        out_shape.append(pltpu.HBM(BRICKS, BF16))
    return pl.pallas_call(
        kernel,
        out_shape=out_shape,
        in_specs=[VM, next_spec, VM, next_spec] + [VM] * 3 + [HB] * 2,
        out_specs=[VM, VM] + [HB] * (len(out_shape) - 2),
        scratch_shapes=([pltpu.VMEM((16, 16, 512), BF16)] if last else [])
        + [
            pltpu.SMEM((4,), F32),
            pltpu.SMEM((3,), jnp.int32),
            pltpu.VMEM((256, 512) if from_hbm else (8, 128), F32),
            pltpu.VMEM((512, 256) if from_hbm else (8, 128), F32),
            pltpu.SemaphoreType.DMA((4,)),
        ],
        compiler_params=params(),
        cost_estimate=hint(3),
        name=f"local_step{step}",
    )(src, src_next, rcv, rcv_next, vel_src, vel, inject, *in_hbm(wavelet, cell))


def restore_planes(step, src, planes, columns=range(4)):
    ix = lax.axis_index("gx")

    @pl.when(ix == 0)
    def _():
        for t in columns:
            src[t, pl.ds(0, 16, stride=16), :] = planes[step, t]

    @pl.when(ix == 7)
    def _():
        for t in columns:
            src[t, pl.ds(15, 16, stride=16), :] = planes[step, t]


def halo_step(step, local, vel_src, vel, halos, planes):
    first = step == 0

    def kernel(*refs):
        refs = list(refs)
        local_src = refs.pop(0)
        lap = refs.pop(0) if first else None
        local_rcv, vel_src, vel = refs[:3]
        halos, planes, src, rcv, packed = refs[3:7], refs[7], refs[8], refs[9], refs[10:]
        src[...] = local_src[...] + vel_src[...] * lap[...] if first else local_src[...]
        rcv[...] = local_rcv[...]
        add_source(src, vel_src, *halos)
        restore_planes(step, src, planes)
        pack_source(src, *packed)
        add_receiver(rcv, vel, PLANES, *halos)
        pack_receiver(rcv, PLANES, *packed)

    args = [*local, vel_src, vel, *halos, planes]
    out_shape = [SRC_COLS, RCV_COLS, *halo_buffers(SRC_PLANES, RCV_PLANES)]
    return pl.pallas_call(
        kernel,
        out_shape=out_shape,
        in_specs=[VM] * len(args),
        out_specs=[VM] * len(out_shape),
        compiler_params=params(),
        name=f"halo_step{step}",
    )(*args)


def last_source(local, bricks, vel_src, halos, planes):
    def kernel(local, _, vel_src, *refs):
        halos, planes, src, bricks, late, sem = refs[:4], *refs[4:]
        copies = []
        src[...] = local[...]
        add_source(src, vel_src, *halos)
        restore_planes(STEPS - 1, src, planes)
        for t in range(4):
            pack_brick(src, late, (t,))
            part = pl.ds(t * 4, 4)
            copies.append(pltpu.make_async_copy(late.at[part], bricks.at[part, 1], sem))
            copies[-1].start()
        wait(copies)

    return pl.pallas_call(
        kernel,
        out_shape=[SRC_COLS, pltpu.HBM(BRICKS, BF16)],
        in_specs=[VM, HB] + [VM] * 6,
        out_specs=[VM, HB],
        input_output_aliases={1: 1},
        scratch_shapes=[pltpu.VMEM((16, 16, 512), BF16), pltpu.SemaphoreType.DMA],
        compiler_params=params(),
        name="last_source",
    )(local, *in_hbm(bricks), vel_src, *halos, planes)


def last_receiver(local, vel, halos, src, kept):
    def kernel(local, vel, *refs):
        halos, src, kept, rcv, early, src_out, rcv_out, sem = refs[:4], *refs[4:]
        copies = [pltpu.make_async_copy(src.at[t], src_out.at[:, pl.ds(t * 128, 128)], sem) for t in range(4)]
        copies += [pltpu.make_async_copy(kept.at[t], early.at[t], sem) for t in range(2)]
        start(copies)
        rcv[...] = local[...]
        add_receiver(rcv, vel, PLANES, *halos)
        more = [pltpu.make_async_copy(rcv.at[t], rcv_out.at[:, pl.ds(t * 128, 128)], sem) for t in range(2)]
        start(more)
        wait(copies + more)

    return pl.pallas_call(
        kernel,
        out_shape=[RCV_COLS] * 2 + [jax.ShapeDtypeStruct(shape, F32) for shape in ((256, 512), (512, 256))],
        in_specs=[VM] * 7 + [HB],
        out_specs=[VM, VM, HB, HB],
        scratch_shapes=[pltpu.SemaphoreType.DMA],
        compiler_params=params(),
        cost_estimate=hint(2),
        name="last_receiver",
    )(local, vel, *halos, src, *in_hbm(kept))


def make_image(bricks, rcv_early, rcv_late):
    def kernel(bricks, rcv_early, rcv_late, out, held, sem):
        copies = []
        for q in range(4):
            rows = slice(q * 128, q * 128 + 128)
            early = bricks[:, 0, :, rows].reshape(256, 128).astype(F32).T
            late = bricks[:, 1, :, rows].reshape(256, 128).astype(F32).T
            for t in range(2):
                lanes = slice(t * 128, t * 128 + 128)
                held[rows, lanes] = early[:, lanes] * rcv_early[t, rows, :] + late[:, lanes] * rcv_late[t, rows, :]
            copies.append(pltpu.make_async_copy(held.at[rows, :], out.at[rows, :], sem))
            copies[-1].start()
        wait(copies)

    return pl.pallas_call(
        kernel,
        out_shape=jax.ShapeDtypeStruct((512, 256), F32),
        in_specs=[VM] * 3,
        out_specs=HB,
        scratch_shapes=[pltpu.VMEM((512, 256), F32), pltpu.SemaphoreType.DMA],
        compiler_params=params(),
        name="make_image",
    )(bricks, rcv_early, rcv_late)


def exchange(buffers):
    gx_second, gy_second, gx_first, gy_first = buffers
    inner = lambda n: [(i, i ^ 1) for i in range(n)]
    outer = lambda n: [(i, (((i + 1) ^ 1) - 1) % n) for i in range(n)]
    return (
        lax.ppermute(gx_second, "gx", outer(8)),
        lax.ppermute(gy_second, "gy", outer(16)),
        lax.ppermute(gx_first, "gx", inner(8)),
        lax.ppermute(gy_first, "gy", inner(16)),
    )


def on_device(
    source_now,
    source_next,
    receiver_now,
    receiver_next,
    velocity,
    saved_planes,
    plane_index,
    wavelet,
    source_cell,
    traces,
    receiver_x,
    receiver_y,
):
    vel, src, rcv, turned = turn_velocity(velocity, source_now, receiver_now)
    pieces = lax.all_to_all(turned.reshape(16, 16, 512), "gy", split_axis=0, concat_axis=0, tiled=True)
    src, rcv, vel = (x.reshape(x.shape[0], -1, 128) for x in (src, rcv, vel))
    halos = exchange(first_halos(src, rcv))
    *local, planes, inject = local_first(
        source_now,
        source_next.reshape(256, 512),
        receiver_now,
        receiver_next.reshape(512, 256),
        vel,
        wavelet,
        source_cell,
        saved_planes,
        plane_index,
        traces,
        receiver_x,
        receiver_y,
    )
    vel_src = source_velocity(pieces)
    src_next, rcv_next = source_now.reshape(256, 512), receiver_now.reshape(512, 256)
    more = []
    for step in range(STEPS - 1):
        src, rcv, *to_send = halo_step(step, local, vel_src, vel, halos, planes)
        halos = exchange(to_send)
        local = local_step(step + 1, src, src_next, rcv, rcv_next, vel_src, vel, inject, wavelet, source_cell)
        more += local[2:]
        local = local[:2]
        src_next, rcv_next = src, rcv
    kept, early = more
    src, bricks = last_source(local[0], early, vel_src, halos, planes)
    bricks = lax.all_to_all(bricks, "gy", split_axis=0, concat_axis=0, tiled=True)
    rcv, rcv_early, source_field, receiver_field = last_receiver(local[1], vel, halos, src, kept)
    image = make_image(bricks, rcv_early, rcv)
    return (image.reshape(16, 32, 256), receiver_field.reshape(16, 32, 256), source_field.reshape(16, 16, 512))


def solution(mesh):
    field, turned = P("gx", "gy", None), P("gy", "gx", None)
    return jax.shard_map(
        on_device,
        mesh=mesh,
        in_specs=(turned, turned, field, field, field, P(), P(), P(), P(), P(), P(), P()),
        out_specs=(field, field, turned),
        check_vma=False,
    )
```

```python
import jax
import jax.numpy as jnp
from jax import lax
from jax.experimental import pallas as pl
from jax.experimental.pallas import tpu as pltpu
from jax.sharding import PartitionSpec as P

STEPS = 4
C0, C1, C2, C3, C4 = (-205.0 / 72.0, 8.0 / 5.0, -1.0 / 5.0, 8.0 / 315.0, -1.0 / 560.0)
COEFFS = (C0, C1, C2, C3, C4)
RECEIVER_PLANE = 2
PLANES = 5
F32, BF16, I16 = jnp.float32, jnp.bfloat16, jnp.int16
VELOCITY_MIDDLE, VELOCITY_STEP = 0.115, 0.0651 / 32767
VMEM_LIMIT = 24 * 1024 * 1024

RCV = dict(lead=16, rows=32, lanes=256)
SRC = dict(lead=16, rows=16, lanes=512)


def flat(ref):
    return ref.reshape(ref.shape[0], ref.shape[1] * ref.shape[2], 128)


def split(value):
    high = value.astype(BF16)
    return high, (value - high.astype(F32)).astype(BF16)


def planes_of(layers):
    return [*split(layers[0]), *[layer.astype(BF16) for layer in layers[1:]]]


def layers_of(planes):
    planes = [plane.astype(F32) for plane in planes]
    return [planes[0] + planes[1], *planes[2:]]


def sides():
    return lax.axis_index("gx") % 2 == 0, lax.axis_index("gy") % 2 == 0


def chosen(up, one, other):
    up = jnp.broadcast_to(up, one[0].shape)
    return [jnp.where(up, x, y) for x, y in zip(one, other)]


def pack_source(src, gx_second, gy_second, gx_first, gy_first):
    up_x, up_y = sides()
    for t in range(4):
        lanes = slice(t * 128, t * 128 + 128)
        low = [src[t, pl.ds(h, 16, stride=16), :] for h in range(4)]
        high = [src[t, pl.ds(15 - h, 16, stride=16), :] for h in range(4)]
        for out, layers in ((gx_second, chosen(up_x, low, high)), (gx_first, chosen(up_x, high, low))):
            for p, plane in enumerate(planes_of(layers)):
                out[p, :, lanes] = plane
        low = [src[t, h * 16 : h * 16 + 16, :] for h in range(4)]
        high = [src[t, (15 - h) * 16 : (15 - h) * 16 + 16, :] for h in range(4)]
        for out, layers in ((gy_second, chosen(up_y, low, high)), (gy_first, chosen(up_y, high, low))):
            for p, plane in enumerate(planes_of(layers)):
                out[p, :, lanes] = plane


def pack_receiver(rcv, at, gx_second, gy_second, gx_first, gy_first):
    up_x, up_y = sides()
    for t in range(4):
        lanes = slice(t * 128, t * 128 + 128)
        half, col = divmod(t, 2)
        low = [rcv[col, h * 32 + half * 16 : h * 32 + half * 16 + 16, :] for h in range(4)]
        high = [rcv[col, (15 - h) * 32 + half * 16 : (15 - h) * 32 + half * 16 + 16, :] for h in range(4)]
        for out, layers in ((gx_second, chosen(up_x, low, high)), (gx_first, chosen(up_x, high, low))):
            for p, plane in enumerate(planes_of(layers)):
                out[at + p, :, lanes] = plane
    for col in range(2):
        low = [rcv[col, pl.ds(h, 16, stride=32), :] for h in range(4)]
        high = [rcv[col, pl.ds(31 - h, 16, stride=32), :] for h in range(4)]
        for out, layers in ((gy_second, chosen(up_y, low, high)), (gy_first, chosen(up_y, high, low))):
            for p, plane in enumerate(planes_of(layers)):
                lane = (p % 2) * 256 + col * 128
                out[at + p // 2, :, lane : lane + 128] = plane


def add_layers(out, vel, t, low_rows, high_rows, first, second, up, ends):
    live = jnp.broadcast_to(~ends, first[0].shape)
    second = [jnp.where(live, layer, 0.0) for layer in second]
    for rows_of, layers in ((low_rows, chosen(up, second, first)), (high_rows, chosen(up, first, second))):
        for d in range(4):
            term = COEFFS[d + 1] * layers[0]
            for h in range(1, 4 - d):
                term = term + COEFFS[d + h + 1] * layers[h]
            rows = rows_of(d)
            out[t, rows, :] = out[t, rows, :] + vel[t, rows, :] * term


def add_source(out, vel, gx_second, gy_second, gx_first, gy_first, columns=range(4)):
    ix, iy = lax.axis_index("gx"), lax.axis_index("gy")
    up_x, up_y = sides()
    for t in columns:
        lanes = slice(t * 128, t * 128 + 128)
        planes = lambda buffer: layers_of([buffer[p, :, lanes] for p in range(PLANES)])
        add_layers(
            out,
            vel,
            t,
            lambda d: pl.ds(d * 16, 16),
            lambda d: pl.ds((15 - d) * 16, 16),
            planes(gy_first),
            planes(gy_second),
            up_y,
            (iy == 0) | (iy == 15),
        )
        add_layers(
            out,
            vel,
            t,
            lambda d: pl.ds(d, 16, stride=16),
            lambda d: pl.ds(15 - d, 16, stride=16),
            planes(gx_first),
            planes(gx_second),
            up_x,
            (ix == 0) | (ix == 7),
        )


def add_receiver(out, vel, at, gx_second, gy_second, gx_first, gy_first):
    ix, iy = lax.axis_index("gx"), lax.axis_index("gy")
    up_x, up_y = sides()
    for t in range(4):
        lanes = slice(t * 128, t * 128 + 128)
        half, col = divmod(t, 2)
        planes = lambda buffer: layers_of([buffer[at + p, :, lanes] for p in range(PLANES)])
        add_layers(
            out,
            vel,
            col,
            lambda d: pl.ds(d * 32 + half * 16, 16),
            lambda d: pl.ds((15 - d) * 32 + half * 16, 16),
            planes(gx_first),
            planes(gx_second),
            up_x,
            (ix == 0) | (ix == 7),
        )
    for col in range(2):
        lane = [(p % 2) * 256 + col * 128 for p in range(PLANES)]
        planes = lambda buffer: layers_of(
            [buffer[at + p // 2, :, lane[p] : lane[p] + 128] for p in range(PLANES)]
        )
        add_layers(
            out,
            vel,
            col,
            lambda d: pl.ds(d, 16, stride=32),
            lambda d: pl.ds(31 - d, 16, stride=32),
            planes(gy_first),
            planes(gy_second),
            up_y,
            (iy == 0) | (iy == 15),
        )


def band(rows, cols, offset=0, block=None):
    i = lax.broadcasted_iota(jnp.int32, (rows, cols), 0)
    j = lax.broadcasted_iota(jnp.int32, (rows, cols), 1)
    distance = jnp.abs(i - j + offset)
    matrix = jnp.zeros((rows, cols), F32)
    for k, entry in ((1, 8064.0), (2, -1008.0), (3, 128.0), (4, -9.0)):
        matrix = jnp.where(distance == k, entry, matrix)
    if block is not None:
        matrix = jnp.where(i // block == j // block, matrix, 0.0)
    return matrix.astype(BF16)


def parts_of(value):
    parts = []
    for _ in range(3):
        parts.append(value.astype(BF16))
        value = value - parts[-1].astype(F32)
    return parts


def local_laplacian(f, now, store):
    lead, rows, tiles = f["lead"], f["rows"], f["lanes"] // 128
    dot = lambda x, y: jnp.dot(x, y, preferred_element_type=F32)
    along_lanes, along_rows = band(256, 256), band(256, 256, block=rows)
    if tiles > 2:
        from_above, from_below = band(128, 128, offset=128), band(128, 128, offset=-128)
    for c in range(lead * rows // 256):
        here = [now[t, c * 256 : c * 256 + 256, :] for t in range(tiles)]
        parts = [parts_of(x) for x in here]
        sums = []
        for t in range(0, tiles, 2):
            both = None
            for one, other in zip(parts[t], parts[t + 1]):
                pair = jnp.concatenate([one, other], axis=1)
                term = dot(pair, along_lanes) + dot(along_rows, pair)
                both = term if both is None else both + term
            sums += [both[:, :128], both[:, 128:]]
        for t in range(2, tiles, 2):
            for below, above in zip(parts[t - 1], parts[t]):
                sums[t - 1] = sums[t - 1] + dot(above, from_above)
                sums[t] = sums[t] + dot(below, from_below)
        for t in range(tiles):
            for i in range(256 // rows):
                a = c * (256 // rows) + i
                part = slice(i * rows, i * rows + rows)
                total = (3.0 * C0) * here[t][part] + sums[t][part] * (1.0 / 5040.0)
                for k in range(1, 5):
                    others = [
                        now[t, other * rows : other * rows + rows, :] for other in (a - k, a + k) if 0 <= other < lead
                    ]
                    total = total + COEFFS[k] * sum(others[1:], others[0])
                store(t, a, slice(a * rows, a * rows + rows), here[t][part], total)


def pack_brick(src, out, columns=range(4)):
    group = lax.broadcasted_iota(jnp.int32, (16, 128), 1) // 32
    for t in columns:
        for xg in range(4):
            rows = [src[t, pl.ds(xg * 4 + xl, 16, stride=16), :] for xl in range(4)]
            rows = [rows[0]] + [pltpu.roll(rows[xl], xl * 32, 1) for xl in range(1, 4)]
            for g in range(4):
                piece = rows[(0 - g) % 4]
                for p in range(1, 4):
                    piece = jnp.where(group == p, rows[(p - g) % 4], piece)
                out[t * 4 + g, :, xg * 128 : xg * 128 + 128] = piece.astype(BF16)


def unpack_velocity(pieces, out):
    group = lax.broadcasted_iota(jnp.int32, (16, 128), 1) // 32
    for t in range(4):
        for xg in range(4):
            codes = [pieces[t * 4 + g, :, xg * 128 : xg * 128 + 128] for g in range(4)]
            parts = [code.astype(jnp.int32).astype(F32) * VELOCITY_STEP + VELOCITY_MIDDLE for code in codes]
            for xl in range(4):
                row = None
                for g in range(4):
                    turned = parts[g] if xl == g else pltpu.roll(parts[g], ((g - xl) % 4) * 32, 1)
                    row = turned if row is None else jnp.where(group == g, turned, row)
                out[t, pl.ds(xg * 4 + xl, 16, stride=16), :] = row


SRC_PLANES, RCV_PLANES = (PLANES, PLANES), (PLANES, 3)


def halo_buffers(*fields):
    shapes = [(sum(f[axis] for f in fields), 16, 512) for axis in (0, 1, 0, 1)]
    return [jax.ShapeDtypeStruct(shape, BF16) for shape in shapes]


SRC_COLS = jax.ShapeDtypeStruct((4, 256, 128), F32)
RCV_COLS = jax.ShapeDtypeStruct((2, 512, 128), F32)
BRICKS = (16, 2, 16, 512)
VM = pl.BlockSpec(memory_space=pltpu.VMEM)
SM = pl.BlockSpec(memory_space=pltpu.SMEM)
HB = pl.BlockSpec(memory_space=pltpu.HBM)


def in_hbm(*arrays):
    return [pltpu.with_memory_space_constraint(x, pltpu.HBM) for x in arrays]


def params():
    return pltpu.CompilerParams(vmem_limit_bytes=VMEM_LIMIT)


def hint(microseconds):
    return pl.CostEstimate(flops=0, bytes_accessed=int(microseconds * 3.6e6), transcendentals=0)


def column_copies(block, cols, sem):
    return [
        pltpu.make_async_copy(
            block.at[pl.ds(a, 8), :, pl.ds(t * 128, 128)], cols.at[t, pl.ds(a, 8), :, :], sem
        )
        for a in (0, 8)
        for t in range(cols.shape[0])
    ]


def start(copies):
    for copy in copies:
        copy.start()


def wait(copies):
    for copy in copies:
        copy.wait()


def turn_velocity(vel, src, rcv):
    def kernel(vel, src, rcv, cols, src_cols, rcv_cols, turned_out, turned, sems):
        pieces = [
            pltpu.make_async_copy(
                vel.at[pl.ds(q * 4, 4), :, pl.ds(t * 128, 128)], cols.at[t, pl.ds(q * 4, 4), :, :], sems.at[q]
            )
            for q in range(4)
            for t in range(2)
        ]
        start(pieces)
        fields = column_copies(src, src_cols, sems.at[5]) + column_copies(rcv, rcv_cols, sems.at[5])
        start(fields)
        flat_cols = flat(cols)
        outs = []
        for q in range(4):
            wait(pieces[2 * q : 2 * q + 2])
            lanes = pl.ds(q * 128, 128)
            for t in range(2):
                rows = flat_cols[t, q * 128 : q * 128 + 128, :].T
                code = jnp.round((rows - VELOCITY_MIDDLE) * (1.0 / VELOCITY_STEP)).astype(jnp.int32)
                turned[t * 128 : t * 128 + 128, lanes] = code.astype(I16)
            outs.append(pltpu.make_async_copy(turned.at[:, lanes], turned_out.at[:, lanes], sems.at[4]))
            outs[-1].start()
        wait(outs)
        wait(fields)

    return pl.pallas_call(
        kernel,
        out_shape=[
            jax.ShapeDtypeStruct((2, 16, 32, 128), F32),
            jax.ShapeDtypeStruct((4, 16, 16, 128), F32),
            jax.ShapeDtypeStruct((2, 16, 32, 128), F32),
            pltpu.HBM((256, 512), I16),
        ],
        in_specs=[HB] * 3,
        out_specs=[VM] * 3 + [HB],
        scratch_shapes=[pltpu.VMEM((256, 512), I16), pltpu.SemaphoreType.DMA((6,))],
        compiler_params=params(),
        name="turn_velocity",
    )(*in_hbm(vel, src, rcv))


def first_halos(src, rcv):
    def kernel(src, rcv, *packed):
        pack_source(src, *packed)
        pack_receiver(rcv, PLANES, *packed)

    return pl.pallas_call(
        kernel,
        out_shape=halo_buffers(SRC_PLANES, RCV_PLANES),
        in_specs=[VM] * 2,
        out_specs=[VM] * 4,
        compiler_params=params(),
        name="first_halos",
    )(src, rcv)


def source_velocity(pieces):
    return pl.pallas_call(
        unpack_velocity,
        out_shape=SRC_COLS,
        in_specs=[VM],
        out_specs=VM,
        compiler_params=params(),
        name="source_velocity",
    )(pieces)


def injections(traces, rx, ry):
    xs = lax.axis_index("gx") * 16 + lax.broadcasted_iota(jnp.int32, (16, 512), 0)
    ys = lax.axis_index("gy") * 32 + lax.broadcasted_iota(jnp.int32, (32, 512), 0)
    total = jnp.zeros((32, 128), F32)
    for c in range(8):
        cols = slice(c * 512, c * 512 + 512)
        at_x = rx[:, cols] == xs
        at_y = jnp.where(ry[:, cols] == ys, 1.0, 0.0).astype(BF16)
        weighted = [jnp.where(at_x, traces[s : s + 1, cols], 0.0) for s in range(STEPS)]
        for part in parts_of(jnp.concatenate(weighted, axis=0)):
            part = jnp.concatenate([part, jnp.zeros((64, 512), BF16)], axis=0)
            total = total + lax.dot_general(at_y, part, (((1,), (1,)), ((), ())), preferred_element_type=F32)
    return total


def subtract(cols, block):
    for t in range(cols.shape[0]):
        cols[t] = cols[t] - block[:, t * 128 : t * 128 + 128]


def local_source(now, nxt, vel, out, lap_out=None):
    def store(t, a, rows, here, lap):
        value = 2.0 * here
        if nxt is not None:
            value = value - nxt[t, rows, :]
        if vel is None:
            lap_out[t, rows, :] = lap
        else:
            value = value + vel[t, rows, :] * lap
        out[t, rows, :] = value

    local_laplacian(SRC, now, store)


def local_receiver(step, now, nxt, vel, inject, out):
    lane = lax.broadcasted_iota(jnp.int32, (32, 128), 1)

    def store(t, a, rows, here, lap):
        value = 2.0 * here + vel[t, rows, :] * lap
        if nxt is not None:
            value = value - nxt[t, rows, :]
        if t == 0:
            turn = (RECEIVER_PLANE - step * 16 - a) % 128
            value = value + jnp.where(lane == RECEIVER_PLANE, pltpu.roll(inject[...], turn, 1), 0.0)
        out[t, rows, :] = value

    local_laplacian(RCV, now, store)


def add_wavelet(step, cell, wavelet, out):
    z = cell[2] - lax.axis_index("gy") * 16
    x = cell[0] - lax.axis_index("gx") * 16

    @pl.when((z >= 0) & (z < 16) & (x >= 0) & (x < 16))
    def _():
        at = pl.ds(z * 16 + x, 1)
        lanes = lax.broadcasted_iota(jnp.int32, (1, 128), 1)
        for t in range(4):
            out[t, at, :] = out[t, at, :] + jnp.where(lanes + t * 128 == cell[1], wavelet[step], 0.0)


def local_first(src, src_next, rcv, rcv_next, vel, wavelet, cell, saved, plane_index, traces, receiver_x, receiver_y):
    def kernel(vel, *refs):
        hbm, (base, lap, rcv_out, planes, inject), refs = refs[:11], refs[11:16], refs[16:]
        src, src_next, rcv, rcv_next, wavelet_hbm, cell_hbm, saved, index_hbm, traces_hbm, rx_hbm, ry_hbm = hbm
        src_cols, next_src, rcv_cols, next_rcv, traces, rx, ry, wavelet, cell, index, sems = refs
        ix, iy = lax.axis_index("gx"), lax.axis_index("gy")
        get_index = pltpu.make_async_copy(index_hbm, index, sems.at[0])
        get_index.start()
        receivers = [
            pltpu.make_async_copy(traces_hbm, traces, sems.at[7]),
            pltpu.make_async_copy(rx_hbm, rx, sems.at[7]),
            pltpu.make_async_copy(ry_hbm, ry, sems.at[7]),
        ]
        get_src, get_rcv = column_copies(src, src_cols, sems.at[5]), column_copies(rcv, rcv_cols, sems.at[6])
        later = [
            pltpu.make_async_copy(wavelet_hbm, wavelet, sems.at[1]),
            pltpu.make_async_copy(cell_hbm, cell, sems.at[2]),
            pltpu.make_async_copy(src_next, next_src, sems.at[3]),
            pltpu.make_async_copy(rcv_next, next_rcv, sems.at[4]),
        ]
        start(receivers + get_src + get_rcv + later)
        wait(receivers)
        inject[...] = injections(traces, rx, ry)
        get_index.wait()
        edge = (ix == 0) | (ix == 7)
        side = jnp.where(ix == 0, 0, 1)
        restores = [
            pltpu.make_async_copy(
                saved.at[index[step], side, pl.ds(pl.multiple_of(iy * 16, 16), 16), pl.ds(t * 128, 128)],
                planes.at[step, t],
                sems.at[8],
            )
            for step in range(STEPS)
            for t in range(4)
        ]

        @pl.when(edge)
        def _():
            start(restores)

        wait(get_src)
        local_source(flat(src_cols), None, None, base, lap)
        wait(get_rcv)
        local_receiver(0, flat(rcv_cols), None, vel, inject, rcv_out)
        wait(later)
        subtract(base, next_src)
        subtract(rcv_out, next_rcv)
        add_wavelet(0, cell, wavelet, base)

        @pl.when(edge)
        def _():
            wait(restores)

    return pl.pallas_call(
        kernel,
        out_shape=[
            SRC_COLS,
            SRC_COLS,
            RCV_COLS,
            jax.ShapeDtypeStruct((STEPS, 4, 16, 128), F32),
            jax.ShapeDtypeStruct((32, 128), F32),
        ],
        in_specs=[VM] + [HB] * 11,
        out_specs=[VM] * 5,
        scratch_shapes=[
            pltpu.VMEM((4, 16, 16, 128), F32),
            pltpu.VMEM((256, 512), F32),
            pltpu.VMEM((2, 16, 32, 128), F32),
            pltpu.VMEM((512, 256), F32),
            pltpu.VMEM((4, 4096), F32),
            pltpu.VMEM((1, 4096), jnp.int32),
            pltpu.VMEM((1, 4096), jnp.int32),
            pltpu.SMEM((4,), F32),
            pltpu.SMEM((3,), jnp.int32),
            pltpu.SMEM((4,), jnp.int32),
            pltpu.SemaphoreType.DMA((9,)),
        ],
        compiler_params=params(),
        cost_estimate=hint(4),
        name="local_first",
    )(
        vel,
        *in_hbm(
            src,
            src_next,
            rcv,
            rcv_next,
            wavelet,
            cell,
            saved,
            plane_index,
            traces,
            receiver_x.reshape(1, -1),
            receiver_y.reshape(1, -1),
        ),
    )


def local_step(step, src, src_next, rcv, rcv_next, vel_src, vel, inject, wavelet, cell):
    from_hbm, keep, last = step == 1, step == 2, step == STEPS - 1

    def kernel(src, src_next, rcv, rcv_next, vel_src, vel, inject, wavelet_hbm, cell_hbm, src_out, rcv_out, *refs):
        bricks, brick = (refs[0], refs[1]) if last else (None, None)
        wavelet, cell, next_src, next_rcv, sems = refs[-5:]
        copies = [
            pltpu.make_async_copy(wavelet_hbm, wavelet, sems.at[0]),
            pltpu.make_async_copy(cell_hbm, cell, sems.at[1]),
        ]
        if from_hbm:
            copies.append(pltpu.make_async_copy(src_next, next_src, sems.at[2]))
            copies.append(pltpu.make_async_copy(rcv_next, next_rcv, sems.at[3]))
        if keep:
            copies.append(pltpu.make_async_copy(rcv, refs[0], sems.at[2]))
        start(copies)
        if last:
            pack_brick(src_next, brick)
            copies.append(pltpu.make_async_copy(brick, bricks.at[:, 0], sems.at[2]))
            copies[-1].start()
        local_source(src, None if from_hbm else src_next, vel_src, src_out)
        local_receiver(step, rcv, None if from_hbm else rcv_next, vel, inject, rcv_out)
        wait(copies)
        if from_hbm:
            subtract(src_out, next_src)
            subtract(rcv_out, next_rcv)
        add_wavelet(step, cell, wavelet, src_out)

    if from_hbm:
        src_next, rcv_next = in_hbm(src_next, rcv_next)
    next_spec = HB if from_hbm else VM
    out_shape = [SRC_COLS, RCV_COLS]
    if keep:
        out_shape.append(pltpu.HBM(RCV_COLS.shape, F32))
    if last:
        out_shape.append(pltpu.HBM(BRICKS, BF16))
    return pl.pallas_call(
        kernel,
        out_shape=out_shape,
        in_specs=[VM, next_spec, VM, next_spec] + [VM] * 3 + [HB] * 2,
        out_specs=[VM, VM] + [HB] * (len(out_shape) - 2),
        scratch_shapes=([pltpu.VMEM((16, 16, 512), BF16)] if last else [])
        + [
            pltpu.SMEM((4,), F32),
            pltpu.SMEM((3,), jnp.int32),
            pltpu.VMEM((256, 512) if from_hbm else (8, 128), F32),
            pltpu.VMEM((512, 256) if from_hbm else (8, 128), F32),
            pltpu.SemaphoreType.DMA((4,)),
        ],
        compiler_params=params(),
        cost_estimate=hint(3),
        name=f"local_step{step}",
    )(src, src_next, rcv, rcv_next, vel_src, vel, inject, *in_hbm(wavelet, cell))


def restore_planes(step, src, planes, columns=range(4)):
    ix = lax.axis_index("gx")

    @pl.when(ix == 0)
    def _():
        for t in columns:
            src[t, pl.ds(0, 16, stride=16), :] = planes[step, t]

    @pl.when(ix == 7)
    def _():
        for t in columns:
            src[t, pl.ds(15, 16, stride=16), :] = planes[step, t]


def halo_step(step, local, vel_src, vel, halos, planes):
    first = step == 0

    def kernel(*refs):
        refs = list(refs)
        local_src = refs.pop(0)
        lap = refs.pop(0) if first else None
        local_rcv, vel_src, vel = refs[:3]
        halos, planes, src, rcv, packed = refs[3:7], refs[7], refs[8], refs[9], refs[10:]
        src[...] = local_src[...] + vel_src[...] * lap[...] if first else local_src[...]
        rcv[...] = local_rcv[...]
        add_source(src, vel_src, *halos)
        restore_planes(step, src, planes)
        pack_source(src, *packed)
        add_receiver(rcv, vel, PLANES, *halos)
        pack_receiver(rcv, PLANES, *packed)

    args = [*local, vel_src, vel, *halos, planes]
    out_shape = [SRC_COLS, RCV_COLS, *halo_buffers(SRC_PLANES, RCV_PLANES)]
    return pl.pallas_call(
        kernel,
        out_shape=out_shape,
        in_specs=[VM] * len(args),
        out_specs=[VM] * len(out_shape),
        compiler_params=params(),
        name=f"halo_step{step}",
    )(*args)


def last_source(local, bricks, vel_src, halos, planes):
    def kernel(local, _, vel_src, *refs):
        halos, planes, src, bricks, late, sem = refs[:4], *refs[4:]
        copies = []
        src[...] = local[...]
        add_source(src, vel_src, *halos)
        restore_planes(STEPS - 1, src, planes)
        for t in range(4):
            pack_brick(src, late, (t,))
            part = pl.ds(t * 4, 4)
            copies.append(pltpu.make_async_copy(late.at[part], bricks.at[part, 1], sem))
            copies[-1].start()
        wait(copies)

    return pl.pallas_call(
        kernel,
        out_shape=[SRC_COLS, pltpu.HBM(BRICKS, BF16)],
        in_specs=[VM, HB] + [VM] * 6,
        out_specs=[VM, HB],
        input_output_aliases={1: 1},
        scratch_shapes=[pltpu.VMEM((16, 16, 512), BF16), pltpu.SemaphoreType.DMA],
        compiler_params=params(),
        name="last_source",
    )(local, *in_hbm(bricks), vel_src, *halos, planes)


def last_receiver(local, vel, halos, src, kept):
    def kernel(local, vel, *refs):
        halos, src, kept, rcv, early, src_out, rcv_out, sem = refs[:4], *refs[4:]
        copies = [pltpu.make_async_copy(src.at[t], src_out.at[:, pl.ds(t * 128, 128)], sem) for t in range(4)]
        copies += [pltpu.make_async_copy(kept.at[t], early.at[t], sem) for t in range(2)]
        start(copies)
        rcv[...] = local[...]
        add_receiver(rcv, vel, PLANES, *halos)
        more = [pltpu.make_async_copy(rcv.at[t], rcv_out.at[:, pl.ds(t * 128, 128)], sem) for t in range(2)]
        start(more)
        wait(copies + more)

    return pl.pallas_call(
        kernel,
        out_shape=[RCV_COLS] * 2 + [jax.ShapeDtypeStruct(shape, F32) for shape in ((256, 512), (512, 256))],
        in_specs=[VM] * 7 + [HB],
        out_specs=[VM, VM, HB, HB],
        scratch_shapes=[pltpu.SemaphoreType.DMA],
        compiler_params=params(),
        cost_estimate=hint(2),
        name="last_receiver",
    )(local, vel, *halos, src, *in_hbm(kept))


def make_image(bricks, rcv_early, rcv_late):
    def kernel(bricks, rcv_early, rcv_late, out, held, sem):
        copies = []
        turn = lax.axis_index("gy") % 4
        for q in range(4):
            rows = slice(q * 128, q * 128 + 128)
            early = bricks[:, 0, :, rows].reshape(256, 128).astype(F32).T
            late = bricks[:, 1, :, rows].reshape(256, 128).astype(F32).T
            for place in range(4):
                part = slice(place * 32, place * 32 + 32)
                at = pl.ds(pl.multiple_of(q * 128 + lax.rem(place + 4 - turn, 4) * 32, 32), 32)
                for t in range(2):
                    lanes = slice(t * 128, t * 128 + 128)
                    held[at, lanes] = early[part, lanes] * rcv_early[t, at, :] + late[part, lanes] * rcv_late[t, at, :]
            copies.append(pltpu.make_async_copy(held.at[rows, :], out.at[rows, :], sem))
            copies[-1].start()
        wait(copies)

    return pl.pallas_call(
        kernel,
        out_shape=jax.ShapeDtypeStruct((512, 256), F32),
        in_specs=[VM] * 3,
        out_specs=HB,
        scratch_shapes=[pltpu.VMEM((512, 256), F32), pltpu.SemaphoreType.DMA],
        compiler_params=params(),
        name="make_image",
    )(bricks, rcv_early, rcv_late)


def exchange(buffers):
    gx_second, gy_second, gx_first, gy_first = buffers
    inner = lambda n: [(i, i ^ 1) for i in range(n)]
    outer = lambda n: [(i, (((i + 1) ^ 1) - 1) % n) for i in range(n)]
    return (
        lax.ppermute(gx_second, "gx", outer(8)),
        lax.ppermute(gy_second, "gy", outer(16)),
        lax.ppermute(gx_first, "gx", inner(8)),
        lax.ppermute(gy_first, "gy", inner(16)),
    )


def on_device(
    source_now,
    source_next,
    receiver_now,
    receiver_next,
    velocity,
    saved_planes,
    plane_index,
    wavelet,
    source_cell,
    traces,
    receiver_x,
    receiver_y,
):
    vel, src, rcv, turned = turn_velocity(velocity, source_now, receiver_now)
    pieces = lax.all_to_all(turned.reshape(16, 16, 512), "gy", split_axis=0, concat_axis=0, tiled=True)
    src, rcv, vel = (x.reshape(x.shape[0], -1, 128) for x in (src, rcv, vel))
    halos = exchange(first_halos(src, rcv))
    *local, planes, inject = local_first(
        source_now,
        source_next.reshape(256, 512),
        receiver_now,
        receiver_next.reshape(512, 256),
        vel,
        wavelet,
        source_cell,
        saved_planes,
        plane_index,
        traces,
        receiver_x,
        receiver_y,
    )
    vel_src = source_velocity(pieces)
    src_next, rcv_next = source_now.reshape(256, 512), receiver_now.reshape(512, 256)
    more = []
    for step in range(STEPS - 1):
        src, rcv, *to_send = halo_step(step, local, vel_src, vel, halos, planes)
        halos = exchange(to_send)
        local = local_step(step + 1, src, src_next, rcv, rcv_next, vel_src, vel, inject, wavelet, source_cell)
        more += local[2:]
        local = local[:2]
        src_next, rcv_next = src, rcv
    kept, early = more
    src, bricks = last_source(local[0], early, vel_src, halos, planes)
    bricks = lax.all_to_all(bricks, "gy", split_axis=0, concat_axis=0, tiled=True)
    rcv, rcv_early, source_field, receiver_field = last_receiver(local[1], vel, halos, src, kept)
    image = make_image(bricks, rcv_early, rcv)
    return (image.reshape(16, 32, 256), receiver_field.reshape(16, 32, 256), source_field.reshape(16, 16, 512))


def solution(mesh):
    field, turned = P("gx", "gy", None), P("gy", "gx", None)
    return jax.shard_map(
        on_device,
        mesh=mesh,
        in_specs=(turned, turned, field, field, field, P(), P(), P(), P(), P(), P(), P()),
        out_specs=(field, field, turned),
        check_vma=False,
    )
```

```python
import jax
import jax.numpy as jnp
from jax import lax
from jax.experimental import pallas as pl
from jax.experimental.pallas import tpu as pltpu
from jax.sharding import PartitionSpec as P

STEPS = 4
C0, C1, C2, C3, C4 = (-205.0 / 72.0, 8.0 / 5.0, -1.0 / 5.0, 8.0 / 315.0, -1.0 / 560.0)
COEFFS = (C0, C1, C2, C3, C4)
RECEIVER_PLANE = 2
PLANES = 5
F32, BF16, I16 = jnp.float32, jnp.bfloat16, jnp.int16
VELOCITY_MIDDLE, VELOCITY_STEP = 0.115, 0.0651 / 32767
VMEM_LIMIT = 24 * 1024 * 1024

RCV = dict(lead=16, rows=32, lanes=256)
SRC = dict(lead=16, rows=16, lanes=512)


def flat(ref):
    return ref.reshape(ref.shape[0], ref.shape[1] * ref.shape[2], 128)


def split(value):
    high = value.astype(BF16)
    return high, (value - high.astype(F32)).astype(BF16)


def planes_of(layers):
    return [*split(layers[0]), *[layer.astype(BF16) for layer in layers[1:]]]


def layers_of(planes):
    planes = [plane.astype(F32) for plane in planes]
    return [planes[0] + planes[1], *planes[2:]]


def sides():
    return lax.axis_index("gx") % 2 == 0, lax.axis_index("gy") % 2 == 0


def chosen(up, one, other):
    up = jnp.broadcast_to(up, one[0].shape)
    return [jnp.where(up, x, y) for x, y in zip(one, other)]


def pack_source(src, gx_second, gy_second, gx_first, gy_first):
    up_x, up_y = sides()
    for t in range(4):
        lanes = slice(t * 128, t * 128 + 128)
        low = [src[t, pl.ds(h, 16, stride=16), :] for h in range(4)]
        high = [src[t, pl.ds(15 - h, 16, stride=16), :] for h in range(4)]
        for out, layers in ((gx_second, chosen(up_x, low, high)), (gx_first, chosen(up_x, high, low))):
            for p, plane in enumerate(planes_of(layers)):
                out[p, :, lanes] = plane
        low = [src[t, h * 16 : h * 16 + 16, :] for h in range(4)]
        high = [src[t, (15 - h) * 16 : (15 - h) * 16 + 16, :] for h in range(4)]
        for out, layers in ((gy_second, chosen(up_y, low, high)), (gy_first, chosen(up_y, high, low))):
            for p, plane in enumerate(planes_of(layers)):
                out[p, :, lanes] = plane


def pack_receiver(rcv, at, gx_second, gy_second, gx_first, gy_first):
    up_x, up_y = sides()
    for t in range(4):
        lanes = slice(t * 128, t * 128 + 128)
        half, col = divmod(t, 2)
        low = [rcv[col, h * 32 + half * 16 : h * 32 + half * 16 + 16, :] for h in range(4)]
        high = [rcv[col, (15 - h) * 32 + half * 16 : (15 - h) * 32 + half * 16 + 16, :] for h in range(4)]
        for out, layers in ((gx_second, chosen(up_x, low, high)), (gx_first, chosen(up_x, high, low))):
            for p, plane in enumerate(planes_of(layers)):
                out[at + p, :, lanes] = plane
    for col in range(2):
        low = [rcv[col, pl.ds(h, 16, stride=32), :] for h in range(4)]
        high = [rcv[col, pl.ds(31 - h, 16, stride=32), :] for h in range(4)]
        for out, layers in ((gy_second, chosen(up_y, low, high)), (gy_first, chosen(up_y, high, low))):
            for p, plane in enumerate(planes_of(layers)):
                lane = (p % 2) * 256 + col * 128
                out[at + p // 2, :, lane : lane + 128] = plane


def add_layers(out, vel, t, low_rows, high_rows, first, second, up, ends):
    live = jnp.broadcast_to(~ends, first[0].shape)
    second = [jnp.where(live, layer, 0.0) for layer in second]
    for rows_of, layers in ((low_rows, chosen(up, second, first)), (high_rows, chosen(up, first, second))):
        for d in range(4):
            term = COEFFS[d + 1] * layers[0]
            for h in range(1, 4 - d):
                term = term + COEFFS[d + h + 1] * layers[h]
            rows = rows_of(d)
            out[t, rows, :] = out[t, rows, :] + vel[t, rows, :] * term


def add_source(out, vel, gx_second, gy_second, gx_first, gy_first, columns=range(4)):
    ix, iy = lax.axis_index("gx"), lax.axis_index("gy")
    up_x, up_y = sides()
    for t in columns:
        lanes = slice(t * 128, t * 128 + 128)
        planes = lambda buffer: layers_of([buffer[p, :, lanes] for p in range(PLANES)])
        add_layers(
            out,
            vel,
            t,
            lambda d: pl.ds(d * 16, 16),
            lambda d: pl.ds((15 - d) * 16, 16),
            planes(gy_first),
            planes(gy_second),
            up_y,
            (iy == 0) | (iy == 15),
        )
        add_layers(
            out,
            vel,
            t,
            lambda d: pl.ds(d, 16, stride=16),
            lambda d: pl.ds(15 - d, 16, stride=16),
            planes(gx_first),
            planes(gx_second),
            up_x,
            (ix == 0) | (ix == 7),
        )


def add_receiver(out, vel, at, gx_second, gy_second, gx_first, gy_first):
    ix, iy = lax.axis_index("gx"), lax.axis_index("gy")
    up_x, up_y = sides()
    for t in range(4):
        lanes = slice(t * 128, t * 128 + 128)
        half, col = divmod(t, 2)
        planes = lambda buffer: layers_of([buffer[at + p, :, lanes] for p in range(PLANES)])
        add_layers(
            out,
            vel,
            col,
            lambda d: pl.ds(d * 32 + half * 16, 16),
            lambda d: pl.ds((15 - d) * 32 + half * 16, 16),
            planes(gx_first),
            planes(gx_second),
            up_x,
            (ix == 0) | (ix == 7),
        )
    for col in range(2):
        lane = [(p % 2) * 256 + col * 128 for p in range(PLANES)]
        planes = lambda buffer: layers_of(
            [buffer[at + p // 2, :, lane[p] : lane[p] + 128] for p in range(PLANES)]
        )
        add_layers(
            out,
            vel,
            col,
            lambda d: pl.ds(d, 16, stride=32),
            lambda d: pl.ds(31 - d, 16, stride=32),
            planes(gy_first),
            planes(gy_second),
            up_y,
            (iy == 0) | (iy == 15),
        )


def band(rows, cols, offset=0, block=None):
    i = lax.broadcasted_iota(jnp.int32, (rows, cols), 0)
    j = lax.broadcasted_iota(jnp.int32, (rows, cols), 1)
    distance = jnp.abs(i - j + offset)
    matrix = jnp.zeros((rows, cols), F32)
    for k, entry in ((1, 8064.0), (2, -1008.0), (3, 128.0), (4, -9.0)):
        matrix = jnp.where(distance == k, entry, matrix)
    if block is not None:
        matrix = jnp.where(i // block == j // block, matrix, 0.0)
    return matrix.astype(BF16)


def parts_of(value):
    parts = []
    for _ in range(3):
        parts.append(value.astype(BF16))
        value = value - parts[-1].astype(F32)
    return parts


def local_laplacian(f, now, store):
    lead, rows, tiles = f["lead"], f["rows"], f["lanes"] // 128
    dot = lambda x, y: jnp.dot(x, y, preferred_element_type=F32)
    along_lanes, along_rows = band(256, 256), band(256, 256, block=rows)
    if tiles > 2:
        from_above, from_below = band(128, 128, offset=128), band(128, 128, offset=-128)
    for c in range(lead * rows // 256):
        here = [now[t, c * 256 : c * 256 + 256, :] for t in range(tiles)]
        parts = [parts_of(x) for x in here]
        sums = []
        for t in range(0, tiles, 2):
            both = None
            for one, other in zip(parts[t], parts[t + 1]):
                pair = jnp.concatenate([one, other], axis=1)
                term = dot(pair, along_lanes) + dot(along_rows, pair)
                both = term if both is None else both + term
            sums += [both[:, :128], both[:, 128:]]
        for t in range(2, tiles, 2):
            for below, above in zip(parts[t - 1], parts[t]):
                sums[t - 1] = sums[t - 1] + dot(above, from_above)
                sums[t] = sums[t] + dot(below, from_below)
        for t in range(tiles):
            for i in range(256 // rows):
                a = c * (256 // rows) + i
                part = slice(i * rows, i * rows + rows)
                total = (3.0 * C0) * here[t][part] + sums[t][part] * (1.0 / 5040.0)
                for k in range(1, 5):
                    others = [
                        now[t, other * rows : other * rows + rows, :] for other in (a - k, a + k) if 0 <= other < lead
                    ]
                    total = total + COEFFS[k] * sum(others[1:], others[0])
                store(t, a, slice(a * rows, a * rows + rows), here[t][part], total)


def pack_brick(src, out, columns=range(4)):
    group = lax.broadcasted_iota(jnp.int32, (16, 128), 1) // 32
    for t in columns:
        for xg in range(4):
            rows = [src[t, pl.ds(xg * 4 + xl, 16, stride=16), :] for xl in range(4)]
            rows = [rows[0]] + [pltpu.roll(rows[xl], xl * 32, 1) for xl in range(1, 4)]
            for g in range(4):
                piece = rows[(0 - g) % 4]
                for p in range(1, 4):
                    piece = jnp.where(group == p, rows[(p - g) % 4], piece)
                out[t * 4 + g, :, xg * 128 : xg * 128 + 128] = piece.astype(BF16)


def unpack_velocity(pieces, out):
    group = lax.broadcasted_iota(jnp.int32, (16, 128), 1) // 32
    for t in range(4):
        for xg in range(4):
            codes = [pieces[t * 4 + g, :, xg * 128 : xg * 128 + 128] for g in range(4)]
            parts = [code.astype(jnp.int32).astype(F32) * VELOCITY_STEP + VELOCITY_MIDDLE for code in codes]
            for xl in range(4):
                row = parts[-xl % 4]
                for p in range(1, 4):
                    row = jnp.where(group == p, parts[(p - xl) % 4], row)
                row = row if xl == 0 else pltpu.roll(row, 128 - xl * 32, 1)
                out[t, pl.ds(xg * 4 + xl, 16, stride=16), :] = row


SRC_PLANES, RCV_PLANES = (PLANES, PLANES), (PLANES, 3)


def halo_buffers(*fields):
    shapes = [(sum(f[axis] for f in fields), 16, 512) for axis in (0, 1, 0, 1)]
    return [jax.ShapeDtypeStruct(shape, BF16) for shape in shapes]


SRC_COLS = jax.ShapeDtypeStruct((4, 256, 128), F32)
RCV_COLS = jax.ShapeDtypeStruct((2, 512, 128), F32)
BRICKS = (16, 2, 16, 512)
VM = pl.BlockSpec(memory_space=pltpu.VMEM)
SM = pl.BlockSpec(memory_space=pltpu.SMEM)
HB = pl.BlockSpec(memory_space=pltpu.HBM)


def in_hbm(*arrays):
    return [pltpu.with_memory_space_constraint(x, pltpu.HBM) for x in arrays]


def params():
    return pltpu.CompilerParams(vmem_limit_bytes=VMEM_LIMIT)


def hint(microseconds):
    return pl.CostEstimate(flops=0, bytes_accessed=int(microseconds * 3.6e6), transcendentals=0)


def column_copies(block, cols, sem):
    return [
        pltpu.make_async_copy(
            block.at[pl.ds(a, 8), :, pl.ds(t * 128, 128)], cols.at[t, pl.ds(a, 8), :, :], sem
        )
        for a in (0, 8)
        for t in range(cols.shape[0])
    ]


def start(copies):
    for copy in copies:
        copy.start()


def wait(copies):
    for copy in copies:
        copy.wait()


def turn_velocity(vel, src, rcv):
    def kernel(vel, src, rcv, cols, src_cols, rcv_cols, turned_out, turned, sems):
        pieces = [
            pltpu.make_async_copy(
                vel.at[pl.ds(q * 4, 4), :, pl.ds(t * 128, 128)], cols.at[t, pl.ds(q * 4, 4), :, :], sems.at[q]
            )
            for q in range(4)
            for t in range(2)
        ]
        start(pieces)
        fields = column_copies(src, src_cols, sems.at[5]) + column_copies(rcv, rcv_cols, sems.at[5])
        start(fields)
        flat_cols = flat(cols)
        outs = []
        for q in range(4):
            wait(pieces[2 * q : 2 * q + 2])
            lanes = pl.ds(q * 128, 128)
            for t in range(2):
                places = [q * 128 + lax.rem(p + 4 - lax.axis_index("gy") % 4, 4) * 32 for p in range(4)]
                rows = [flat_cols[t, pl.ds(pl.multiple_of(at, 32), 32), :] for at in places]
                rows = jnp.concatenate(rows, axis=0).T
                code = jnp.round((rows - VELOCITY_MIDDLE) * (1.0 / VELOCITY_STEP)).astype(jnp.int32)
                turned[t * 128 : t * 128 + 128, lanes] = code.astype(I16)
            outs.append(pltpu.make_async_copy(turned.at[:, lanes], turned_out.at[:, lanes], sems.at[4]))
            outs[-1].start()
        wait(outs)
        wait(fields)

    return pl.pallas_call(
        kernel,
        out_shape=[
            jax.ShapeDtypeStruct((2, 16, 32, 128), F32),
            jax.ShapeDtypeStruct((4, 16, 16, 128), F32),
            jax.ShapeDtypeStruct((2, 16, 32, 128), F32),
            pltpu.HBM((256, 512), I16),
        ],
        in_specs=[HB] * 3,
        out_specs=[VM] * 3 + [HB],
        scratch_shapes=[pltpu.VMEM((256, 512), I16), pltpu.SemaphoreType.DMA((6,))],
        compiler_params=params(),
        name="turn_velocity",
    )(*in_hbm(vel, src, rcv))


def first_halos(src, rcv):
    def kernel(src, rcv, *packed):
        pack_source(src, *packed)
        pack_receiver(rcv, PLANES, *packed)

    return pl.pallas_call(
        kernel,
        out_shape=halo_buffers(SRC_PLANES, RCV_PLANES),
        in_specs=[VM] * 2,
        out_specs=[VM] * 4,
        compiler_params=params(),
        name="first_halos",
    )(src, rcv)


def source_velocity(pieces):
    return pl.pallas_call(
        unpack_velocity,
        out_shape=SRC_COLS,
        in_specs=[VM],
        out_specs=VM,
        compiler_params=params(),
        name="source_velocity",
    )(pieces)


def injections(traces, rx, ry):
    xs = lax.axis_index("gx") * 16 + lax.broadcasted_iota(jnp.int32, (16, 512), 0)
    ys = lax.axis_index("gy") * 32 + lax.broadcasted_iota(jnp.int32, (32, 512), 0)
    total = jnp.zeros((32, 128), F32)
    for c in range(8):
        cols = slice(c * 512, c * 512 + 512)
        at_x = rx[:, cols] == xs
        at_y = jnp.where(ry[:, cols] == ys, 1.0, 0.0).astype(BF16)
        weighted = [jnp.where(at_x, traces[s : s + 1, cols], 0.0) for s in range(STEPS)]
        for part in parts_of(jnp.concatenate(weighted, axis=0)):
            part = jnp.concatenate([part, jnp.zeros((64, 512), BF16)], axis=0)
            total = total + lax.dot_general(at_y, part, (((1,), (1,)), ((), ())), preferred_element_type=F32)
    return total


def subtract(cols, block):
    for t in range(cols.shape[0]):
        cols[t] = cols[t] - block[:, t * 128 : t * 128 + 128]


def local_source(now, nxt, vel, out, lap_out=None):
    def store(t, a, rows, here, lap):
        value = 2.0 * here
        if nxt is not None:
            value = value - nxt[t, rows, :]
        if vel is None:
            lap_out[t, rows, :] = lap
        else:
            value = value + vel[t, rows, :] * lap
        out[t, rows, :] = value

    local_laplacian(SRC, now, store)


def local_receiver(step, now, nxt, vel, inject, out):
    lane = lax.broadcasted_iota(jnp.int32, (32, 128), 1)

    def store(t, a, rows, here, lap):
        value = 2.0 * here + vel[t, rows, :] * lap
        if nxt is not None:
            value = value - nxt[t, rows, :]
        if t == 0:
            turn = (RECEIVER_PLANE - step * 16 - a) % 128
            value = value + jnp.where(lane == RECEIVER_PLANE, pltpu.roll(inject[...], turn, 1), 0.0)
        out[t, rows, :] = value

    local_laplacian(RCV, now, store)


def add_wavelet(step, cell, wavelet, out):
    z = cell[2] - lax.axis_index("gy") * 16
    x = cell[0] - lax.axis_index("gx") * 16

    @pl.when((z >= 0) & (z < 16) & (x >= 0) & (x < 16))
    def _():
        at = pl.ds(z * 16 + x, 1)
        lanes = lax.broadcasted_iota(jnp.int32, (1, 128), 1)
        for t in range(4):
            out[t, at, :] = out[t, at, :] + jnp.where(lanes + t * 128 == cell[1], wavelet[step], 0.0)


def local_first(src, src_next, rcv, rcv_next, vel, wavelet, cell, saved, plane_index, traces, receiver_x, receiver_y):
    def kernel(vel, *refs):
        hbm, (base, lap, rcv_out, planes, inject), refs = refs[:11], refs[11:16], refs[16:]
        src, src_next, rcv, rcv_next, wavelet_hbm, cell_hbm, saved, index_hbm, traces_hbm, rx_hbm, ry_hbm = hbm
        src_cols, next_src, rcv_cols, next_rcv, traces, rx, ry, wavelet, cell, index, sems = refs
        ix, iy = lax.axis_index("gx"), lax.axis_index("gy")
        get_index = pltpu.make_async_copy(index_hbm, index, sems.at[0])
        get_index.start()
        receivers = [
            pltpu.make_async_copy(traces_hbm, traces, sems.at[7]),
            pltpu.make_async_copy(rx_hbm, rx, sems.at[7]),
            pltpu.make_async_copy(ry_hbm, ry, sems.at[7]),
        ]
        get_src, get_rcv = column_copies(src, src_cols, sems.at[5]), column_copies(rcv, rcv_cols, sems.at[6])
        later = [
            pltpu.make_async_copy(wavelet_hbm, wavelet, sems.at[1]),
            pltpu.make_async_copy(cell_hbm, cell, sems.at[2]),
            pltpu.make_async_copy(src_next, next_src, sems.at[3]),
            pltpu.make_async_copy(rcv_next, next_rcv, sems.at[4]),
        ]
        start(receivers + get_src + get_rcv + later)
        wait(receivers)
        inject[...] = injections(traces, rx, ry)
        get_index.wait()
        edge = (ix == 0) | (ix == 7)
        side = jnp.where(ix == 0, 0, 1)
        restores = [
            pltpu.make_async_copy(
                saved.at[index[step], side, pl.ds(pl.multiple_of(iy * 16, 16), 16), pl.ds(t * 128, 128)],
                planes.at[step, t],
                sems.at[8],
            )
            for step in range(STEPS)
            for t in range(4)
        ]

        @pl.when(edge)
        def _():
            start(restores)

        wait(get_src)
        local_source(flat(src_cols), None, None, base, lap)
        wait(get_rcv)
        local_receiver(0, flat(rcv_cols), None, vel, inject, rcv_out)
        wait(later)
        subtract(base, next_src)
        subtract(rcv_out, next_rcv)
        add_wavelet(0, cell, wavelet, base)

        @pl.when(edge)
        def _():
            wait(restores)

    return pl.pallas_call(
        kernel,
        out_shape=[
            SRC_COLS,
            SRC_COLS,
            RCV_COLS,
            jax.ShapeDtypeStruct((STEPS, 4, 16, 128), F32),
            jax.ShapeDtypeStruct((32, 128), F32),
        ],
        in_specs=[VM] + [HB] * 11,
        out_specs=[VM] * 5,
        scratch_shapes=[
            pltpu.VMEM((4, 16, 16, 128), F32),
            pltpu.VMEM((256, 512), F32),
            pltpu.VMEM((2, 16, 32, 128), F32),
            pltpu.VMEM((512, 256), F32),
            pltpu.VMEM((4, 4096), F32),
            pltpu.VMEM((1, 4096), jnp.int32),
            pltpu.VMEM((1, 4096), jnp.int32),
            pltpu.SMEM((4,), F32),
            pltpu.SMEM((3,), jnp.int32),
            pltpu.SMEM((4,), jnp.int32),
            pltpu.SemaphoreType.DMA((9,)),
        ],
        compiler_params=params(),
        cost_estimate=hint(4),
        name="local_first",
    )(
        vel,
        *in_hbm(
            src,
            src_next,
            rcv,
            rcv_next,
            wavelet,
            cell,
            saved,
            plane_index,
            traces,
            receiver_x.reshape(1, -1),
            receiver_y.reshape(1, -1),
        ),
    )


def local_step(step, src, src_next, rcv, rcv_next, vel_src, vel, inject, wavelet, cell):
    from_hbm, keep, last = step == 1, step == 2, step == STEPS - 1

    def kernel(src, src_next, rcv, rcv_next, vel_src, vel, inject, wavelet_hbm, cell_hbm, src_out, rcv_out, *refs):
        bricks, brick = (refs[0], refs[1]) if last else (None, None)
        wavelet, cell, next_src, next_rcv, sems = refs[-5:]
        copies = [
            pltpu.make_async_copy(wavelet_hbm, wavelet, sems.at[0]),
            pltpu.make_async_copy(cell_hbm, cell, sems.at[1]),
        ]
        if from_hbm:
            copies.append(pltpu.make_async_copy(src_next, next_src, sems.at[2]))
            copies.append(pltpu.make_async_copy(rcv_next, next_rcv, sems.at[3]))
        if keep:
            copies.append(pltpu.make_async_copy(rcv, refs[0], sems.at[2]))
        start(copies)
        if last:
            pack_brick(src_next, brick)
            copies.append(pltpu.make_async_copy(brick, bricks.at[:, 0], sems.at[2]))
            copies[-1].start()
        local_source(src, None if from_hbm else src_next, vel_src, src_out)
        local_receiver(step, rcv, None if from_hbm else rcv_next, vel, inject, rcv_out)
        wait(copies)
        if from_hbm:
            subtract(src_out, next_src)
            subtract(rcv_out, next_rcv)
        add_wavelet(step, cell, wavelet, src_out)

    if from_hbm:
        src_next, rcv_next = in_hbm(src_next, rcv_next)
    next_spec = HB if from_hbm else VM
    out_shape = [SRC_COLS, RCV_COLS]
    if keep:
        out_shape.append(pltpu.HBM(RCV_COLS.shape, F32))
    if last:
        out_shape.append(pltpu.HBM(BRICKS, BF16))
    return pl.pallas_call(
        kernel,
        out_shape=out_shape,
        in_specs=[VM, next_spec, VM, next_spec] + [VM] * 3 + [HB] * 2,
        out_specs=[VM, VM] + [HB] * (len(out_shape) - 2),
        scratch_shapes=([pltpu.VMEM((16, 16, 512), BF16)] if last else [])
        + [
            pltpu.SMEM((4,), F32),
            pltpu.SMEM((3,), jnp.int32),
            pltpu.VMEM((256, 512) if from_hbm else (8, 128), F32),
            pltpu.VMEM((512, 256) if from_hbm else (8, 128), F32),
            pltpu.SemaphoreType.DMA((4,)),
        ],
        compiler_params=params(),
        cost_estimate=hint(3),
        name=f"local_step{step}",
    )(src, src_next, rcv, rcv_next, vel_src, vel, inject, *in_hbm(wavelet, cell))


def restore_planes(step, src, planes, columns=range(4)):
    ix = lax.axis_index("gx")

    @pl.when(ix == 0)
    def _():
        for t in columns:
            src[t, pl.ds(0, 16, stride=16), :] = planes[step, t]

    @pl.when(ix == 7)
    def _():
        for t in columns:
            src[t, pl.ds(15, 16, stride=16), :] = planes[step, t]


def halo_step(step, local, vel_src, vel, halos, planes):
    first = step == 0

    def kernel(*refs):
        refs = list(refs)
        local_src = refs.pop(0)
        lap = refs.pop(0) if first else None
        local_rcv, vel_src, vel = refs[:3]
        halos, planes, src, rcv, packed = refs[3:7], refs[7], refs[8], refs[9], refs[10:]
        src[...] = local_src[...] + vel_src[...] * lap[...] if first else local_src[...]
        rcv[...] = local_rcv[...]
        add_source(src, vel_src, *halos)
        restore_planes(step, src, planes)
        pack_source(src, *packed)
        add_receiver(rcv, vel, PLANES, *halos)
        pack_receiver(rcv, PLANES, *packed)

    args = [*local, vel_src, vel, *halos, planes]
    out_shape = [SRC_COLS, RCV_COLS, *halo_buffers(SRC_PLANES, RCV_PLANES)]
    return pl.pallas_call(
        kernel,
        out_shape=out_shape,
        in_specs=[VM] * len(args),
        out_specs=[VM] * len(out_shape),
        compiler_params=params(),
        name=f"halo_step{step}",
    )(*args)


def last_source(local, bricks, vel_src, halos, planes):
    def kernel(local, _, vel_src, *refs):
        halos, planes, src, bricks, late, sem = refs[:4], *refs[4:]
        copies = []
        src[...] = local[...]
        add_source(src, vel_src, *halos)
        restore_planes(STEPS - 1, src, planes)
        for t in range(4):
            pack_brick(src, late, (t,))
            part = pl.ds(t * 4, 4)
            copies.append(pltpu.make_async_copy(late.at[part], bricks.at[part, 1], sem))
            copies[-1].start()
        wait(copies)

    return pl.pallas_call(
        kernel,
        out_shape=[SRC_COLS, pltpu.HBM(BRICKS, BF16)],
        in_specs=[VM, HB] + [VM] * 6,
        out_specs=[VM, HB],
        input_output_aliases={1: 1},
        scratch_shapes=[pltpu.VMEM((16, 16, 512), BF16), pltpu.SemaphoreType.DMA],
        compiler_params=params(),
        name="last_source",
    )(local, *in_hbm(bricks), vel_src, *halos, planes)


def last_receiver(local, vel, halos, src, kept):
    def kernel(local, vel, *refs):
        halos, src, kept, rcv, early, src_out, rcv_out, sem = refs[:4], *refs[4:]
        copies = [pltpu.make_async_copy(src.at[t], src_out.at[:, pl.ds(t * 128, 128)], sem) for t in range(4)]
        copies += [pltpu.make_async_copy(kept.at[t], early.at[t], sem) for t in range(2)]
        start(copies)
        rcv[...] = local[...]
        add_receiver(rcv, vel, PLANES, *halos)
        more = [pltpu.make_async_copy(rcv.at[t], rcv_out.at[:, pl.ds(t * 128, 128)], sem) for t in range(2)]
        start(more)
        wait(copies + more)

    return pl.pallas_call(
        kernel,
        out_shape=[RCV_COLS] * 2 + [jax.ShapeDtypeStruct(shape, F32) for shape in ((256, 512), (512, 256))],
        in_specs=[VM] * 7 + [HB],
        out_specs=[VM, VM, HB, HB],
        scratch_shapes=[pltpu.SemaphoreType.DMA],
        compiler_params=params(),
        cost_estimate=hint(2),
        name="last_receiver",
    )(local, vel, *halos, src, *in_hbm(kept))


def make_image(bricks, rcv_early, rcv_late):
    def kernel(bricks, rcv_early, rcv_late, out, held, sem):
        copies = []
        turn = lax.axis_index("gy") % 4
        for q in range(4):
            rows = slice(q * 128, q * 128 + 128)
            early = bricks[:, 0, :, rows].reshape(256, 128).astype(F32).T
            late = bricks[:, 1, :, rows].reshape(256, 128).astype(F32).T
            for place in range(4):
                part = slice(place * 32, place * 32 + 32)
                at = pl.ds(pl.multiple_of(q * 128 + lax.rem(place + 4 - turn, 4) * 32, 32), 32)
                for t in range(2):
                    lanes = slice(t * 128, t * 128 + 128)
                    held[at, lanes] = early[part, lanes] * rcv_early[t, at, :] + late[part, lanes] * rcv_late[t, at, :]
            copies.append(pltpu.make_async_copy(held.at[rows, :], out.at[rows, :], sem))
            copies[-1].start()
        wait(copies)

    return pl.pallas_call(
        kernel,
        out_shape=jax.ShapeDtypeStruct((512, 256), F32),
        in_specs=[VM] * 3,
        out_specs=HB,
        scratch_shapes=[pltpu.VMEM((512, 256), F32), pltpu.SemaphoreType.DMA],
        compiler_params=params(),
        name="make_image",
    )(bricks, rcv_early, rcv_late)


def exchange(buffers):
    gx_second, gy_second, gx_first, gy_first = buffers
    inner = lambda n: [(i, i ^ 1) for i in range(n)]
    outer = lambda n: [(i, (((i + 1) ^ 1) - 1) % n) for i in range(n)]
    return (
        lax.ppermute(gx_second, "gx", outer(8)),
        lax.ppermute(gy_second, "gy", outer(16)),
        lax.ppermute(gx_first, "gx", inner(8)),
        lax.ppermute(gy_first, "gy", inner(16)),
    )


def on_device(
    source_now,
    source_next,
    receiver_now,
    receiver_next,
    velocity,
    saved_planes,
    plane_index,
    wavelet,
    source_cell,
    traces,
    receiver_x,
    receiver_y,
):
    vel, src, rcv, turned = turn_velocity(velocity, source_now, receiver_now)
    pieces = lax.all_to_all(turned.reshape(16, 16, 512), "gy", split_axis=0, concat_axis=0, tiled=True)
    src, rcv, vel = (x.reshape(x.shape[0], -1, 128) for x in (src, rcv, vel))
    halos = exchange(first_halos(src, rcv))
    *local, planes, inject = local_first(
        source_now,
        source_next.reshape(256, 512),
        receiver_now,
        receiver_next.reshape(512, 256),
        vel,
        wavelet,
        source_cell,
        saved_planes,
        plane_index,
        traces,
        receiver_x,
        receiver_y,
    )
    vel_src = source_velocity(pieces)
    src_next, rcv_next = source_now.reshape(256, 512), receiver_now.reshape(512, 256)
    more = []
    for step in range(STEPS - 1):
        src, rcv, *to_send = halo_step(step, local, vel_src, vel, halos, planes)
        halos = exchange(to_send)
        local = local_step(step + 1, src, src_next, rcv, rcv_next, vel_src, vel, inject, wavelet, source_cell)
        more += local[2:]
        local = local[:2]
        src_next, rcv_next = src, rcv
    kept, early = more
    src, bricks = last_source(local[0], early, vel_src, halos, planes)
    bricks = lax.all_to_all(bricks, "gy", split_axis=0, concat_axis=0, tiled=True)
    rcv, rcv_early, source_field, receiver_field = last_receiver(local[1], vel, halos, src, kept)
    image = make_image(bricks, rcv_early, rcv)
    return (image.reshape(16, 32, 256), receiver_field.reshape(16, 32, 256), source_field.reshape(16, 16, 512))


def solution(mesh):
    field, turned = P("gx", "gy", None), P("gy", "gx", None)
    return jax.shard_map(
        on_device,
        mesh=mesh,
        in_specs=(turned, turned, field, field, field, P(), P(), P(), P(), P(), P(), P()),
        out_specs=(field, field, turned),
        check_vma=False,
    )
```
